32 devices in a mesh: wide: 32 (over z, y, x, core).
Axes of the slice: x: 2, y: 2, z: 4, core: 2. Of those that a mesh axis runs over, the one named last changes fastest.
Arguments:
- tokens: bfloat16 [64, 512, 768], P('wide'), may hold values from -6 to 6
- segments: int32 [64, 512], P('wide'), may hold values from 0 to 7, never falling along the last dimension, each value on 1 to 128 neighbouring positions
- pairing: int32 [512, 2], replicated, may hold values from 0 to 511, as said below
- pair_weight: float32 [512], replicated, may hold values from 0.2 to 6
- triple_weight: bfloat16 [768, 2304], replicated, may hold values from -0.21875 to 0.21875
- query_bias: float32 [768], replicated, may hold values from -3 to 3
- value_bias: float32 [768], replicated, may hold values from -3 to 3
- mixer_weight: bfloat16 [768, 768], replicated, may hold values from -1.75 to 1.75
- mixer_bias: float32 [768], replicated, may hold values from -3 to 3
- norm_gain: float32 [768], replicated, may hold values from 0.5 to 1.5
- norm_shift: float32 [768], replicated, may hold values from -2 to 2
- expand_weight: bfloat16 [768, 3072], replicated, may hold values from -0.21875 to 0.21875
- expand_bias: float32 [3072], replicated, may hold values from -3 to 3
- shrink_weight: bfloat16 [3072, 768], replicated, may hold values from -0.109375 to 0.109375
- shrink_bias: float32 [768], replicated, may hold values from -3 to 3
- final_gain: float32 [768], replicated, may hold values from 0.5 to 1.5
- final_shift: float32 [768], replicated, may hold values from -0.6 to 0.6
Outputs:
- loss: float32 [], replicated
- layer_output: bfloat16 [64, 512, 768], P('wide')
- token_grad: float32 [64, 512, 768], P('wide')
- triple_weight_grad: float32 [768, 2304], replicated
- query_bias_grad: float32 [768], replicated
- value_bias_grad: float32 [768], replicated
- mixer_weight_grad: float32 [768, 768], replicated
- mixer_bias_grad: float32 [768], replicated
- norm_gain_grad: float32 [768], replicated
- norm_shift_grad: float32 [768], replicated
- expand_weight_grad: float32 [768, 3072], replicated
- expand_bias_grad: float32 [3072], replicated
- shrink_weight_grad: float32 [3072, 768], replicated
- shrink_bias_grad: float32 [768], replicated
- final_gain_grad: float32 [768], replicated
- final_shift_grad: float32 [768], replicated
The draws below stay inside these ranges and needn't reach their ends.
Inputs may be any that keep to these rules, and one draw needn't show every extreme that they name: In each row the segment numbers never fall, and each of the 8 segments holds 1 to 128 tokens. `pairing`: each of the two columns names every segment number exactly once.
All inputs are finite; a program needn't handle non-finite values.
Results may differ from the reference program's by a relative error of at most 0.01.
Values may be sent and summed in bfloat16 or wider, within the bound.
No kernel may reach another device: no remote copies, remote signals or barrier semaphores. Data moves between devices by JAX's collectives and lax.ppermute only.
A program may use at most 192 MiB of HBM per device.

```python
import math
import jax
import jax.numpy as jnp
import numpy as np
from jax import lax

D = 768
HEAD_DIM = 64
FF = 3072
LEN = 512
SEG_ROW = 8
MOST = 128
ROWS = 64
SEG = 512
PAIRS = 512


def draw_pairing(key, part):
    key = jax.random.fold_in(key, 5)
    first_key, second_key = jax.random.split(key)
    anchor_ids = jax.random.permutation(first_key, SEG)
    positive_ids = jax.random.permutation(second_key, SEG)
    return jnp.stack([anchor_ids, positive_ids], axis=1).astype(jnp.int32)


def draw_pair_weight(key, part):
    key = jax.random.fold_in(key, 7)
    place = jnp.arange(PAIRS, dtype=jnp.float32) / PAIRS
    rough = jax.random.uniform(key, (PAIRS,), jnp.float32, 0.7, 1.3)
    return (0.4 * jnp.exp(1.791759 * place) * rough).astype(jnp.float32)


def block_levels(key, shape, cuts, low, largest):
    loudness, own = 1.0, jax.random.fold_in(key, 6)
    for dim, blocks in cuts:
        heights = jnp.exp(jax.random.uniform(jax.random.fold_in(own, dim), (blocks,), jnp.float32, low / len(cuts), largest / len(cuts)))
        loudness = loudness * jnp.repeat(heights, shape[dim] // blocks).reshape([-1 if axis == dim else 1 for axis in range(len(shape))])
    return loudness


def profile(count, total, limit, lean):
    portions = [(1 << 20) // math.isqrt(standing ** lean) + 1 for standing in range(2, count + 1)]
    spare, counts = total - limit - (count - 1), [1] * (count - 1)
    while spare > 0:
        free = [i for i in range(count - 1) if counts[i] < limit]
        whole, budget = sum([portions[i] for i in free]), spare
        for i in free:
            addition = min(limit - counts[i], max(1, budget * portions[i] // whole), spare)
            counts[i] = counts[i] + addition
            spare = spare - addition
    return np.array([limit] + counts)


def ragged(stream_key, count, total, bound, skew):
    if count == 2:
        one = jax.random.randint(stream_key, (), max(1, total - bound), min(bound, total - 1) + 1)
        return jnp.stack([one, total - one])
    sizes = jnp.asarray(profile(count, total, bound, skew), jnp.int32)
    pairs = (count - 1) // 2
    source_of, sink = sizes[1:1 + 2 * pairs:2], sizes[2:2 + 2 * pairs:2]
    room = jnp.minimum(source_of - 1, bound - sink)
    shifted = jax.random.randint(jax.random.fold_in(stream_key, 1), (pairs,), 0, 1 << 20) % (room + 1)
    sizes = sizes.at[1:1 + 2 * pairs:2].set(source_of - shifted).at[2:2 + 2 * pairs:2].set(sink + shifted)
    return sizes[jax.random.permutation(jax.random.fold_in(stream_key, 2), count)]


def normal_values(key, dims, scale, most, cuts=(), kind=jnp.bfloat16):
    level = block_levels(key, dims, cuts, -0.22, 0.18) if cuts else 1.0
    array = jax.random.normal(key, dims, jnp.float32) * scale * level
    return jnp.minimum(jnp.maximum(array, -most), most).astype(kind)


def setup_inputs(seed: int = 0) -> dict:
    key_of = jax.random.split(jax.random.key(seed), 18)
    tokens = normal_values(key_of[0], (ROWS, LEN, D), 1.0, 6.0, ((0, 32),))
    segments = jax.vmap(lambda own: jnp.searchsorted(jnp.cumsum(ragged(own, SEG_ROW, LEN, MOST, 1)), jnp.arange(LEN), side="right"))(jax.random.split(key_of[1], ROWS)).reshape((ROWS, LEN)).astype(jnp.int32)
    pairing = draw_pairing(jax.random.fold_in(key_of[17], 71), 0)
    pair_weight = draw_pair_weight(jax.random.fold_in(key_of[17], 71), 0)
    triple_weight = normal_values(key_of[4], (D, 3 * D), D ** -0.5, 0.21875)
    query_bias = normal_values(key_of[5], (D,), 0.5, 3.0, (), jnp.float32)
    value_bias = normal_values(key_of[6], (D,), 0.5, 3.0, (), jnp.float32)
    mixer_weight = normal_values(key_of[7], (D, D), (D // 64) ** -0.5, 1.75)
    mixer_bias = normal_values(key_of[8], (D,), 0.5, 3.0, (), jnp.float32)
    norm_gain = jnp.clip(1.0 + 0.1 * jax.random.normal(key_of[9], (D,), jnp.float32), 0.5, 1.5)
    norm_shift = normal_values(key_of[10], (D,), 0.3, 2.0, (), jnp.float32)
    expand_weight = normal_values(key_of[11], (D, FF), D ** -0.5, 0.21875)
    expand_bias = normal_values(key_of[12], (FF,), 0.5, 3.0, (), jnp.float32)
    shrink_weight = normal_values(key_of[13], (FF, D), FF ** -0.5, 0.109375)
    shrink_bias = normal_values(key_of[14], (D,), 0.5, 3.0, (), jnp.float32)
    final_gain = jnp.clip(1.0 + 0.1 * jax.random.normal(key_of[15], (D,), jnp.float32), 0.5, 1.5)
    final_shift = normal_values(key_of[16], (D,), 0.1, 0.6, (), jnp.float32)
    return {"tokens": tokens, "segments": segments, "pairing": pairing, "pair_weight": pair_weight, "triple_weight": triple_weight, "query_bias": query_bias, "value_bias": value_bias, "mixer_weight": mixer_weight, "mixer_bias": mixer_bias, "norm_gain": norm_gain, "norm_shift": norm_shift, "expand_weight": expand_weight, "expand_bias": expand_bias, "shrink_weight": shrink_weight, "shrink_bias": shrink_bias, "final_gain": final_gain, "final_shift": final_shift}


@jax.custom_vjp
def low(v):
    return lax.optimization_barrier(v.astype(jnp.bfloat16)).astype(jnp.float32)

@jax.custom_vjp
def low_back(v):
    return v

def low_keep(v):
    return (low(v), None)

def low_pass(kept, grad):
    return (grad,)

def back_keep(v):
    return (v, None)

def back_low(kept, grad):
    return (low(grad),)
low.defvjp(low_keep, low_pass)
low_back.defvjp(back_keep, back_low)
highest = lax.Precision.HIGHEST
temper = 0.05

def prefixes(width):
    return (width // 12, width // 6, width // 3, 2 * width // 3, width)

def norm_rows(value, gain, shift):
    centre = value - lax.optimization_barrier(jnp.mean(value, axis=-1, keepdims=True))
    scaled = centre * lax.rsqrt(lax.optimization_barrier(jnp.mean(centre * centre, axis=-1, keepdims=True)) + 1e-05)
    return scaled * gain + shift

def one_row(params, row_in, row_seg):
    triple, qbias, vbias, mixer, mbias, gain_a, shift_a, expand, ebias, shrink, sbias, gain_b, shift_b = params
    length, width = row_in.shape
    heads = width // HEAD_DIM
    mixed = jnp.dot(row_in, triple, precision=highest)
    query = low_back(low(mixed[:, :width] + qbias)).reshape(length, heads, HEAD_DIM)
    keys = low_back(low(mixed[:, width:2 * width])).reshape(length, heads, HEAD_DIM)
    values = low_back(low(mixed[:, 2 * width:] + vbias)).reshape(length, heads, HEAD_DIM)
    scores = low_back(jnp.einsum('qhd,khd->hqk', query, keys, precision=highest) * 0.125)
    mask = row_seg[:, None] == row_seg[None, :]
    masked = jnp.where(mask[None], scores, -1e+30)
    top = lax.optimization_barrier(jnp.max(masked, axis=-1, keepdims=True))
    expo = jnp.exp(masked - top)
    probs = expo / lax.optimization_barrier(jnp.sum(expo, axis=-1, keepdims=True))
    attended = jnp.einsum('hqk,khd->qhd', low(probs), values, precision=highest).reshape(length, width)
    attended = low_back(low(attended))
    branch = low_back(jnp.dot(attended, mixer, precision=highest) + mbias)
    first = norm_rows(row_in + branch, gain_a, shift_a)
    expanded = low_back(jnp.dot(low(first), expand, precision=highest) + ebias)
    active = low(jax.nn.gelu(expanded, approximate=False))
    shrunk = low_back(jnp.dot(active, shrink, precision=highest) + sbias)
    final = norm_rows(first + shrunk, gain_b, shift_b)
    member = (row_seg[None, :] == jnp.arange(SEG_ROW, dtype=jnp.int32)[:, None]).astype(jnp.float32)
    pooled = jnp.dot(member, final, precision=highest) / lax.optimization_barrier(jnp.sum(member, axis=1, keepdims=True))
    return (final, low(pooled))

def unit_rows(block):
    return block * lax.rsqrt(lax.optimization_barrier(jnp.sum(block * block, axis=1, keepdims=True)) + 1e-06)

def contrast(table, pairing, weights):
    anchors = table[pairing[:, 0]]
    positives = table[pairing[:, 1]]
    total = jnp.zeros((), jnp.float32)
    for cut in prefixes(table.shape[1]):
        sims = jnp.dot(unit_rows(anchors[:, :cut]), unit_rows(positives[:, :cut]).T, precision=highest) / temper
        top = lax.optimization_barrier(jnp.max(sims, axis=1))
        spread = top + jnp.log(lax.optimization_barrier(jnp.sum(jnp.exp(sims - top[:, None]), axis=1)))
        total = total + jnp.sum(weights * (spread - jnp.diagonal(sims)))
    return total

def reference(tokens, segments, pairing, pair_weight, triple_weight, query_bias, value_bias, mixer_weight, mixer_bias, norm_gain, norm_shift, expand_weight, expand_bias, shrink_weight, shrink_bias, final_gain, final_shift):
    params = tuple((p.astype(jnp.float32) for p in (triple_weight, query_bias, value_bias, mixer_weight, mixer_bias, norm_gain, norm_shift, expand_weight, expand_bias, shrink_weight, shrink_bias, final_gain, final_shift)))
    inputs = tokens.astype(jnp.float32)
    weights = pair_weight.astype(jnp.float32)

    def forward(inputs, params):

        def per_row(item):
            return one_row(params, item[0], item[1])
        outputs, pooled = lax.map(jax.checkpoint(per_row), (inputs, segments))
        table = pooled.reshape(SEG, D)
        return (contrast(table, pairing, weights), outputs)
    (total, outputs), pullback = jax.vjp(forward, inputs, params)
    token_grad, grads = pullback((jnp.ones((), jnp.float32), jnp.zeros_like(outputs)))
    return (total / PAIRS, outputs.astype(jnp.bfloat16), token_grad, grads[0], grads[1], grads[2], grads[3], grads[4], grads[5], grads[6], grads[7], grads[8], grads[9], grads[10], grads[11], grads[12])
```

```python
import functools

import jax
import jax.numpy as jnp
from jax import lax
from jax.experimental import pallas as pl
from jax.experimental.pallas import tpu as pltpu
from jax.sharding import PartitionSpec as P

HEADS = 12
HEAD_DIM = 64
SEG_ROW = 8
AXIS = "wide"
F32 = jnp.float32
BF16 = jnp.bfloat16

highest = lax.Precision.HIGHEST
scale = 20.0


def prefixes(width):
    return (width // 12, width // 6, width // 3, 2 * width // 3, width)


def dot(a, b):
    return jnp.dot(a, b, preferred_element_type=F32)


def dot_nt(a, b):
    return lax.dot_general(a, b, (((1,), (1,)), ((), ())), preferred_element_type=F32)


def window(array, low, high):
    first, last = low // 128 * 128, -(-high // 128) * 128
    piece = array[:, first:last]
    if first == low and last == high:
        return piece, first, last
    lane = first + lax.broadcasted_iota(jnp.int32, (1, last - first), 1)
    return jnp.where((lane >= low) & (lane < high), piece, jnp.zeros_like(piece)), first, last


def split(value):
    high = value.astype(BF16)
    return high, (value - high.astype(F32)).astype(BF16)


def flip(size, low, high):
    return [(i, i ^ (high if i & 1 else low)) for i in range(size)]


def bit_of(me, bit):
    return (me // bit) % 2


def stages(me, size):
    out = [(flip(size, 1, 1), bit_of(me, 1))]
    bits = [1 << k for k in range(1, size.bit_length() - 1)]
    if len(bits) > 1:
        a, b = bits[0], bits[1]
        core = bit_of(me, 1)
        one, two = bit_of(me, a), bit_of(me, b)
        out.append((flip(size, a, b), jnp.where(core == 0, one, two)))
        out.append((flip(size, b, a), jnp.where(core == 0, two, one)))
        bits = bits[2:]
    for bit in bits:
        out.append((flip(size, bit, bit), bit_of(me, bit)))
    return out


def gather_rows(block, size):
    bit = size // 2
    while bit:
        other = lax.ppermute(block, AXIS, flip(size, bit, bit))
        block = jnp.concatenate([block, other], axis=0)
        bit //= 2
    return block


def sum_over(value, plan):
    for pairs, mine in plan:
        half = value.shape[0] // 2
        keep = lax.dynamic_slice_in_dim(value, mine * half, half, 0)
        send = lax.dynamic_slice_in_dim(value, (1 - mine) * half, half, 0)
        got = lax.ppermute(send, AXIS, pairs)
        value = (keep.astype(F32) + got.astype(F32)).astype(BF16)
    for pairs, mine in plan[::-1]:
        got = lax.ppermute(value, AXIS, pairs)
        value = jnp.where(
            mine == 0,
            jnp.concatenate([value, got], axis=0),
            jnp.concatenate([got, value], axis=0),
        )
    return value.astype(F32)


def sum_small(value, size):
    bit = 1
    while bit < size:
        value = value + lax.ppermute(value, AXIS, flip(size, bit, bit))
        bit *= 2
    return value


def contrast_kernel(
    size, me_ref, gathered, own_ref, cols_ref, rows_ref, load_col_ref, load_row_ref, loss_ref, grad_ref, table, total, aim
):
    me = me_ref[0]
    count, width = table.shape
    share = own_ref.shape[0]
    block = 128
    levels = size.bit_length() - 1
    for place in range(size):
        mask = sum(((place >> k) & 1) << (levels - 1 - k) for k in range(levels))
        owner = me ^ mask
        table[pl.ds(pl.multiple_of(owner * share, share), share), :] = gathered[
            place * share : (place + 1) * share, :
        ]
    cuts = prefixes(width)
    spans = list(zip((0,) + cuts[:-1], cuts))
    lane_ids = lax.broadcasted_iota(jnp.int32, (1, count), 1)

    def place_pairs(i, carry):
        partner, load = carry
        rows = pl.ds(pl.multiple_of(i * block, block), block)
        hit = cols_ref[rows, 0:1] == lane_ids
        partner = partner + jnp.sum(
            jnp.where(hit, cols_ref[rows, 1:2].astype(F32), 0.0), axis=0, keepdims=True
        )
        load = load + jnp.sum(jnp.where(hit, load_col_ref[rows, :], 0.0), axis=0, keepdims=True)
        return partner, load

    zero_row = jnp.zeros((1, count), F32)
    partner_row, load_row = lax.fori_loop(0, count // block, place_pairs, (zero_row, zero_row))
    own_ids = me * share + lax.broadcasted_iota(jnp.int32, (share, 1), 0)
    hit = rows_ref[0:1, :] == own_ids
    partner_own = jnp.sum(jnp.where(hit, rows_ref[1:2, :].astype(F32), 0.0), axis=1, keepdims=True)
    load_own = jnp.sum(jnp.where(hit, load_row_ref[...], 0.0), axis=1, keepdims=True)

    squares = jnp.zeros((count, 1), F32)
    side = jnp.zeros((count, 128), F32)
    for k, (low, high) in enumerate(spans):
        piece, first, last = window(table, low, high)
        wide = piece.astype(F32)
        squares = squares + jnp.sum(wide * wide, axis=1, keepdims=True)
        lane = lax.broadcasted_iota(jnp.int32, (1, 128), 1)
        side = jnp.where(lane == k, squares, side)
    upright = lax.rsqrt(jnp.transpose(side)[0:8, :] + 1e-06) * scale
    inverse_rows = [upright[k : k + 1, :] for k in range(len(cuts))]

    total[...] = jnp.zeros_like(total)
    aim[...] = jnp.zeros_like(aim)

    def add_rows(i, carry):
        start = pl.multiple_of(i * block, block)
        sims = jnp.zeros((block, count), F32)
        squares = jnp.zeros((block, 1), F32)
        row_ids = (start + lax.broadcasted_iota(jnp.int32, (block, 1), 0)).astype(F32)
        chosen = partner_row == row_ids
        for k, (low, high) in enumerate(spans):
            piece, first, last = window(table.at[pl.ds(start, block), :], low, high)
            wide = piece.astype(F32)
            squares = squares + jnp.sum(wide * wide, axis=1, keepdims=True)
            sims = sims + dot_nt(piece, table[:, first:last])
            value = sims * lax.rsqrt(squares + 1e-06) * inverse_rows[k]
            total[k : k + 1, :] += jnp.sum(jnp.exp(value - scale), axis=0, keepdims=True)
            aim[k : k + 1, :] += jnp.sum(jnp.where(chosen, value, 0.0), axis=0, keepdims=True)
        return carry

    lax.fori_loop(0, count // block, add_rows, 0)

    spreads = scale + jnp.log(total[0 : len(cuts), :])
    gaps = jnp.sum(spreads - aim[0 : len(cuts), :], axis=0, keepdims=True)
    loss_ref[...] = jnp.broadcast_to(
        jnp.sum(gaps * load_row, axis=1, keepdims=True) / count, loss_ref.shape
    )

    sims = jnp.zeros((share, count), F32)
    squares = jnp.zeros((share, 1), F32)
    out_hit = (partner_own == lane_ids.astype(F32)).astype(F32)
    in_hit = (partner_row == own_ids.astype(F32)).astype(F32)
    grad_ref[...] = jnp.zeros_like(grad_ref)
    for k, (low, high) in enumerate(spans):
        piece, first, last = window(own_ref, low, high)
        wide = piece.astype(F32)
        squares = squares + jnp.sum(wide * wide, axis=1, keepdims=True)
        inverse = lax.rsqrt(squares + 1e-06)
        sims = sims + dot_nt(piece, table[:, first:last])
        value = sims * inverse * inverse_rows[k]
        spread = scale + jnp.log(jnp.sum(jnp.exp(value - scale), axis=1, keepdims=True))
        dsims = load_own * (jnp.exp(value - spread) - out_hit) + load_row * (
            jnp.exp(value - spreads[k : k + 1, :]) - in_hit
        )
        big, small = split(dsims * inverse_rows[k])
        unit, _, last = window(own_ref, 0, high)
        unit = unit.astype(F32) * inverse
        dunit = dot(big, table[:, :last]) + dot(small, table[:, :last])
        if last != high:
            lane = lax.broadcasted_iota(jnp.int32, (1, last), 1)
            dunit = jnp.where(lane < high, dunit, 0.0)
        along = jnp.sum(dunit * unit, axis=1, keepdims=True)
        grad_ref[:, :last] += inverse * (dunit - unit * along)


def contrast(gathered, own, pairing, pair_weight, me, size):
    share, width = own.shape
    count = share * size
    vmem = pl.BlockSpec(memory_space=pltpu.VMEM)
    loss, grad = pl.pallas_call(
        functools.partial(contrast_kernel, size),
        out_shape=(
            jax.ShapeDtypeStruct((8, 128), F32),
            jax.ShapeDtypeStruct((share, width), F32),
        ),
        in_specs=[pl.BlockSpec(memory_space=pltpu.SMEM)] + [vmem] * 6,
        out_specs=(vmem, vmem),
        scratch_shapes=[
            pltpu.VMEM((count, width), BF16),
            pltpu.VMEM((8, count), F32),
            pltpu.VMEM((8, count), F32),
        ],
        compiler_params=pltpu.CompilerParams(vmem_limit_bytes=56 * 1024 * 1024),
        name="contrast",
    )(
        me.reshape(1),
        gathered,
        own,
        pairing,
        pairing.T,
        pair_weight[:, None],
        pair_weight[None, :],
    )
    return loss[0, 0], grad


def norm_forward(value, gain, shift):
    centre = value - jnp.mean(value, axis=-1, keepdims=True)
    inverse = lax.rsqrt(jnp.mean(centre * centre, axis=-1, keepdims=True) + 1e-05)
    scaled = centre * inverse
    return (scaled * gain + shift, scaled, inverse)


def norm_backward(grad, scaled, inverse, gain):
    inner = grad * gain
    back = inverse * (
        inner
        - jnp.mean(inner, axis=-1, keepdims=True)
        - scaled * jnp.mean(inner * scaled, axis=-1, keepdims=True)
    )
    return (back, jnp.sum(grad * scaled, axis=0), jnp.sum(grad, axis=0))


def row_scores(query, keys, row_seg):
    scores = jnp.einsum("qhd,khd->hqk", query, keys, preferred_element_type=jnp.float32) * 0.125
    mask = row_seg[:, None] == row_seg[None, :]
    return jnp.where(mask[None], scores, -1e30)


def attend_row(items):
    query, keys, values, row_seg = items
    scores = row_scores(query, keys, row_seg)
    top = jnp.max(scores, axis=-1, keepdims=True)
    expo = jnp.exp(scores - top)
    total = jnp.sum(expo, axis=-1, keepdims=True)
    probs = expo / total
    mixed = jnp.einsum(
        "hqk,khd->qhd", probs.astype(jnp.bfloat16), values, preferred_element_type=jnp.float32
    )
    return (mixed.astype(jnp.bfloat16), top + jnp.log(total))


def attend_back(items):
    query, keys, values, row_seg, spread, grad_out = items
    probs = jnp.exp(row_scores(query, keys, row_seg) - spread)
    weights = probs.astype(jnp.bfloat16)
    dprobs = jnp.einsum("qhd,khd->hqk", grad_out, values, preferred_element_type=jnp.float32)
    dvalues = jnp.einsum("hqk,qhd->khd", weights, grad_out, preferred_element_type=jnp.float32)
    dscores = (probs * (dprobs - jnp.sum(dprobs * probs, axis=-1, keepdims=True))).astype(
        jnp.bfloat16
    )
    dquery = jnp.einsum("hqk,khd->qhd", dscores, keys, preferred_element_type=jnp.float32) * 0.125
    dkeys = jnp.einsum("hqk,qhd->khd", dscores, query, preferred_element_type=jnp.float32) * 0.125
    return (dquery.astype(jnp.bfloat16), dkeys.astype(jnp.bfloat16), dvalues.astype(jnp.bfloat16))


def on_device(
    tokens,
    segments,
    pairing,
    pair_weight,
    triple_weight,
    query_bias,
    value_bias,
    mixer_weight,
    mixer_bias,
    norm_gain,
    norm_shift,
    expand_weight,
    expand_bias,
    shrink_weight,
    shrink_bias,
    final_gain,
    final_shift,
):
    rows, length, width = tokens.shape
    flat = tokens.reshape(rows * length, width)

    def shaped(tensor):
        return tensor.reshape(rows, length, HEADS, HEAD_DIM)

    mixed = jnp.dot(flat, triple_weight, preferred_element_type=jnp.float32)
    query = (mixed[:, :width] + query_bias).astype(jnp.bfloat16)
    keys = mixed[:, width : 2 * width].astype(jnp.bfloat16)
    values = (mixed[:, 2 * width :] + value_bias).astype(jnp.bfloat16)
    attended, spread = lax.map(attend_row, (shaped(query), shaped(keys), shaped(values), segments))
    attended = attended.reshape(rows * length, width)
    branch = jnp.dot(attended, mixer_weight, preferred_element_type=jnp.float32) + mixer_bias
    first, scaled_a, inverse_a = norm_forward(
        flat.astype(jnp.float32) + branch, norm_gain, norm_shift
    )
    first_low = first.astype(jnp.bfloat16)
    expanded = jnp.dot(first_low, expand_weight, preferred_element_type=jnp.float32) + expand_bias
    active = jax.nn.gelu(expanded, approximate=False).astype(jnp.bfloat16)
    shrunk = jnp.dot(active, shrink_weight, preferred_element_type=jnp.float32) + shrink_bias
    final, scaled_b, inverse_b = norm_forward(first + shrunk, final_gain, final_shift)
    member = (segments[:, None, :] == jnp.arange(SEG_ROW, dtype=jnp.int32)[None, :, None]).astype(
        jnp.float32
    )
    counts = jnp.sum(member, axis=2, keepdims=True)
    pooled = (
        jnp.einsum("rsl,rld->rsd", member, final.reshape(rows, length, width), precision=highest)
        / counts
    )
    size = lax.axis_size(AXIS)
    me = lax.axis_index(AXIS)
    own = pooled.reshape(rows * SEG_ROW, width).astype(BF16)
    loss, dpooled = contrast(gather_rows(own, size), own, pairing, pair_weight, me, size)
    dfinal = jnp.einsum(
        "rsl,rsd->rld", member, dpooled.reshape(rows, SEG_ROW, width) / counts, precision=highest
    ).reshape(rows * length, width)
    dsecond, dgain_b, dshift_b = norm_backward(dfinal, scaled_b, inverse_b, final_gain)
    dshrunk = dsecond.astype(jnp.bfloat16)
    dshrink_w = jnp.dot(active.T, dshrunk, preferred_element_type=jnp.float32)
    dshrink_b = jnp.sum(dshrunk.astype(jnp.float32), axis=0)
    dactive = jnp.dot(dshrunk, shrink_weight.T, preferred_element_type=jnp.float32)
    normal_cdf = 0.5 * (1.0 + lax.erf(expanded * 0.7071067811865476))
    normal_pdf = jnp.exp(-0.5 * expanded * expanded) * 0.3989422804014327
    dexpanded = (dactive * (normal_cdf + expanded * normal_pdf)).astype(jnp.bfloat16)
    dexpand_w = jnp.dot(first_low.T, dexpanded, preferred_element_type=jnp.float32)
    dexpand_b = jnp.sum(dexpanded.astype(jnp.float32), axis=0)
    dfirst = dsecond + jnp.dot(dexpanded, expand_weight.T, preferred_element_type=jnp.float32)
    dbranch, dgain_a, dshift_a = norm_backward(dfirst, scaled_a, inverse_a, norm_gain)
    dbranch_low = dbranch.astype(jnp.bfloat16)
    dmixer_w = jnp.dot(attended.T, dbranch_low, preferred_element_type=jnp.float32)
    dmixer_b = jnp.sum(dbranch_low.astype(jnp.float32), axis=0)
    dattended = jnp.dot(dbranch_low, mixer_weight.T, preferred_element_type=jnp.float32).astype(
        jnp.bfloat16
    )
    dquery, dkeys, dvalues = lax.map(
        attend_back,
        (shaped(query), shaped(keys), shaped(values), segments, spread, shaped(dattended)),
    )
    dquery = dquery.reshape(rows * length, width)
    dvalues = dvalues.reshape(rows * length, width)
    dmixed = jnp.concatenate([dquery, dkeys.reshape(rows * length, width), dvalues], axis=1)
    dtriple = jnp.dot(flat.T, dmixed, preferred_element_type=jnp.float32)
    dquery_b = jnp.sum(dquery.astype(jnp.float32), axis=0)
    dvalue_b = jnp.sum(dvalues.astype(jnp.float32), axis=0)
    token_grad = dbranch + jnp.dot(dmixed, triple_weight.T, preferred_element_type=jnp.float32)
    plan = stages(me, size)
    small = sum_small(
        jnp.concatenate(
            [dquery_b, dvalue_b, dmixer_b, dgain_a, dshift_a, dexpand_b, dshrink_b, dgain_b, dshift_b]
        ).reshape(-1, width),
        size,
    )
    fan = expand_bias.shape[0] // width
    dshrink_w = sum_over(dshrink_w.astype(BF16), plan)
    dexpand_w = sum_over(dexpand_w.astype(BF16), plan)
    both = sum_over(jnp.concatenate([dtriple, dmixer_w], axis=1).astype(BF16), plan)
    summed = (
        both[:, : 3 * width],
        small[0],
        small[1],
        both[:, 3 * width :],
        small[2],
        small[3],
        small[4],
        dexpand_w,
        small[5 : 5 + fan].reshape(-1),
        dshrink_w,
        small[5 + fan],
        small[6 + fan],
        small[7 + fan],
    )
    return (
        loss,
        final.reshape(rows, length, width).astype(jnp.bfloat16),
        token_grad.reshape(rows, length, width),
        summed[0],
        summed[1],
        summed[2],
        summed[3],
        summed[4],
        summed[5],
        summed[6],
        summed[7],
        summed[8],
        summed[9],
        summed[10],
        summed[11],
        summed[12],
    )


def solution(mesh):
    return jax.shard_map(
        on_device,
        mesh=mesh,
        in_specs=(
            P("wide", None, None),
            P("wide", None),
            P(),
            P(),
            P(),
            P(),
            P(),
            P(),
            P(),
            P(),
            P(),
            P(),
            P(),
            P(),
            P(),
            P(),
            P(),
        ),
        out_specs=(
            P(),
            P("wide", None, None),
            P("wide", None, None),
            P(),
            P(),
            P(),
            P(),
            P(),
            P(),
            P(),
            P(),
            P(),
            P(),
            P(),
            P(),
            P(),
        ),
        check_vma=False,
    )
```

```python
import functools

import jax
import jax.numpy as jnp
from jax import lax
from jax.experimental import pallas as pl
from jax.experimental.pallas import tpu as pltpu
from jax.sharding import PartitionSpec as P

HEADS = 12
HEAD_DIM = 64
SEG_ROW = 8
AXIS = "wide"
F32 = jnp.float32
BF16 = jnp.bfloat16

highest = lax.Precision.HIGHEST
scale = 20.0
MIB = 1024 * 1024


def prefixes(width):
    return (width // 12, width // 6, width // 3, 2 * width // 3, width)


def cost(micros):
    return pl.CostEstimate(flops=int(micros * 1.15e9), bytes_accessed=0, transcendentals=0)


def dot(a, b):
    return jnp.dot(a, b, preferred_element_type=F32)


def dot_nt(a, b):
    return lax.dot_general(a, b, (((1,), (1,)), ((), ())), preferred_element_type=F32)


def dot_tn(a, b):
    return lax.dot_general(a, b, (((0,), (0,)), ((), ())), preferred_element_type=F32)


def window(array, low, high):
    first, last = low // 128 * 128, -(-high // 128) * 128
    piece = array[:, first:last]
    if first == low and last == high:
        return piece, first, last
    lane = first + lax.broadcasted_iota(jnp.int32, (1, last - first), 1)
    return jnp.where((lane >= low) & (lane < high), piece, jnp.zeros_like(piece)), first, last


def split(value):
    high = value.astype(BF16)
    return high, (value - high.astype(F32)).astype(BF16)


def flip(size, low, high):
    return [(i, i ^ (high if i & 1 else low)) for i in range(size)]


def bit_of(me, bit):
    return (me // bit) % 2


def gather_rows(block, size, works):
    bit, results = size // 2, []
    while bit:
        pairs = flip(size, bit, bit)
        if len(results) < len(works):
            work, value = works[len(results)]
            block, value = lax.optimization_barrier((block, value))
            other, result = lax.optimization_barrier((lax.ppermute(block, AXIS, pairs), work(value)))
            results.append(result)
        else:
            other = lax.ppermute(block, AXIS, pairs)
        block = jnp.concatenate([block, other], axis=0)
        bit //= 2
    return block, results


def contrast_kernel(
    size, me_ref, gathered, own_ref, cols_ref, rows_ref, load_col_ref, load_row_ref, loss_ref, grad_ref, table, total, aim
):
    me = me_ref[0]
    count, width = table.shape
    share = own_ref.shape[0]
    block = 128
    levels = size.bit_length() - 1
    for place in range(size):
        mask = sum(((place >> k) & 1) << (levels - 1 - k) for k in range(levels))
        owner = me ^ mask
        table[pl.ds(pl.multiple_of(owner * share, share), share), :] = gathered[
            place * share : (place + 1) * share, :
        ]
    cuts = prefixes(width)
    spans = list(zip((0,) + cuts[:-1], cuts))
    lane_ids = lax.broadcasted_iota(jnp.int32, (1, count), 1)

    def place_pairs(i, carry):
        partner, load = carry
        rows = pl.ds(pl.multiple_of(i * block, block), block)
        hit = cols_ref[rows, 0:1] == lane_ids
        partner = partner + jnp.sum(
            jnp.where(hit, cols_ref[rows, 1:2].astype(F32), 0.0), axis=0, keepdims=True
        )
        load = load + jnp.sum(jnp.where(hit, load_col_ref[rows, :], 0.0), axis=0, keepdims=True)
        return partner, load

    zero_row = jnp.zeros((1, count), F32)
    partner_row, load_row = lax.fori_loop(0, count // block, place_pairs, (zero_row, zero_row))
    own_ids = me * share + lax.broadcasted_iota(jnp.int32, (share, 1), 0)
    hit = rows_ref[0:1, :] == own_ids
    partner_own = jnp.sum(jnp.where(hit, rows_ref[1:2, :].astype(F32), 0.0), axis=1, keepdims=True)
    load_own = jnp.sum(jnp.where(hit, load_row_ref[...], 0.0), axis=1, keepdims=True)

    squares = jnp.zeros((count, 1), F32)
    side = jnp.zeros((count, 128), F32)
    for k, (low, high) in enumerate(spans):
        piece, first, last = window(table, low, high)
        wide = piece.astype(F32)
        squares = squares + jnp.sum(wide * wide, axis=1, keepdims=True)
        lane = lax.broadcasted_iota(jnp.int32, (1, 128), 1)
        side = jnp.where(lane == k, squares, side)
    upright = lax.rsqrt(jnp.transpose(side)[0:8, :] + 1e-06) * scale
    inverse_rows = [upright[k : k + 1, :] for k in range(len(cuts))]

    total[...] = jnp.zeros_like(total)
    aim[...] = jnp.zeros_like(aim)

    def add_rows(i, carry):
        start = pl.multiple_of(i * block, block)
        sims = jnp.zeros((block, count), F32)
        squares = jnp.zeros((block, 1), F32)
        row_ids = (start + lax.broadcasted_iota(jnp.int32, (block, 1), 0)).astype(F32)
        chosen = partner_row == row_ids
        for k, (low, high) in enumerate(spans):
            piece, first, last = window(table.at[pl.ds(start, block), :], low, high)
            wide = piece.astype(F32)
            squares = squares + jnp.sum(wide * wide, axis=1, keepdims=True)
            sims = sims + dot_nt(piece, table[:, first:last])
            value = sims * lax.rsqrt(squares + 1e-06) * inverse_rows[k]
            total[k : k + 1, :] += jnp.sum(jnp.exp(value - scale), axis=0, keepdims=True)
            aim[k : k + 1, :] += jnp.sum(jnp.where(chosen, value, 0.0), axis=0, keepdims=True)
        return carry

    lax.fori_loop(0, count // block, add_rows, 0)

    spreads = scale + jnp.log(total[0 : len(cuts), :])
    gaps = jnp.sum(spreads - aim[0 : len(cuts), :], axis=0, keepdims=True)
    loss_ref[...] = jnp.broadcast_to(
        jnp.sum(gaps * load_row, axis=1, keepdims=True) / count, loss_ref.shape
    )

    sims = jnp.zeros((share, count), F32)
    squares = jnp.zeros((share, 1), F32)
    out_hit = (partner_own == lane_ids.astype(F32)).astype(F32)
    in_hit = (partner_row == own_ids.astype(F32)).astype(F32)
    grad_ref[...] = jnp.zeros_like(grad_ref)
    for k, (low, high) in enumerate(spans):
        piece, first, last = window(own_ref, low, high)
        wide = piece.astype(F32)
        squares = squares + jnp.sum(wide * wide, axis=1, keepdims=True)
        inverse = lax.rsqrt(squares + 1e-06)
        sims = sims + dot_nt(piece, table[:, first:last])
        value = sims * inverse * inverse_rows[k]
        spread = scale + jnp.log(jnp.sum(jnp.exp(value - scale), axis=1, keepdims=True))
        dsims = load_own * (jnp.exp(value - spread) - out_hit) + load_row * (
            jnp.exp(value - spreads[k : k + 1, :]) - in_hit
        )
        big, small = split(dsims * inverse_rows[k])
        unit, _, last = window(own_ref, 0, high)
        unit = unit.astype(F32) * inverse
        dunit = dot(big, table[:, :last]) + dot(small, table[:, :last])
        if last != high:
            lane = lax.broadcasted_iota(jnp.int32, (1, last), 1)
            dunit = jnp.where(lane < high, dunit, 0.0)
        along = jnp.sum(dunit * unit, axis=1, keepdims=True)
        grad_ref[:, :last] += inverse * (dunit - unit * along)


def contrast(gathered, own, pairing, pair_weight, me, size):
    share, width = own.shape
    count = share * size
    vmem = pl.BlockSpec(memory_space=pltpu.VMEM)
    loss, grad = pl.pallas_call(
        functools.partial(contrast_kernel, size),
        out_shape=(
            jax.ShapeDtypeStruct((8, 128), F32),
            jax.ShapeDtypeStruct((share, width), F32),
        ),
        in_specs=[pl.BlockSpec(memory_space=pltpu.SMEM)] + [vmem] * 6,
        out_specs=(vmem, vmem),
        scratch_shapes=[
            pltpu.VMEM((count, width), BF16),
            pltpu.VMEM((8, count), F32),
            pltpu.VMEM((8, count), F32),
        ],
        compiler_params=pltpu.CompilerParams(vmem_limit_bytes=16 * MIB),
        cost_estimate=cost(6),
        name="contrast",
    )(
        me.reshape(1),
        gathered,
        own,
        pairing,
        pairing.T,
        pair_weight[:, None],
        pair_weight[None, :],
    )
    return loss[0, 0], grad


def attention_windows(length):
    block = 128
    return [
        (i, max(0, i - block), min(length, i + 2 * block)) for i in range(0, length, block)
    ]


def segment_column(seg_row):
    wide = jnp.broadcast_to(seg_row.astype(F32), (128, seg_row.shape[1]))
    return jnp.transpose(wide)[:, 0:1].astype(jnp.int32)


def both_heads(pair):
    left = lax.broadcasted_iota(jnp.int32, (1, 128), 1) < HEAD_DIM
    zero = jnp.zeros((), pair.dtype)
    return jnp.concatenate([jnp.where(left, pair, zero), jnp.where(left, zero, pair)], axis=0)


def layer_kernel(
    tokens,
    segments,
    triple_hbm,
    query_bias,
    value_bias,
    mixer_hbm,
    mixer_bias,
    norm_gain,
    norm_shift,
    expand_hbm,
    expand_bias,
    shrink_hbm,
    shrink_bias,
    final_gain,
    final_shift,
    qkv,
    spread,
    stats,
    attended,
    scaled_a,
    first_low,
    active,
    slope,
    scaled_b,
    output,
    pooled,
    triple,
    mixer,
    expand,
    shrink,
    bias,
    values_t,
    first,
    total,
    sems,
):
    step = pl.program_id(0)
    length, width = tokens.shape[1:]
    fan = expand.shape[1]
    held = (triple, mixer, expand, shrink)
    copies = [
        pltpu.make_async_copy(src, dst, sems.at[k])
        for k, (src, dst) in enumerate(zip((triple_hbm, mixer_hbm, expand_hbm, shrink_hbm), held))
    ]

    @pl.when(step == 0)
    def _():
        for copy in copies:
            copy.start()
        copies[0].wait()

    seg_row = segments[pl.ds(step, 1), :]
    seg_col = segment_column(seg_row)
    windows = attention_windows(length)
    for k, (at, low, high) in enumerate(windows):
        same = seg_col[low:high, :] == seg_row[:, at : at + 128]
        bias[k, : high - low, :] = jnp.where(same, 0.0, -1e30)

    chunk = width
    x = tokens[0]
    mixed = dot(x, triple[:, 0:chunk]) + query_bias[...][None, :]
    qkv[0, :, 0:chunk] = (mixed.astype(BF16).astype(F32) * 0.125).astype(BF16)
    qkv[0, :, chunk : 2 * chunk] = dot(x, triple[:, chunk : 2 * chunk]).astype(BF16)
    qkv[0, :, 2 * chunk :] = (dot(x, triple[:, 2 * chunk :]) + value_bias[...][None, :]).astype(BF16)

    values_t[...] = jnp.transpose(qkv[0, :, 2 * chunk :])
    spread[...] = jnp.zeros_like(spread)
    for k, (at, low, high) in enumerate(windows):
        wall = bias[k, : high - low, :]
        wall = jnp.concatenate([wall, wall], axis=1)
        for p in range(width // 128):
            cols = slice(p * 128, p * 128 + 128)
            query = both_heads(qkv[0, at : at + 128, cols])
            keys = qkv[0, low:high, width + p * 128 : width + p * 128 + 128]
            scores = dot_nt(keys, query) + wall
            top = jnp.max(scores, axis=0, keepdims=True)
            expo = jnp.exp(scores - top)
            amount = jnp.sum(expo, axis=0, keepdims=True)
            found = dot(values_t[cols, low:high], expo.astype(BF16)) * (1.0 / amount)
            found = found.astype(BF16)
            mid = p * 128 + HEAD_DIM
            attended[0, p * 128 : mid, at : at + 128] = found[:HEAD_DIM, :128]
            attended[0, mid : p * 128 + 128, at : at + 128] = found[HEAD_DIM:, 128:]
            marks = top + jnp.log(amount)
            spread[0, 2 * p : 2 * p + 1, at : at + 128] = marks[:, :128]
            spread[0, 2 * p + 1 : 2 * p + 2, at : at + 128] = marks[:, 128:]

    @pl.when(step == 0)
    def _():
        copies[1].wait()

    summed = tokens[0].astype(F32) + (dot_tn(attended[0], mixer[...]) + mixer_bias[...][None, :])
    centre = summed - jnp.mean(summed, axis=1, keepdims=True)
    inverse = lax.rsqrt(jnp.mean(centre * centre, axis=1, keepdims=True) + 1e-05)
    scaled = centre * inverse
    scaled_a[0] = scaled.astype(BF16)
    inverse_a = inverse
    value = scaled * norm_gain[...][None, :] + norm_shift[...][None, :]
    first[...] = value
    first_low[0] = value.astype(BF16)

    @pl.when(step == 0)
    def _():
        copies[2].wait()
        copies[3].wait()

    part = 512
    for j in range(fan // part):
        cols = slice(j * part, (j + 1) * part)
        value = dot(first_low[0], expand[:, cols]) + expand_bias[cols][None, :]
        gauss = jnp.exp(value * value * -0.5)
        near = 1.0 / (1.0 + 0.3275911 * 0.7071067811865476 * jnp.abs(value))
        poly = near * (
            0.5 * 0.254829592
            + near
            * (
                0.5 * -0.284496736
                + near * (0.5 * 1.421413741 + near * (0.5 * -1.453152027 + near * (0.5 * 1.061405429)))
            )
        )
        tail = poly * gauss
        below = jnp.where(value < 0, tail, 1.0 - tail)
        rounded = (value * below).astype(BF16)
        active[0, :, cols] = rounded
        slope[0, :, cols] = (below + value * (gauss * 0.3989422804014327)).astype(BF16)
        product = dot(rounded, shrink[cols, :])
        if j == 0:
            total[...] = product
        else:
            total[...] += product

    summed = first[...] + (total[...] + shrink_bias[...][None, :])
    centre = summed - jnp.mean(summed, axis=1, keepdims=True)
    inverse = lax.rsqrt(jnp.mean(centre * centre, axis=1, keepdims=True) + 1e-05)
    scaled = centre * inverse
    scaled_b[0] = scaled.astype(BF16)
    lane = lax.broadcasted_iota(jnp.int32, (1, 128), 1)
    stats[0] = jnp.where(lane == 0, inverse_a, inverse)
    final = scaled * final_gain[...][None, :] + final_shift[...][None, :]
    output[0] = final.astype(BF16)
    member = (
        lax.broadcasted_iota(jnp.int32, (SEG_ROW, length), 0) == seg_row
    ).astype(F32)
    counts = jnp.sum(member, axis=1, keepdims=True)
    gathered = jnp.dot(member, final, preferred_element_type=F32, precision=highest)
    pooled[0] = (gathered / counts).astype(BF16)


def layer(tokens, segments, triple_weight, query_bias, value_bias, mixer_weight, mixer_bias, norm_gain, norm_shift, expand_weight, expand_bias, shrink_weight, shrink_bias, final_gain, final_shift):
    rows, length, width = tokens.shape
    fan = expand_weight.shape[1]

    def by_row(*shape):
        return pl.BlockSpec((1,) + shape, lambda r: (r,) + (0,) * len(shape))

    def whole(size):
        return pl.BlockSpec((size,), lambda r: (0,))

    hbm = pl.BlockSpec(memory_space=pl.ANY)
    outs = (
        ((length, 3 * width), BF16),
        ((16, length), F32),
        ((length, 128), F32),
        ((width, length), BF16),
        ((length, width), BF16),
        ((length, width), BF16),
        ((length, fan), BF16),
        ((length, fan), BF16),
        ((length, width), BF16),
        ((length, width), BF16),
        ((SEG_ROW, width), BF16),
    )
    weights = (triple_weight, mixer_weight, expand_weight, shrink_weight)
    return pl.pallas_call(
        layer_kernel,
        grid=(rows,),
        out_shape=tuple(jax.ShapeDtypeStruct((rows,) + shape, kind) for shape, kind in outs),
        in_specs=[
            by_row(length, width),
            pl.BlockSpec((rows, length), lambda r: (0, 0)),
            hbm,
            whole(width),
            whole(width),
            hbm,
            whole(width),
            whole(width),
            whole(width),
            hbm,
            whole(fan),
            hbm,
            whole(width),
            whole(width),
            whole(width),
        ],
        out_specs=tuple(by_row(*shape) for shape, _ in outs),
        scratch_shapes=[pltpu.VMEM(w.shape, BF16) for w in weights]
        + [
            pltpu.VMEM((length // 128, 384, 128), F32),
            pltpu.VMEM((width, length), BF16),
            pltpu.VMEM((length, width), F32),
            pltpu.VMEM((length, width), F32),
            pltpu.SemaphoreType.DMA((4,)),
        ],
        compiler_params=pltpu.CompilerParams(vmem_limit_bytes=56 * MIB),
        cost_estimate=cost(50),
        name="layer",
    )(
        tokens,
        segments,
        triple_weight,
        query_bias,
        value_bias,
        mixer_weight,
        mixer_bias,
        norm_gain,
        norm_shift,
        expand_weight,
        expand_bias,
        shrink_weight,
        shrink_bias,
        final_gain,
        final_shift,
    )


def fixed(shape):
    return pl.BlockSpec(shape, lambda *_: (0,) * len(shape), pipeline_mode=pl.Buffered(1))


def second_grad_kernel(segments, dpooled, scaled, stats, gain, dsecond, dshrunk, sums):
    r = pl.program_id(0)
    length = scaled.shape[1]
    scale_row = gain[...][None, :]
    member = (
        lax.broadcasted_iota(jnp.int32, (SEG_ROW, length), 0) == segments[pl.ds(r, 1), :]
    ).astype(F32)
    counts = jnp.sum(member, axis=1, keepdims=True)
    inner = dpooled[...] / counts * scale_row
    table = jnp.concatenate(split(inner), axis=0)
    member = jnp.concatenate([member, member], axis=0).astype(BF16)
    inner = dot_tn(member, table)
    norm = scaled[0].astype(F32)
    product = inner * norm
    value = stats[0][:, 127:128] * (
        inner
        - jnp.mean(inner, axis=1, keepdims=True)
        - norm * jnp.mean(product, axis=1, keepdims=True)
    )
    low = value.astype(BF16)
    dsecond[0] = value
    dshrunk[0] = low

    @pl.when(r == 0)
    def _():
        sums[...] = jnp.zeros_like(sums)

    sums[0:1, :] += jnp.sum(product, axis=0, keepdims=True) / scale_row
    sums[1:2, :] += jnp.sum(dpooled[...], axis=0, keepdims=True)
    sums[2:3, :] += jnp.sum(low.astype(F32), axis=0, keepdims=True)


def second_grad(segments, dpooled, scaled, stats, gain):
    rows, length, width = scaled.shape

    def by_row(*shape):
        return pl.BlockSpec((1,) + shape, lambda r: (r,) + (0,) * len(shape))

    return pl.pallas_call(
        second_grad_kernel,
        grid=(rows,),
        in_specs=[
            fixed(segments.shape),
            pl.BlockSpec((SEG_ROW, width), lambda r: (r, 0)),
            by_row(length, width),
            by_row(length, 128),
            fixed(gain.shape),
        ],
        out_specs=(by_row(length, width), by_row(length, width), fixed((8, width))),
        out_shape=(
            jax.ShapeDtypeStruct((rows, length, width), F32),
            jax.ShapeDtypeStruct((rows, length, width), BF16),
            jax.ShapeDtypeStruct((8, width), F32),
        ),
        compiler_params=pltpu.CompilerParams(vmem_limit_bytes=16 * MIB),
        cost_estimate=cost(3),
        name="second_grad",
    )(segments, dpooled, scaled, stats, gain)


def put_pair(out, order, g, value, along=1):
    turned = order[2 * g] % 2
    cut = value.shape[along] // 2
    value = value.astype(BF16)
    out[turned] = value[:cut] if along == 0 else value[:, :cut]
    out[1 - turned] = value[cut:] if along == 0 else value[:, cut:]


def put_half(g, send, keep, put):
    @pl.when(g < 2)
    def _():
        put(send)

    @pl.when(g >= 2)
    def _():
        put(keep)


def half_specs(height, width):
    return (
        pl.BlockSpec((2, height, width), lambda g, order: (jnp.minimum(g, 1), 0, 0)),
        pl.BlockSpec((2, height, width), lambda g, order: (jnp.maximum(g - 2, 0), 0, 0)),
    )


def shrink_grad_kernel(half, order, dshrunk, active, out):
    rows, length, width = dshrunk.shape
    value = dot_tn(
        active[...].reshape(rows * length, active.shape[2]), dshrunk[...].reshape(rows * length, width)
    )
    put_pair(out, order, 2 * half + pl.program_id(0), value, 0)


def shrink_grad(half, order, dshrunk, active):
    rows, length, width = dshrunk.shape
    part = active.shape[2] // 4
    return pl.pallas_call(
        functools.partial(shrink_grad_kernel, half),
        grid_spec=pltpu.PrefetchScalarGridSpec(
            num_scalar_prefetch=1,
            grid=(2,),
            in_specs=[
                fixed(dshrunk.shape),
                pl.BlockSpec(
                    (rows, length, part), lambda g, order: (0, 0, order[4 * half + 2 * g] // 2)
                ),
            ],
            out_specs=pl.BlockSpec((2, part // 2, width), lambda g, order: (g, 0, 0)),
        ),
        out_shape=jax.ShapeDtypeStruct((4, part // 2, width), BF16),
        compiler_params=pltpu.CompilerParams(vmem_limit_bytes=20 * MIB),
        cost_estimate=cost(4),
        name="shrink_grad",
    )(order, dshrunk, active)


def expand_grad_kernel(quarter, order, dshrunk, shrink, slope, turned, *refs):
    out, dexpanded, sums = refs[-3:]
    rows, length, width = dshrunk.shape
    part = slope.shape[2]
    dactive = dot_nt(dshrunk[...].reshape(rows * length, width), shrink[...])
    low = (dactive * slope[...].reshape(rows * length, part).astype(F32)).astype(BF16)
    sums[...] = jnp.broadcast_to(jnp.sum(low.astype(F32), axis=0, keepdims=True), sums.shape)
    put_pair(out, order, quarter, dot(turned[...], low))
    dexpanded[...] = low.reshape(rows, length, part)


def expand_grad(quarter, order, dshrunk, shrink_weight, slope, turned, blocks=None):
    rows, length, width = dshrunk.shape
    part = slope.shape[2] // 4
    pair = lambda g, order: order[2 * quarter] // 2
    given = [] if blocks is None else [blocks]
    return pl.pallas_call(
        functools.partial(expand_grad_kernel, quarter),
        grid_spec=pltpu.PrefetchScalarGridSpec(
            num_scalar_prefetch=1,
            grid=(1,),
            in_specs=[
                fixed(dshrunk.shape),
                pl.BlockSpec((part, width), lambda g, order: (pair(g, order), 0)),
                pl.BlockSpec((rows, length, part), lambda g, order: (0, 0, pair(g, order))),
                fixed(turned.shape),
            ]
            + [pl.BlockSpec(memory_space=pl.ANY) for _ in given],
            out_specs=(
                pl.BlockSpec((2, width, part // 2), lambda g, order: (quarter % 2, 0, 0)),
                fixed((rows, length, part)),
                fixed((8, part)),
            ),
        ),
        out_shape=(
            jax.ShapeDtypeStruct((4, width, part // 2), BF16),
            jax.ShapeDtypeStruct((rows, length, part), BF16),
            jax.ShapeDtypeStruct((8, part), F32),
        ),
        input_output_aliases={5: 0} if given else {},
        compiler_params=pltpu.CompilerParams(vmem_limit_bytes=24 * MIB),
        cost_estimate=cost(4),
        name="expand_grad",
    )(order, dshrunk, shrink_weight, slope, turned, *given)


def first_grad_kernel(order, dsecond, expand, *refs):
    *parts, out = refs
    width = parts[0].shape[2]
    value = dsecond[0]
    for q, part in enumerate(parts):
        columns = pl.ds(pl.multiple_of(order[2 * q] // 2 * width, 128), width)
        value = value + dot_nt(part[0], expand[:, columns])
    out[0] = value


def first_grad(order, dsecond, expand_weight, parts):
    rows, length, width = dsecond.shape
    block = pl.BlockSpec((1, length, width), lambda r, order: (r, 0, 0))
    return pl.pallas_call(
        first_grad_kernel,
        grid_spec=pltpu.PrefetchScalarGridSpec(
            num_scalar_prefetch=1,
            grid=(rows,),
            in_specs=[block, fixed(expand_weight.shape)]
            + [pl.BlockSpec((1,) + part.shape[1:], lambda r, order: (r, 0, 0)) for part in parts],
            out_specs=block,
        ),
        out_shape=jax.ShapeDtypeStruct(dsecond.shape, F32),
        compiler_params=pltpu.CompilerParams(vmem_limit_bytes=28 * MIB),
        cost_estimate=cost(5.5),
        name="first_grad",
    )(order, dsecond, expand_weight, *parts)


def turn_kernel(value, out):
    out[...] = jnp.transpose(value[0])


def turn(value):
    rows, length, width = value.shape
    return pl.pallas_call(
        turn_kernel,
        grid=(rows,),
        in_specs=[pl.BlockSpec((1, length, width), lambda r: (r, 0, 0))],
        out_specs=pl.BlockSpec((width, length), lambda r: (0, r)),
        out_shape=jax.ShapeDtypeStruct((width, rows * length), value.dtype),
        compiler_params=pltpu.CompilerParams(vmem_limit_bytes=10 * MIB),
        cost_estimate=cost(1.5),
        name="turn",
    )(value)


def branch_grad_kernel(
    given, scaled, stats, gain, mixer, attended, dbranch, dbranch_low, dattended, dots, sums
):
    r = pl.program_id(0)
    width = given.shape[2]
    dfirst = given[0]
    inner = dfirst * gain[...][None, :]
    norm = scaled[0].astype(F32)
    value = stats[0][:, 0:1] * (
        inner
        - jnp.mean(inner, axis=1, keepdims=True)
        - norm * jnp.mean(inner * norm, axis=1, keepdims=True)
    )
    low = value.astype(BF16)
    dbranch[0] = value
    dbranch_low[0] = low

    @pl.when(r == 0)
    def _():
        sums[...] = jnp.zeros_like(sums)

    sums[0:1, :] += jnp.sum(dfirst * norm, axis=0, keepdims=True)
    sums[1:2, :] += jnp.sum(dfirst, axis=0, keepdims=True)
    sums[2:3, :] += jnp.sum(low.astype(F32), axis=0, keepdims=True)
    dattended[0] = dot_nt(low, mixer[...]).astype(BF16)
    turned = dot_nt(mixer[...], low).astype(BF16)
    product = turned.astype(F32) * attended[0].astype(F32)
    dots[...] = jnp.zeros_like(dots)
    for h in range(width // HEAD_DIM):
        dots[0, h : h + 1, :] = jnp.sum(
            product[h * HEAD_DIM : (h + 1) * HEAD_DIM, :], axis=0, keepdims=True
        )


def branch_grad(dfirst, scaled, stats, gain, mixer_weight, attended):
    rows, length, width = dfirst.shape

    def by_row(*shape):
        return pl.BlockSpec((1,) + shape, lambda r: (r,) + (0,) * len(shape))

    wide, low = by_row(length, width), by_row(length, width)
    return pl.pallas_call(
        branch_grad_kernel,
        grid=(rows,),
        in_specs=[
            wide,
            low,
            by_row(length, 128),
            fixed(gain.shape),
            fixed(mixer_weight.shape),
            by_row(width, length),
        ],
        out_specs=(wide, low, low, by_row(16, length), fixed((8, width))),
        out_shape=(
            jax.ShapeDtypeStruct((rows, length, width), F32),
            jax.ShapeDtypeStruct((rows, length, width), BF16),
            jax.ShapeDtypeStruct((rows, length, width), BF16),
            jax.ShapeDtypeStruct((rows, 16, length), F32),
            jax.ShapeDtypeStruct((8, width), F32),
        ),
        compiler_params=pltpu.CompilerParams(vmem_limit_bytes=28 * MIB),
        cost_estimate=cost(5.5),
        name="branch_grad",
    )(dfirst, scaled, stats, gain, mixer_weight, attended)


def attention_grad_kernel(row, segments, qkv, dattended, spread, dots, dmixed, sums, bias, dkeys, dvalues):
    r = row
    length, width = dattended.shape[1:]
    seg_row = segments[r : r + 1, :]
    seg_col = segment_column(seg_row)
    windows = attention_windows(length)
    for k, (at, low, high) in enumerate(windows):
        same = seg_col[low:high, :] == seg_row[:, at : at + 128]
        bias[k, : high - low, :] = jnp.where(same, 0.0, -1e30)
    dkeys[...] = jnp.zeros_like(dkeys)
    dvalues[...] = jnp.zeros_like(dvalues)
    left = lax.broadcasted_iota(jnp.int32, (1, 128), 1) < HEAD_DIM
    for k, (at, low, high) in enumerate(windows):
        wall = bias[k, : high - low, :]
        wall = jnp.concatenate([wall, wall], axis=1)
        for p in range(width // 128):
            cols = slice(p * 128, p * 128 + 128)
            query = both_heads(qkv[0, at : at + 128, cols])
            keys = qkv[0, low:high, width + p * 128 : width + p * 128 + 128]
            values = qkv[0, low:high, 2 * width + p * 128 : 2 * width + p * 128 + 128]
            grad = both_heads(dattended[0, at : at + 128, cols])
            lse, delta = [
                jnp.concatenate(
                    [ref[0, 2 * p : 2 * p + 1, at : at + 128], ref[0, 2 * p + 1 : 2 * p + 2, at : at + 128]],
                    axis=1,
                )
                for ref in (spread, dots)
            ]
            probs = jnp.exp(dot_nt(keys, query) + wall - lse)
            dscores = (probs * (dot_nt(values, grad) - delta)).astype(BF16)
            dvalues[low:high, cols] += dot(probs.astype(BF16), grad)
            dkeys[low:high, cols] += dot(dscores, query)
            dquery = dot_tn(dscores, keys)
            dmixed[0, at : at + 128, cols] = (
                jnp.where(left, dquery[:128], dquery[128:]) * 0.125
            ).astype(BF16)
    dmixed[0, :, width : 2 * width] = dkeys[...].astype(BF16)
    dmixed[0, :, 2 * width :] = dvalues[...].astype(BF16)

    sums[...] = jnp.zeros_like(sums)
    sums[0:1, :] = jnp.sum(dmixed[0, :, :width].astype(F32), axis=0, keepdims=True)
    sums[1:2, :] = jnp.sum(dmixed[0, :, 2 * width :].astype(F32), axis=0, keepdims=True)


def attention_grad(row, segments, qkv, dattended, spread, dots):
    rows, length, width = dattended.shape

    def by_row(*shape):
        return pl.BlockSpec((1,) + shape, lambda _: (row,) + (0,) * len(shape))

    return pl.pallas_call(
        functools.partial(attention_grad_kernel, row),
        grid=(1,),
        in_specs=[
            fixed(segments.shape),
            by_row(length, 3 * width),
            by_row(length, width),
            by_row(16, length),
            by_row(16, length),
        ],
        out_specs=(fixed((1, length, 3 * width)), fixed((8, width))),
        out_shape=(
            jax.ShapeDtypeStruct((1, length, 3 * width), BF16),
            jax.ShapeDtypeStruct((8, width), F32),
        ),
        scratch_shapes=[
            pltpu.VMEM((length // 128, 384, 128), F32),
            pltpu.VMEM((length, width), F32),
            pltpu.VMEM((length, width), F32),
        ],
        compiler_params=pltpu.CompilerParams(vmem_limit_bytes=20 * MIB),
        cost_estimate=cost(8),
        name="attention_grad",
    )(segments, qkv, dattended, spread, dots)


def triple_grad_kernel(order, turned, attended, dbranch, *refs):
    *dmixed, send, keep = refs
    g = pl.program_id(0)
    rows, length = dbranch.shape[:2]
    pair = order[2 * g] // 2

    @pl.when(pair < 3)
    def _():
        value = dot(turned[:, :length], dmixed[0][0])
        for r in range(1, rows):
            value = value + dot(turned[:, r * length : (r + 1) * length], dmixed[r][0])
        put_half(g, send, keep, lambda out: put_pair(out, order, g, value))

    @pl.when(pair >= 3)
    def _():
        value = dot(attended[0], dbranch[0])
        for r in range(1, rows):
            value = value + dot(attended[r], dbranch[r])
        put_half(g, send, keep, lambda out: put_pair(out, order, g, value))


def triple_grad(order, turned, attended, dmixed, dbranch):
    rows, length, width = dbranch.shape
    shape = jax.ShapeDtypeStruct((4, width, width // 2), BF16)
    return pl.pallas_call(
        triple_grad_kernel,
        grid_spec=pltpu.PrefetchScalarGridSpec(
            num_scalar_prefetch=1,
            grid=(4,),
            in_specs=[fixed(turned.shape), fixed(attended.shape), fixed(dbranch.shape)]
            + [
                pl.BlockSpec(
                    (1, length, width), lambda g, order: (0, 0, jnp.minimum(order[2 * g] // 2, 2))
                )
                for _ in dmixed
            ],
            out_specs=half_specs(width, width // 2),
        ),
        out_shape=(shape, shape),
        compiler_params=pltpu.CompilerParams(vmem_limit_bytes=22 * MIB),
        cost_estimate=cost(7),
        name="triple_grad",
    )(order, turned, attended, dbranch, *dmixed)


def token_grad_kernel(dbranch, triple, *refs):
    *dmixed, out = refs
    r = pl.program_id(0)
    for k, ref in enumerate(dmixed):

        @pl.when(r == k)
        def _():
            out[0] = dbranch[0] + dot_nt(ref[0], triple[...])


def token_grad(dbranch, dmixed, triple_weight):
    rows, length, width = dbranch.shape
    return pl.pallas_call(
        token_grad_kernel,
        grid=(rows,),
        in_specs=[pl.BlockSpec((1, length, width), lambda r: (r, 0, 0)), fixed(triple_weight.shape)]
        + [fixed(part.shape) for part in dmixed],
        out_specs=pl.BlockSpec((1, length, width), lambda r: (r, 0, 0)),
        out_shape=jax.ShapeDtypeStruct(dbranch.shape, F32),
        compiler_params=pltpu.CompilerParams(vmem_limit_bytes=24 * MIB),
        cost_estimate=cost(5.5),
        name="token_grad",
    )(dbranch, triple_weight, *dmixed)


def block_order(me):
    core = bit_of(me, 1)
    one, two = bit_of(me, 2), bit_of(me, 4)
    near, far = jnp.where(core == 0, one, two), jnp.where(core == 0, two, one)
    order = []
    for owner, high, low in ((1 - core, far, near), (core, near, far)):
        for a in (1, 0):
            for b in (1, 0):
                order.append(owner * 4 + (high ^ a) * 2 + (low ^ b))
    order = jnp.stack(order).astype(jnp.int32)
    places = jnp.sum(
        jnp.where(order[None, :] == jnp.arange(8)[:, None], jnp.arange(8)[None, :], 0), axis=1
    ).astype(jnp.int32)
    return order, places


def beside(value, work, starts=(), ends=(), rest=None):
    value, nexts = lax.optimization_barrier((value, [chain.next for chain in starts]))
    for chain, array in zip(starts, nexts):
        chain.next = array
        chain.start()
    result = work(value)
    result, moving = lax.optimization_barrier((result, [chain.moving for chain in ends]))
    if rest is not None:
        rest.keep = result
    for chain, array in zip(ends, moving):
        chain.moving = array
        chain.finish()
    return result


class Summing:
    def __init__(self, send, me, size, whole=True):
        self.me, self.size = me, size
        self.next, self.moving = send, None
        rest = [1 << k for k in range(3, size.bit_length() - 1)]
        steps = [(k, flip(size, *bits)) for k, bits in enumerate(((1, 1), (2, 4), (4, 2)))]
        self.steps = steps + [("halve", bit) for bit in rest]
        if whole:
            self.steps += [("double", bit) for bit in rest[::-1]]
            self.steps += [("join", pairs) for _, pairs in steps[::-1]]

    @property
    def done(self):
        return not self.steps

    def start(self):
        kind, detail = self.steps[0]
        pairs = flip(self.size, detail, detail) if kind in ("halve", "double") else detail
        self.moving = lax.ppermute(self.next, AXIS, pairs)

    def finish(self):
        kind, detail = self.steps.pop(0)
        got = self.moving
        f32 = lambda t: t.astype(F32)
        if kind == 0:
            self.first = got
            self.next = (f32(self.keep[0:2]) + f32(got[0:2])).astype(BF16)
        elif kind == 1:
            self.second = got
            self.next = (f32(self.keep[2:3]) + f32(self.first[2:3]) + f32(got[0:1])).astype(BF16)
        elif kind == 2:
            own = f32(self.keep[3]) + f32(self.first[3]) + f32(self.second[1]) + f32(got[0])
            self.cut(own)
        elif kind == "halve":
            self.cut(self.own + f32(got))
        elif kind == "double":
            mine = bit_of(self.me, detail)
            self.next = jnp.where(
                mine == 0,
                jnp.concatenate([self.next, got], axis=0),
                jnp.concatenate([got, self.next], axis=0),
            )
            self.lift()
        elif len(self.steps):
            self.next = jnp.concatenate([got, self.next], axis=0)
        else:
            self.result = (got, self.next)

    def cut(self, own):
        kind, detail = self.steps[0] if self.steps else (None, None)
        if kind == "halve":
            mine = bit_of(self.me, detail)
            half = own.shape[0] // 2
            self.own = lax.dynamic_slice_in_dim(own, mine * half, half, 0)
            own = lax.dynamic_slice_in_dim(own, (1 - mine) * half, half, 0)
        self.next = own.astype(BF16)
        self.lift()

    def lift(self):
        if self.steps and self.steps[0][0] == "join":
            self.next = self.next[None]


def spread_kernel(ranges, places, *refs):
    outs = refs[2 * len(ranges) :]
    b = pl.program_id(0)
    half = pl.num_programs(0) // 2

    def store(out, value):
        value = value.astype(F32)
        height, width = out.shape
        if value.shape[1] == width:
            out[...] = value
        else:
            out[:, : width // 2] = value[:height]
            out[:, width // 2 :] = value[height:]

    for k, (low, high) in enumerate(ranges):
        here = (b >= low) & (b < high)

        @pl.when(here & (places[b] < half))
        def _():
            store(outs[k], refs[2 * k][0])

        @pl.when(here & (places[b] >= half))
        def _():
            store(outs[k], refs[2 * k + 1][0])


def spread_blocks(places, halves, parts):
    got, own = halves
    half, _, width = got.shape
    in_specs, out_specs, shapes = [], [], []

    def spec(shape, index):
        return pl.BlockSpec(shape, index)

    for shape, along, (low, high), height, skip in parts:
        at = lambda b, low=low, high=high: jnp.clip(b, low, high - 1)
        block = (1, height, width)
        in_specs.append(
            spec(block, lambda b, p, at=at, skip=skip: (jnp.minimum(p[at(b)], half - 1), skip, 0))
        )
        in_specs.append(
            spec(block, lambda b, p, at=at, skip=skip: (jnp.maximum(p[at(b)] - half, 0), skip, 0))
        )
        count = high - low
        if along == 0:
            out = (shape[0] // count, shape[1])
            out_specs.append(spec(out, lambda b, p, at=at, low=low: (at(b) - low, 0)))
        else:
            out = (shape[0], shape[1] // count)
            out_specs.append(spec(out, lambda b, p, at=at, low=low: (0, at(b) - low)))
        shapes.append(jax.ShapeDtypeStruct(shape, F32))
    return pl.pallas_call(
        functools.partial(spread_kernel, [part[2] for part in parts]),
        grid_spec=pltpu.PrefetchScalarGridSpec(
            num_scalar_prefetch=1, grid=(2 * half,), in_specs=in_specs, out_specs=tuple(out_specs)
        ),
        out_shape=tuple(shapes),
        compiler_params=pltpu.CompilerParams(vmem_limit_bytes=20 * MIB),
        cost_estimate=cost(5),
        name="spread_blocks",
    )(places, *(half for _ in parts for half in (got, own)))


def on_device(
    tokens,
    segments,
    pairing,
    pair_weight,
    triple_weight,
    query_bias,
    value_bias,
    mixer_weight,
    mixer_bias,
    norm_gain,
    norm_shift,
    expand_weight,
    expand_bias,
    shrink_weight,
    shrink_bias,
    final_gain,
    final_shift,
):
    rows, length, width = tokens.shape
    fan = expand_weight.shape[1]
    size = lax.axis_size(AXIS)
    me = lax.axis_index(AXIS)
    order, places = block_order(me)
    (
        qkv,
        spread,
        stats,
        attended,
        scaled_a,
        first_low,
        active,
        slope,
        scaled_b,
        output,
        pooled,
    ) = layer(
        tokens,
        segments,
        triple_weight,
        query_bias,
        value_bias,
        mixer_weight,
        mixer_bias,
        norm_gain,
        norm_shift,
        expand_weight,
        expand_bias,
        shrink_weight,
        shrink_bias,
        final_gain,
        final_shift,
    )
    active, slope, qkv, expand_weight, shrink_weight, triple_weight = [
        pltpu.with_memory_space_constraint(array, pltpu.HBM)
        for array in (active, slope, qkv, expand_weight, shrink_weight, triple_weight)
    ]
    own = pooled.reshape(rows * SEG_ROW, width)
    gathered, (first_t, tokens_t) = gather_rows(own, size, [(turn, first_low), (turn, tokens)])
    loss, dpooled = contrast(gathered, own, pairing, pair_weight, me, size)

    dsecond, dshrunk, sums_b = second_grad(segments, dpooled, scaled_b, stats, final_gain)
    one = Summing(shrink_grad(0, order, dshrunk, active), me, size)
    beside(dshrunk, lambda t: shrink_grad(1, order, t, active), [one], [one], one)

    dexpanded, fan_sums = [], []

    def expand_part(quarter, blocks, starts, ends):
        blocks, part, sums = beside(
            dshrunk,
            lambda t: expand_grad(quarter, order, t, shrink_weight, slope, first_t, blocks),
            starts,
            ends,
        )
        dexpanded.append(part)
        fan_sums.append(sums)
        return blocks

    send = expand_part(0, None, [one], [])
    send = expand_part(1, send, [], [])
    two = Summing(send, me, size)
    keep = expand_part(2, None, [], [one])
    two.keep = expand_part(3, keep, [one, two], [one])
    two.moving = lax.optimization_barrier((two.moving, fan_sums[3]))[0]
    two.finish()
    dfirst = beside(
        dsecond, lambda t: first_grad(order, t, expand_weight, dexpanded), [two, one], [one]
    )
    dbranch, dbranch_low, dattended, dots, sums_a = beside(
        dfirst,
        lambda t: branch_grad(t, scaled_a, stats, norm_gain, mixer_weight, attended),
        [one],
        [one, two],
    )
    dmixed, sums_c = [], []
    for row in range(rows):
        part, sums = beside(
            dattended,
            lambda t: attention_grad(row, segments, qkv, t, spread, dots),
            [one, two] if row < 2 else [],
            [two, one] if row < 2 else [],
        )
        dmixed.append(part)
        sums_c.append(sums[0:2])
    send, keep = beside(
        tokens_t,
        lambda t: triple_grad(order, t, attended, dmixed, dbranch_low),
        [one, two],
        [one, two],
    )
    three = Summing(send, me, size)
    three.keep = keep
    fan_sums = jnp.concatenate([part[0:1] for part in fan_sums], axis=0)
    pairs = order[0::2] // 2
    fan_sums = jnp.sum(
        jnp.where(pairs[None, :, None] == jnp.arange(4)[:, None, None], fan_sums[None], 0.0), axis=1
    )
    small = jnp.concatenate([sums_a[0:3], sums_b[0:3], sum(sums_c), fan_sums], axis=0)
    trades = [1 << k for k in range(size.bit_length() - 1)]

    def trade(value):
        if not trades:
            return value
        bit = trades.pop(0)
        return value + lax.ppermute(value, AXIS, flip(size, bit, bit))

    def slot(starts, ends, work=lambda t: t):
        nonlocal small
        small = beside(small, work, starts, ends)

    def spread_beside(chain, parts, others):
        nonlocal small
        small, *grads = beside(
            small, lambda t: (t, *spread_blocks(places, chain.result, parts)), others, others
        )
        return grads

    slot([one, two, three], [three, two])
    tokens_out = beside(
        dbranch, lambda t: token_grad(t, dmixed, triple_weight), [three, two], [one, three, two]
    )
    slot([three, one], [three, one], trade)
    while not one.done:
        slot([three, one], [three, one], trade)
    (dshrink,) = spread_beside(one, [((fan, width), 0, (0, 8), fan // 8, 0)], [three, two])
    slot([three, two], [three], trade)
    slot([three], [three, two], trade)
    while not two.done:
        chains = [chain for chain in (three, two) if not chain.done]
        slot(chains, chains, trade)
    chains = [] if three.done else [three]
    (dexpand,) = spread_beside(two, [((width, fan), 1, (0, 8), width, 0)], chains)
    while trades or not three.done:
        chains = [] if three.done else [three]
        slot(chains, chains, trade)
    dtriple, dmixer = spread_blocks(
        places,
        three.result,
        [((width, 3 * width), 1, (0, 6), width, 0), ((width, width), 1, (6, 8), width, 0)],
    )
    return (
        loss,
        output,
        tokens_out,
        dtriple,
        small[6],
        small[7],
        dmixer,
        small[2],
        small[0],
        small[1],
        dexpand,
        small[8:].reshape(-1),
        dshrink,
        small[5],
        small[3],
        small[4],
    )


def solution(mesh):
    wide = P(AXIS, None, None)
    return jax.shard_map(
        on_device,
        mesh=mesh,
        in_specs=(wide, P(AXIS, None)) + (P(),) * 15,
        out_specs=(P(), wide, wide) + (P(),) * 13,
        check_vma=False,
    )
```

```python
import functools

import jax
import jax.numpy as jnp
from jax import lax
from jax.experimental import pallas as pl
from jax.experimental.pallas import tpu as pltpu
from jax.sharding import PartitionSpec as P

HEADS = 12
HEAD_DIM = 64
SEG_ROW = 8
AXIS = "wide"
F32 = jnp.float32
BF16 = jnp.bfloat16

highest = lax.Precision.HIGHEST
scale = 20.0
MIB = 1024 * 1024


def prefixes(width):
    return (width // 12, width // 6, width // 3, 2 * width // 3, width)


def cost(micros):
    return pl.CostEstimate(flops=int(micros * 1.15e9), bytes_accessed=0, transcendentals=0)


def dot(a, b):
    return jnp.dot(a, b, preferred_element_type=F32)


def dot_nt(a, b):
    return lax.dot_general(a, b, (((1,), (1,)), ((), ())), preferred_element_type=F32)


def dot_tn(a, b):
    return lax.dot_general(a, b, (((0,), (0,)), ((), ())), preferred_element_type=F32)


def window(array, low, high):
    first, last = low // 128 * 128, -(-high // 128) * 128
    piece = array[:, first:last]
    if first == low and last == high:
        return piece, first, last
    lane = first + lax.broadcasted_iota(jnp.int32, (1, last - first), 1)
    return jnp.where((lane >= low) & (lane < high), piece, jnp.zeros_like(piece)), first, last


def split(value):
    high = value.astype(BF16)
    return high, (value - high.astype(F32)).astype(BF16)


def flip(size, low, high):
    return [(i, i ^ (high if i & 1 else low)) for i in range(size)]


def bit_of(me, bit):
    return (me // bit) % 2


def gather_rows(block, size, works):
    bit, results = size // 2, []
    while bit:
        pairs = flip(size, bit, bit)
        if len(results) < len(works):
            work, value = works[len(results)]
            block, value = lax.optimization_barrier((block, value))
            other, result = lax.optimization_barrier((lax.ppermute(block, AXIS, pairs), work(value)))
            results.append(result)
        else:
            other = lax.ppermute(block, AXIS, pairs)
        block = jnp.concatenate([block, other], axis=0)
        bit //= 2
    return block, results


def contrast_kernel(
    size, me_ref, gathered, own_ref, cols_ref, rows_ref, load_col_ref, load_row_ref, loss_ref, grad_ref, table, total, aim
):
    me = me_ref[0]
    count, width = table.shape
    share = own_ref.shape[0]
    block = 128
    levels = size.bit_length() - 1
    for place in range(size):
        mask = sum(((place >> k) & 1) << (levels - 1 - k) for k in range(levels))
        owner = me ^ mask
        table[pl.ds(pl.multiple_of(owner * share, share), share), :] = gathered[
            place * share : (place + 1) * share, :
        ]
    cuts = prefixes(width)
    spans = list(zip((0,) + cuts[:-1], cuts))
    lane_ids = lax.broadcasted_iota(jnp.int32, (1, count), 1)

    def place_pairs(i, carry):
        partner, load = carry
        rows = pl.ds(pl.multiple_of(i * block, block), block)
        hit = cols_ref[rows, 0:1] == lane_ids
        partner = partner + jnp.sum(
            jnp.where(hit, cols_ref[rows, 1:2].astype(F32), 0.0), axis=0, keepdims=True
        )
        load = load + jnp.sum(jnp.where(hit, load_col_ref[rows, :], 0.0), axis=0, keepdims=True)
        return partner, load

    zero_row = jnp.zeros((1, count), F32)
    partner_row, load_row = lax.fori_loop(0, count // block, place_pairs, (zero_row, zero_row))
    own_ids = me * share + lax.broadcasted_iota(jnp.int32, (share, 1), 0)
    hit = rows_ref[0:1, :] == own_ids
    partner_own = jnp.sum(jnp.where(hit, rows_ref[1:2, :].astype(F32), 0.0), axis=1, keepdims=True)
    load_own = jnp.sum(jnp.where(hit, load_row_ref[...], 0.0), axis=1, keepdims=True)

    squares = jnp.zeros((count, 1), F32)
    side = jnp.zeros((count, 128), F32)
    for k, (low, high) in enumerate(spans):
        piece, first, last = window(table, low, high)
        wide = piece.astype(F32)
        squares = squares + jnp.sum(wide * wide, axis=1, keepdims=True)
        lane = lax.broadcasted_iota(jnp.int32, (1, 128), 1)
        side = jnp.where(lane == k, squares, side)
    upright = lax.rsqrt(jnp.transpose(side)[0:8, :] + 1e-06) * scale
    inverse_rows = [upright[k : k + 1, :] for k in range(len(cuts))]

    total[...] = jnp.zeros_like(total)
    aim[...] = jnp.zeros_like(aim)

    def add_rows(i, carry):
        start = pl.multiple_of(i * block, block)
        sims = jnp.zeros((block, count), F32)
        squares = jnp.zeros((block, 1), F32)
        row_ids = (start + lax.broadcasted_iota(jnp.int32, (block, 1), 0)).astype(F32)
        chosen = partner_row == row_ids
        for k, (low, high) in enumerate(spans):
            piece, first, last = window(table.at[pl.ds(start, block), :], low, high)
            wide = piece.astype(F32)
            squares = squares + jnp.sum(wide * wide, axis=1, keepdims=True)
            sims = sims + dot_nt(piece, table[:, first:last])
            value = sims * lax.rsqrt(squares + 1e-06) * inverse_rows[k]
            total[k : k + 1, :] += jnp.sum(jnp.exp(value - scale), axis=0, keepdims=True)
            aim[k : k + 1, :] += jnp.sum(jnp.where(chosen, value, 0.0), axis=0, keepdims=True)
        return carry

    lax.fori_loop(0, count // block, add_rows, 0)

    spreads = scale + jnp.log(total[0 : len(cuts), :])
    gaps = jnp.sum(spreads - aim[0 : len(cuts), :], axis=0, keepdims=True)
    loss_ref[...] = jnp.broadcast_to(
        jnp.sum(gaps * load_row, axis=1, keepdims=True) / count, loss_ref.shape
    )

    sims = jnp.zeros((share, count), F32)
    squares = jnp.zeros((share, 1), F32)
    out_hit = (partner_own == lane_ids.astype(F32)).astype(F32)
    in_hit = (partner_row == own_ids.astype(F32)).astype(F32)
    grad_ref[...] = jnp.zeros_like(grad_ref)
    for k, (low, high) in enumerate(spans):
        piece, first, last = window(own_ref, low, high)
        wide = piece.astype(F32)
        squares = squares + jnp.sum(wide * wide, axis=1, keepdims=True)
        inverse = lax.rsqrt(squares + 1e-06)
        sims = sims + dot_nt(piece, table[:, first:last])
        value = sims * inverse * inverse_rows[k]
        spread = scale + jnp.log(jnp.sum(jnp.exp(value - scale), axis=1, keepdims=True))
        dsims = load_own * (jnp.exp(value - spread) - out_hit) + load_row * (
            jnp.exp(value - spreads[k : k + 1, :]) - in_hit
        )
        big, small = split(dsims * inverse_rows[k])
        unit, _, last = window(own_ref, 0, high)
        unit = unit.astype(F32) * inverse
        dunit = dot(big, table[:, :last]) + dot(small, table[:, :last])
        if last != high:
            lane = lax.broadcasted_iota(jnp.int32, (1, last), 1)
            dunit = jnp.where(lane < high, dunit, 0.0)
        along = jnp.sum(dunit * unit, axis=1, keepdims=True)
        grad_ref[:, :last] += inverse * (dunit - unit * along)


def contrast(gathered, own, pairing, pair_weight, me, size):
    share, width = own.shape
    count = share * size
    vmem = pl.BlockSpec(memory_space=pltpu.VMEM)
    loss, grad = pl.pallas_call(
        functools.partial(contrast_kernel, size),
        out_shape=(
            jax.ShapeDtypeStruct((8, 128), F32),
            jax.ShapeDtypeStruct((share, width), F32),
        ),
        in_specs=[pl.BlockSpec(memory_space=pltpu.SMEM)] + [vmem] * 6,
        out_specs=(vmem, vmem),
        scratch_shapes=[
            pltpu.VMEM((count, width), BF16),
            pltpu.VMEM((8, count), F32),
            pltpu.VMEM((8, count), F32),
        ],
        compiler_params=pltpu.CompilerParams(vmem_limit_bytes=16 * MIB),
        cost_estimate=cost(6),
        name="contrast",
    )(
        me.reshape(1),
        gathered,
        own,
        pairing,
        pairing.T,
        pair_weight[:, None],
        pair_weight[None, :],
    )
    return loss[0, 0], grad


def attention_windows(length):
    block = 128
    return [
        (i, max(0, i - block), min(length, i + 2 * block)) for i in range(0, length, block)
    ]


def segment_column(seg_row):
    wide = jnp.broadcast_to(seg_row.astype(F32), (128, seg_row.shape[1]))
    return jnp.transpose(wide)[:, 0:1].astype(jnp.int32)


def both_heads(pair):
    left = lax.broadcasted_iota(jnp.int32, (1, 128), 1) < HEAD_DIM
    zero = jnp.zeros((), pair.dtype)
    return jnp.concatenate([jnp.where(left, pair, zero), jnp.where(left, zero, pair)], axis=0)


def layer_kernel(
    tokens,
    segments,
    triple_hbm,
    query_bias,
    value_bias,
    mixer_hbm,
    mixer_bias,
    norm_gain,
    norm_shift,
    expand_hbm,
    expand_bias,
    shrink_hbm,
    shrink_bias,
    final_gain,
    final_shift,
    qkv,
    spread,
    stats,
    attended,
    scaled_a,
    first_low,
    active,
    slope,
    scaled_b,
    output,
    pooled,
    triple,
    mixer,
    expand,
    shrink,
    bias,
    joined,
    first,
    total,
    sems,
):
    step = pl.program_id(0)
    length, width = tokens.shape[1:]
    fan = expand.shape[1]
    held = (triple, mixer, expand, shrink)
    copies = [
        pltpu.make_async_copy(src, dst, sems.at[k])
        for k, (src, dst) in enumerate(zip((triple_hbm, mixer_hbm, expand_hbm, shrink_hbm), held))
    ]

    @pl.when(step == 0)
    def _():
        for copy in copies:
            copy.start()
        copies[0].wait()

    seg_row = segments[pl.ds(step, 1), :]
    seg_col = segment_column(seg_row)
    windows = attention_windows(length)
    for k, (at, low, high) in enumerate(windows):
        same = seg_col[low:high, :] == seg_row[:, at : at + 128]
        bias[k, : high - low, :] = jnp.where(same, 0.0, -1e30)

    chunk = width
    x = tokens[0]
    mixed = dot(x, triple[:, 0:chunk]) + query_bias[...][None, :]
    qkv[0, :, 0:chunk] = (mixed.astype(BF16).astype(F32) * 0.125).astype(BF16)
    qkv[0, :, chunk : 2 * chunk] = dot(x, triple[:, chunk : 2 * chunk]).astype(BF16)
    qkv[0, :, 2 * chunk :] = (dot(x, triple[:, 2 * chunk :]) + value_bias[...][None, :]).astype(BF16)

    left = lax.broadcasted_iota(jnp.int32, (1, 128), 1) < HEAD_DIM
    spread[...] = jnp.zeros_like(spread)
    for k, (at, low, high) in enumerate(windows):
        wall = bias[k, : high - low, :]
        wall = jnp.concatenate([wall, wall], axis=1)
        for p in range(width // 128):
            cols = slice(p * 128, p * 128 + 128)
            query = both_heads(qkv[0, at : at + 128, cols])
            keys = qkv[0, low:high, width + p * 128 : width + p * 128 + 128]
            scores = dot_nt(keys, query) + wall
            top = jnp.max(scores, axis=0, keepdims=True)
            expo = jnp.exp(scores - top)
            amount = jnp.sum(expo, axis=0, keepdims=True)
            values = qkv[0, low:high, 2 * width + p * 128 : 2 * width + p * 128 + 128]
            share = jnp.transpose(jnp.broadcast_to(1.0 / amount, (128, amount.shape[1])))
            found = dot_tn(expo.astype(BF16), values) * share
            joined[at : at + 128, cols] = jnp.where(left, found[:128], found[128:]).astype(BF16)
            marks = top + jnp.log(amount)
            spread[0, 2 * p : 2 * p + 1, at : at + 128] = marks[:, :128]
            spread[0, 2 * p + 1 : 2 * p + 2, at : at + 128] = marks[:, 128:]

    attended[0] = jnp.transpose(joined[...])

    @pl.when(step == 0)
    def _():
        copies[1].wait()

    summed = tokens[0].astype(F32) + (dot(joined[...], mixer[...]) + mixer_bias[...][None, :])
    centre = summed - jnp.mean(summed, axis=1, keepdims=True)
    inverse = lax.rsqrt(jnp.mean(centre * centre, axis=1, keepdims=True) + 1e-05)
    scaled = centre * inverse
    scaled_a[0] = scaled.astype(BF16)
    inverse_a = inverse
    value = scaled * norm_gain[...][None, :] + norm_shift[...][None, :]
    first[...] = value
    first_low[0] = value.astype(BF16)

    @pl.when(step == 0)
    def _():
        copies[2].wait()
        copies[3].wait()

    part = 1024
    for j in range(fan // part):
        cols = slice(j * part, (j + 1) * part)
        value = dot(first_low[0], expand[:, cols]) + expand_bias[cols][None, :]
        gauss = jnp.exp(value * value * -0.5)
        near = 1.0 / (1.0 + 0.3275911 * 0.7071067811865476 * jnp.abs(value))
        poly = near * (
            0.5 * 0.254829592
            + near
            * (
                0.5 * -0.284496736
                + near * (0.5 * 1.421413741 + near * (0.5 * -1.453152027 + near * (0.5 * 1.061405429)))
            )
        )
        tail = poly * gauss
        below = jnp.where(value < 0, tail, 1.0 - tail)
        rounded = (value * below).astype(BF16)
        active[0, :, cols] = rounded
        slope[0, :, cols] = (below + value * (gauss * 0.3989422804014327)).astype(BF16)
        product = dot(rounded, shrink[cols, :])
        if j == 0:
            total[...] = product
        else:
            total[...] += product

    summed = first[...] + (total[...] + shrink_bias[...][None, :])
    centre = summed - jnp.mean(summed, axis=1, keepdims=True)
    inverse = lax.rsqrt(jnp.mean(centre * centre, axis=1, keepdims=True) + 1e-05)
    scaled = centre * inverse
    scaled_b[0] = scaled.astype(BF16)
    lane = lax.broadcasted_iota(jnp.int32, (1, 128), 1)
    stats[0] = jnp.where(lane == 0, inverse_a, inverse)
    final = scaled * final_gain[...][None, :] + final_shift[...][None, :]
    output[0] = final.astype(BF16)
    member = (
        lax.broadcasted_iota(jnp.int32, (SEG_ROW, length), 0) == seg_row
    ).astype(F32)
    counts = jnp.sum(member, axis=1, keepdims=True)
    gathered = jnp.dot(member, final, preferred_element_type=F32, precision=highest)
    pooled[0] = (gathered / counts).astype(BF16)


def layer(tokens, segments, triple_weight, query_bias, value_bias, mixer_weight, mixer_bias, norm_gain, norm_shift, expand_weight, expand_bias, shrink_weight, shrink_bias, final_gain, final_shift):
    rows, length, width = tokens.shape
    fan = expand_weight.shape[1]

    def by_row(*shape):
        return pl.BlockSpec((1,) + shape, lambda r: (r,) + (0,) * len(shape))

    def whole(size):
        return pl.BlockSpec((size,), lambda r: (0,))

    hbm = pl.BlockSpec(memory_space=pl.ANY)
    outs = (
        ((length, 3 * width), BF16),
        ((16, length), F32),
        ((length, 128), F32),
        ((width, length), BF16),
        ((length, width), BF16),
        ((length, width), BF16),
        ((length, fan), BF16),
        ((length, fan), BF16),
        ((length, width), BF16),
        ((length, width), BF16),
        ((SEG_ROW, width), BF16),
    )
    weights = (triple_weight, mixer_weight, expand_weight, shrink_weight)
    return pl.pallas_call(
        layer_kernel,
        grid=(rows,),
        out_shape=tuple(jax.ShapeDtypeStruct((rows,) + shape, kind) for shape, kind in outs),
        in_specs=[
            by_row(length, width),
            pl.BlockSpec((rows, length), lambda r: (0, 0)),
            hbm,
            whole(width),
            whole(width),
            hbm,
            whole(width),
            whole(width),
            whole(width),
            hbm,
            whole(fan),
            hbm,
            whole(width),
            whole(width),
            whole(width),
        ],
        out_specs=tuple(by_row(*shape) for shape, _ in outs),
        scratch_shapes=[pltpu.VMEM(w.shape, BF16) for w in weights]
        + [
            pltpu.VMEM((length // 128, 384, 128), F32),
            pltpu.VMEM((length, width), BF16),
            pltpu.VMEM((length, width), F32),
            pltpu.VMEM((length, width), F32),
            pltpu.SemaphoreType.DMA((4,)),
        ],
        compiler_params=pltpu.CompilerParams(vmem_limit_bytes=56 * MIB),
        cost_estimate=cost(50),
        name="layer",
    )(
        tokens,
        segments,
        triple_weight,
        query_bias,
        value_bias,
        mixer_weight,
        mixer_bias,
        norm_gain,
        norm_shift,
        expand_weight,
        expand_bias,
        shrink_weight,
        shrink_bias,
        final_gain,
        final_shift,
    )


def fixed(shape):
    return pl.BlockSpec(shape, lambda *_: (0,) * len(shape), pipeline_mode=pl.Buffered(1))


def second_grad_kernel(segments, dpooled, scaled, stats, gain, dsecond, dshrunk, sums):
    r = pl.program_id(0)
    length = scaled.shape[1]
    scale_row = gain[...][None, :]
    member = (
        lax.broadcasted_iota(jnp.int32, (SEG_ROW, length), 0) == segments[pl.ds(r, 1), :]
    ).astype(F32)
    counts = jnp.sum(member, axis=1, keepdims=True)
    inner = dpooled[...] / counts * scale_row
    table = jnp.concatenate(split(inner), axis=0)
    member = jnp.concatenate([member, member], axis=0).astype(BF16)
    inner = dot_tn(member, table)
    norm = scaled[0].astype(F32)
    product = inner * norm
    value = stats[0][:, 127:128] * (
        inner
        - jnp.mean(inner, axis=1, keepdims=True)
        - norm * jnp.mean(product, axis=1, keepdims=True)
    )
    low = value.astype(BF16)
    dsecond[0] = value
    dshrunk[0] = low

    @pl.when(r == 0)
    def _():
        sums[...] = jnp.zeros_like(sums)

    sums[0:1, :] += jnp.sum(product, axis=0, keepdims=True) / scale_row
    sums[1:2, :] += jnp.sum(dpooled[...], axis=0, keepdims=True)
    sums[2:3, :] += jnp.sum(low.astype(F32), axis=0, keepdims=True)


def second_grad(segments, dpooled, scaled, stats, gain):
    rows, length, width = scaled.shape

    def by_row(*shape):
        return pl.BlockSpec((1,) + shape, lambda r: (r,) + (0,) * len(shape))

    return pl.pallas_call(
        second_grad_kernel,
        grid=(rows,),
        in_specs=[
            fixed(segments.shape),
            pl.BlockSpec((SEG_ROW, width), lambda r: (r, 0)),
            by_row(length, width),
            by_row(length, 128),
            fixed(gain.shape),
        ],
        out_specs=(by_row(length, width), by_row(length, width), fixed((8, width))),
        out_shape=(
            jax.ShapeDtypeStruct((rows, length, width), F32),
            jax.ShapeDtypeStruct((rows, length, width), BF16),
            jax.ShapeDtypeStruct((8, width), F32),
        ),
        compiler_params=pltpu.CompilerParams(vmem_limit_bytes=16 * MIB),
        cost_estimate=cost(3),
        name="second_grad",
    )(segments, dpooled, scaled, stats, gain)


def put_pair(out, order, g, value, along=1):
    turned = order[2 * g] % 2
    cut = value.shape[along] // 2
    value = value.astype(BF16)
    out[turned] = value[:cut] if along == 0 else value[:, :cut]
    out[1 - turned] = value[cut:] if along == 0 else value[:, cut:]


def put_half(g, send, keep, put):
    @pl.when(g < 2)
    def _():
        put(send)

    @pl.when(g >= 2)
    def _():
        put(keep)


def half_specs(height, width):
    return (
        pl.BlockSpec((2, height, width), lambda g, order: (jnp.minimum(g, 1), 0, 0)),
        pl.BlockSpec((2, height, width), lambda g, order: (jnp.maximum(g - 2, 0), 0, 0)),
    )


def shrink_grad_kernel(half, order, dshrunk, active, out):
    rows, length, width = dshrunk.shape
    value = dot_tn(
        active[...].reshape(rows * length, active.shape[2]), dshrunk[...].reshape(rows * length, width)
    )
    put_pair(out, order, 2 * half + pl.program_id(0), value, 0)


def shrink_grad(half, order, dshrunk, active):
    rows, length, width = dshrunk.shape
    part = active.shape[2] // 4
    return pl.pallas_call(
        functools.partial(shrink_grad_kernel, half),
        grid_spec=pltpu.PrefetchScalarGridSpec(
            num_scalar_prefetch=1,
            grid=(2,),
            in_specs=[
                fixed(dshrunk.shape),
                pl.BlockSpec(
                    (rows, length, part), lambda g, order: (0, 0, order[4 * half + 2 * g] // 2)
                ),
            ],
            out_specs=pl.BlockSpec((2, part // 2, width), lambda g, order: (g, 0, 0)),
        ),
        out_shape=jax.ShapeDtypeStruct((4, part // 2, width), BF16),
        compiler_params=pltpu.CompilerParams(vmem_limit_bytes=20 * MIB),
        cost_estimate=cost(4),
        name="shrink_grad",
    )(order, dshrunk, active)


def expand_grad_kernel(quarter, order, dshrunk, shrink, slope, turned, *refs):
    out, dexpanded, sums = refs[-3:]
    rows, length, width = dshrunk.shape
    part = slope.shape[2]
    dactive = dot_nt(dshrunk[...].reshape(rows * length, width), shrink[...])
    low = (dactive * slope[...].reshape(rows * length, part).astype(F32)).astype(BF16)
    sums[...] = jnp.broadcast_to(jnp.sum(low.astype(F32), axis=0, keepdims=True), sums.shape)
    put_pair(out, order, quarter, dot(turned[...], low))
    dexpanded[...] = low.reshape(rows, length, part)


def expand_grad(quarter, order, dshrunk, shrink_weight, slope, turned, blocks=None):
    rows, length, width = dshrunk.shape
    part = slope.shape[2] // 4
    pair = lambda g, order: order[2 * quarter] // 2
    given = [] if blocks is None else [blocks]
    return pl.pallas_call(
        functools.partial(expand_grad_kernel, quarter),
        grid_spec=pltpu.PrefetchScalarGridSpec(
            num_scalar_prefetch=1,
            grid=(1,),
            in_specs=[
                fixed(dshrunk.shape),
                pl.BlockSpec((part, width), lambda g, order: (pair(g, order), 0)),
                pl.BlockSpec((rows, length, part), lambda g, order: (0, 0, pair(g, order))),
                fixed(turned.shape),
            ]
            + [pl.BlockSpec(memory_space=pl.ANY) for _ in given],
            out_specs=(
                pl.BlockSpec((2, width, part // 2), lambda g, order: (quarter % 2, 0, 0)),
                fixed((rows, length, part)),
                fixed((8, part)),
            ),
        ),
        out_shape=(
            jax.ShapeDtypeStruct((4, width, part // 2), BF16),
            jax.ShapeDtypeStruct((rows, length, part), BF16),
            jax.ShapeDtypeStruct((8, part), F32),
        ),
        input_output_aliases={5: 0} if given else {},
        compiler_params=pltpu.CompilerParams(vmem_limit_bytes=24 * MIB),
        cost_estimate=cost(4),
        name="expand_grad",
    )(order, dshrunk, shrink_weight, slope, turned, *given)


def first_grad_kernel(order, dsecond, expand, *refs):
    *parts, out = refs
    width = parts[0].shape[2]
    value = dsecond[0]
    for q, part in enumerate(parts):
        columns = pl.ds(pl.multiple_of(order[2 * q] // 2 * width, 128), width)
        value = value + dot_nt(part[0], expand[:, columns])
    out[0] = value


def first_grad(order, dsecond, expand_weight, parts):
    rows, length, width = dsecond.shape
    block = pl.BlockSpec((1, length, width), lambda r, order: (r, 0, 0))
    return pl.pallas_call(
        first_grad_kernel,
        grid_spec=pltpu.PrefetchScalarGridSpec(
            num_scalar_prefetch=1,
            grid=(rows,),
            in_specs=[block, fixed(expand_weight.shape)]
            + [pl.BlockSpec((1,) + part.shape[1:], lambda r, order: (r, 0, 0)) for part in parts],
            out_specs=block,
        ),
        out_shape=jax.ShapeDtypeStruct(dsecond.shape, F32),
        compiler_params=pltpu.CompilerParams(vmem_limit_bytes=28 * MIB),
        cost_estimate=cost(5.5),
        name="first_grad",
    )(order, dsecond, expand_weight, *parts)


def turn_kernel(value, out):
    out[...] = jnp.transpose(value[0])


def turn(value):
    rows, length, width = value.shape
    return pl.pallas_call(
        turn_kernel,
        grid=(rows,),
        in_specs=[pl.BlockSpec((1, length, width), lambda r: (r, 0, 0))],
        out_specs=pl.BlockSpec((width, length), lambda r: (0, r)),
        out_shape=jax.ShapeDtypeStruct((width, rows * length), value.dtype),
        compiler_params=pltpu.CompilerParams(vmem_limit_bytes=10 * MIB),
        cost_estimate=cost(1.5),
        name="turn",
    )(value)


def branch_grad_kernel(
    given, scaled, stats, gain, mixer, attended, dbranch, dbranch_low, dattended, dots, sums
):
    r = pl.program_id(0)
    width = given.shape[2]
    dfirst = given[0]
    inner = dfirst * gain[...][None, :]
    norm = scaled[0].astype(F32)
    value = stats[0][:, 0:1] * (
        inner
        - jnp.mean(inner, axis=1, keepdims=True)
        - norm * jnp.mean(inner * norm, axis=1, keepdims=True)
    )
    low = value.astype(BF16)
    dbranch[0] = value
    dbranch_low[0] = low

    @pl.when(r == 0)
    def _():
        sums[...] = jnp.zeros_like(sums)

    sums[0:1, :] += jnp.sum(dfirst * norm, axis=0, keepdims=True)
    sums[1:2, :] += jnp.sum(dfirst, axis=0, keepdims=True)
    sums[2:3, :] += jnp.sum(low.astype(F32), axis=0, keepdims=True)
    dattended[0] = dot_nt(low, mixer[...]).astype(BF16)
    turned = dot_nt(mixer[...], low).astype(BF16)
    product = turned.astype(F32) * attended[0].astype(F32)
    dots[...] = jnp.zeros_like(dots)
    for h in range(width // HEAD_DIM):
        dots[0, h : h + 1, :] = jnp.sum(
            product[h * HEAD_DIM : (h + 1) * HEAD_DIM, :], axis=0, keepdims=True
        )


def branch_grad(dfirst, scaled, stats, gain, mixer_weight, attended):
    rows, length, width = dfirst.shape

    def by_row(*shape):
        return pl.BlockSpec((1,) + shape, lambda r: (r,) + (0,) * len(shape))

    wide, low = by_row(length, width), by_row(length, width)
    return pl.pallas_call(
        branch_grad_kernel,
        grid=(rows,),
        in_specs=[
            wide,
            low,
            by_row(length, 128),
            fixed(gain.shape),
            fixed(mixer_weight.shape),
            by_row(width, length),
        ],
        out_specs=(wide, low, low, by_row(16, length), fixed((8, width))),
        out_shape=(
            jax.ShapeDtypeStruct((rows, length, width), F32),
            jax.ShapeDtypeStruct((rows, length, width), BF16),
            jax.ShapeDtypeStruct((rows, length, width), BF16),
            jax.ShapeDtypeStruct((rows, 16, length), F32),
            jax.ShapeDtypeStruct((8, width), F32),
        ),
        compiler_params=pltpu.CompilerParams(vmem_limit_bytes=28 * MIB),
        cost_estimate=cost(5.5),
        name="branch_grad",
    )(dfirst, scaled, stats, gain, mixer_weight, attended)


def attention_grad_kernel(row, segments, qkv, dattended, spread, dots, dmixed, sums, bias, dkeys, dvalues):
    r = row
    length, width = dattended.shape[1:]
    seg_row = segments[r : r + 1, :]
    seg_col = segment_column(seg_row)
    windows = attention_windows(length)
    for k, (at, low, high) in enumerate(windows):
        same = seg_col[low:high, :] == seg_row[:, at : at + 128]
        bias[k, : high - low, :] = jnp.where(same, 0.0, -1e30)
    dkeys[...] = jnp.zeros_like(dkeys)
    dvalues[...] = jnp.zeros_like(dvalues)
    left = lax.broadcasted_iota(jnp.int32, (1, 128), 1) < HEAD_DIM
    for k, (at, low, high) in enumerate(windows):
        wall = bias[k, : high - low, :]
        wall = jnp.concatenate([wall, wall], axis=1)
        for p in range(width // 128):
            cols = slice(p * 128, p * 128 + 128)
            query = both_heads(qkv[0, at : at + 128, cols])
            keys = qkv[0, low:high, width + p * 128 : width + p * 128 + 128]
            values = qkv[0, low:high, 2 * width + p * 128 : 2 * width + p * 128 + 128]
            grad = both_heads(dattended[0, at : at + 128, cols])
            lse, delta = [
                jnp.concatenate(
                    [ref[0, 2 * p : 2 * p + 1, at : at + 128], ref[0, 2 * p + 1 : 2 * p + 2, at : at + 128]],
                    axis=1,
                )
                for ref in (spread, dots)
            ]
            probs = jnp.exp(dot_nt(keys, query) + wall - lse)
            dscores = (probs * (dot_nt(values, grad) - delta)).astype(BF16)
            dvalues[low:high, cols] += dot(probs.astype(BF16), grad)
            dkeys[low:high, cols] += dot(dscores, query)
            dquery = dot_tn(dscores, keys)
            dmixed[0, at : at + 128, cols] = (
                jnp.where(left, dquery[:128], dquery[128:]) * 0.125
            ).astype(BF16)
    dmixed[0, :, width : 2 * width] = dkeys[...].astype(BF16)
    dmixed[0, :, 2 * width :] = dvalues[...].astype(BF16)

    sums[...] = jnp.zeros_like(sums)
    sums[0:1, :] = jnp.sum(dmixed[0, :, :width].astype(F32), axis=0, keepdims=True)
    sums[1:2, :] = jnp.sum(dmixed[0, :, 2 * width :].astype(F32), axis=0, keepdims=True)


def attention_grad(row, segments, qkv, dattended, spread, dots):
    rows, length, width = dattended.shape

    def by_row(*shape):
        return pl.BlockSpec((1,) + shape, lambda _: (row,) + (0,) * len(shape))

    return pl.pallas_call(
        functools.partial(attention_grad_kernel, row),
        grid=(1,),
        in_specs=[
            fixed(segments.shape),
            by_row(length, 3 * width),
            by_row(length, width),
            by_row(16, length),
            by_row(16, length),
        ],
        out_specs=(fixed((1, length, 3 * width)), fixed((8, width))),
        out_shape=(
            jax.ShapeDtypeStruct((1, length, 3 * width), BF16),
            jax.ShapeDtypeStruct((8, width), F32),
        ),
        scratch_shapes=[
            pltpu.VMEM((length // 128, 384, 128), F32),
            pltpu.VMEM((length, width), F32),
            pltpu.VMEM((length, width), F32),
        ],
        compiler_params=pltpu.CompilerParams(vmem_limit_bytes=20 * MIB),
        cost_estimate=cost(8),
        name="attention_grad",
    )(segments, qkv, dattended, spread, dots)


def triple_grad_kernel(order, turned, attended, dbranch, *refs):
    *dmixed, send, keep = refs
    g = pl.program_id(0)
    rows, length = dbranch.shape[:2]
    pair = order[2 * g] // 2

    @pl.when(pair < 3)
    def _():
        value = dot(turned[:, :length], dmixed[0][0])
        for r in range(1, rows):
            value = value + dot(turned[:, r * length : (r + 1) * length], dmixed[r][0])
        put_half(g, send, keep, lambda out: put_pair(out, order, g, value))

    @pl.when(pair >= 3)
    def _():
        value = dot(attended[0], dbranch[0])
        for r in range(1, rows):
            value = value + dot(attended[r], dbranch[r])
        put_half(g, send, keep, lambda out: put_pair(out, order, g, value))


def triple_grad(order, turned, attended, dmixed, dbranch):
    rows, length, width = dbranch.shape
    shape = jax.ShapeDtypeStruct((4, width, width // 2), BF16)
    return pl.pallas_call(
        triple_grad_kernel,
        grid_spec=pltpu.PrefetchScalarGridSpec(
            num_scalar_prefetch=1,
            grid=(4,),
            in_specs=[fixed(turned.shape), fixed(attended.shape), fixed(dbranch.shape)]
            + [
                pl.BlockSpec(
                    (1, length, width), lambda g, order: (0, 0, jnp.minimum(order[2 * g] // 2, 2))
                )
                for _ in dmixed
            ],
            out_specs=half_specs(width, width // 2),
        ),
        out_shape=(shape, shape),
        compiler_params=pltpu.CompilerParams(vmem_limit_bytes=22 * MIB),
        cost_estimate=cost(7),
        name="triple_grad",
    )(order, turned, attended, dbranch, *dmixed)


def token_grad_kernel(dbranch, triple, *refs):
    *dmixed, out = refs
    r = pl.program_id(0)
    for k, ref in enumerate(dmixed):

        @pl.when(r == k)
        def _():
            out[0] = dbranch[0] + dot_nt(ref[0], triple[...])


def token_grad(dbranch, dmixed, triple_weight):
    rows, length, width = dbranch.shape
    return pl.pallas_call(
        token_grad_kernel,
        grid=(rows,),
        in_specs=[pl.BlockSpec((1, length, width), lambda r: (r, 0, 0)), fixed(triple_weight.shape)]
        + [fixed(part.shape) for part in dmixed],
        out_specs=pl.BlockSpec((1, length, width), lambda r: (r, 0, 0)),
        out_shape=jax.ShapeDtypeStruct(dbranch.shape, F32),
        compiler_params=pltpu.CompilerParams(vmem_limit_bytes=24 * MIB),
        cost_estimate=cost(5.5),
        name="token_grad",
    )(dbranch, triple_weight, *dmixed)


def block_order(me):
    core = bit_of(me, 1)
    one, two = bit_of(me, 2), bit_of(me, 4)
    near, far = jnp.where(core == 0, one, two), jnp.where(core == 0, two, one)
    order = []
    for owner, high, low in ((1 - core, far, near), (core, near, far)):
        for a in (1, 0):
            for b in (1, 0):
                order.append(owner * 4 + (high ^ a) * 2 + (low ^ b))
    order = jnp.stack(order).astype(jnp.int32)
    places = jnp.sum(
        jnp.where(order[None, :] == jnp.arange(8)[:, None], jnp.arange(8)[None, :], 0), axis=1
    ).astype(jnp.int32)
    return order, places


def beside(value, work, starts=(), ends=(), rest=None):
    value, nexts = lax.optimization_barrier((value, [chain.next for chain in starts]))
    for chain, array in zip(starts, nexts):
        chain.next = array
        chain.start()
    result = work(value)
    result, moving = lax.optimization_barrier((result, [chain.moving for chain in ends]))
    if rest is not None:
        rest.keep = result
    for chain, array in zip(ends, moving):
        chain.moving = array
        chain.finish()
    return result


class Summing:
    def __init__(self, send, me, size, whole=True):
        self.me, self.size = me, size
        self.next, self.moving = send, None
        rest = [1 << k for k in range(3, size.bit_length() - 1)]
        steps = [(k, flip(size, *bits)) for k, bits in enumerate(((1, 1), (2, 4), (4, 2)))]
        self.steps = steps + [("halve", bit) for bit in rest]
        if whole:
            self.steps += [("double", bit) for bit in rest[::-1]]
            self.steps += [("join", pairs) for _, pairs in steps[::-1]]

    @property
    def done(self):
        return not self.steps

    def start(self):
        kind, detail = self.steps[0]
        pairs = flip(self.size, detail, detail) if kind in ("halve", "double") else detail
        self.moving = lax.ppermute(self.next, AXIS, pairs)

    def finish(self):
        kind, detail = self.steps.pop(0)
        got = self.moving
        f32 = lambda t: t.astype(F32)
        if kind == 0:
            self.first = got
            self.next = (f32(self.keep[0:2]) + f32(got[0:2])).astype(BF16)
        elif kind == 1:
            self.second = got
            self.next = (f32(self.keep[2:3]) + f32(self.first[2:3]) + f32(got[0:1])).astype(BF16)
        elif kind == 2:
            own = f32(self.keep[3]) + f32(self.first[3]) + f32(self.second[1]) + f32(got[0])
            self.cut(own)
        elif kind == "halve":
            self.cut(self.own + f32(got))
        elif kind == "double":
            mine = bit_of(self.me, detail)
            self.next = jnp.where(
                mine == 0,
                jnp.concatenate([self.next, got], axis=0),
                jnp.concatenate([got, self.next], axis=0),
            )
            self.lift()
        elif len(self.steps):
            self.next = jnp.concatenate([got, self.next], axis=0)
        else:
            self.result = (got, self.next)

    def cut(self, own):
        kind, detail = self.steps[0] if self.steps else (None, None)
        if kind == "halve":
            mine = bit_of(self.me, detail)
            half = own.shape[0] // 2
            self.own = lax.dynamic_slice_in_dim(own, mine * half, half, 0)
            own = lax.dynamic_slice_in_dim(own, (1 - mine) * half, half, 0)
        self.next = own.astype(BF16)
        self.lift()

    def lift(self):
        if self.steps and self.steps[0][0] == "join":
            self.next = self.next[None]


def spread_kernel(ranges, places, *refs):
    outs = refs[2 * len(ranges) :]
    b = pl.program_id(0)
    half = pl.num_programs(0) // 2

    def store(out, value):
        value = value.astype(F32)
        height, width = out.shape
        if value.shape[1] == width:
            out[...] = value
        else:
            out[:, : width // 2] = value[:height]
            out[:, width // 2 :] = value[height:]

    for k, (low, high) in enumerate(ranges):
        here = (b >= low) & (b < high)

        @pl.when(here & (places[b] < half))
        def _():
            store(outs[k], refs[2 * k][0])

        @pl.when(here & (places[b] >= half))
        def _():
            store(outs[k], refs[2 * k + 1][0])


def spread_blocks(places, halves, parts):
    got, own = halves
    half, _, width = got.shape
    in_specs, out_specs, shapes = [], [], []

    def spec(shape, index):
        return pl.BlockSpec(shape, index)

    for shape, along, (low, high), height, skip in parts:
        at = lambda b, low=low, high=high: jnp.clip(b, low, high - 1)
        block = (1, height, width)
        in_specs.append(
            spec(block, lambda b, p, at=at, skip=skip: (jnp.minimum(p[at(b)], half - 1), skip, 0))
        )
        in_specs.append(
            spec(block, lambda b, p, at=at, skip=skip: (jnp.maximum(p[at(b)] - half, 0), skip, 0))
        )
        count = high - low
        if along == 0:
            out = (shape[0] // count, shape[1])
            out_specs.append(spec(out, lambda b, p, at=at, low=low: (at(b) - low, 0)))
        else:
            out = (shape[0], shape[1] // count)
            out_specs.append(spec(out, lambda b, p, at=at, low=low: (0, at(b) - low)))
        shapes.append(jax.ShapeDtypeStruct(shape, F32))
    return pl.pallas_call(
        functools.partial(spread_kernel, [part[2] for part in parts]),
        grid_spec=pltpu.PrefetchScalarGridSpec(
            num_scalar_prefetch=1, grid=(2 * half,), in_specs=in_specs, out_specs=tuple(out_specs)
        ),
        out_shape=tuple(shapes),
        compiler_params=pltpu.CompilerParams(vmem_limit_bytes=20 * MIB),
        cost_estimate=cost(5),
        name="spread_blocks",
    )(places, *(half for _ in parts for half in (got, own)))


def settle_kernel(first, order, half, *refs):
    triple, mixer, wide, sems = refs[-4:]
    width = wide.shape[2]
    split_at = triple.shape[1] // width
    copies = []
    for k in range(4):
        slot, label = k % 2, order[first + k]
        if k >= 2:
            copies[k - 2].wait()
        wide[slot] = half[k].astype(F32)

        @pl.when(label < split_at)
        def _():
            at = pl.multiple_of(label * width, 128)
            pltpu.make_async_copy(wide.at[slot], triple.at[:, pl.ds(at, width)], sems.at[slot]).start()

        @pl.when(label >= split_at)
        def _():
            at = pl.multiple_of((label - split_at) * width, 128)
            pltpu.make_async_copy(wide.at[slot], mixer.at[:, pl.ds(at, width)], sems.at[slot]).start()

        copies.append(pltpu.make_async_copy(wide.at[slot], mixer.at[:, pl.ds(0, width)], sems.at[slot]))
    copies[2].wait()
    copies[3].wait()


def settle(first, order, half, grads=None):
    _, height, width = half.shape
    shapes = (
        jax.ShapeDtypeStruct((height, 3 * height), F32),
        jax.ShapeDtypeStruct((height, height), F32),
    )
    given = [] if grads is None else list(grads)
    far = pl.BlockSpec(memory_space=pl.ANY)
    return pl.pallas_call(
        functools.partial(settle_kernel, first),
        grid_spec=pltpu.PrefetchScalarGridSpec(
            num_scalar_prefetch=1,
            grid=(1,),
            in_specs=[fixed(half.shape)] + [far] * len(given),
            out_specs=(far, far),
            scratch_shapes=[pltpu.VMEM((2, height, width), F32), pltpu.SemaphoreType.DMA((2,))],
        ),
        out_shape=shapes,
        input_output_aliases={2: 0, 3: 1} if given else {},
        compiler_params=pltpu.CompilerParams(vmem_limit_bytes=12 * MIB),
        cost_estimate=cost(3),
        name="settle",
    )(order, half, *given)


def on_device(
    tokens,
    segments,
    pairing,
    pair_weight,
    triple_weight,
    query_bias,
    value_bias,
    mixer_weight,
    mixer_bias,
    norm_gain,
    norm_shift,
    expand_weight,
    expand_bias,
    shrink_weight,
    shrink_bias,
    final_gain,
    final_shift,
):
    rows, length, width = tokens.shape
    fan = expand_weight.shape[1]
    size = lax.axis_size(AXIS)
    me = lax.axis_index(AXIS)
    order, places = block_order(me)
    (
        qkv,
        spread,
        stats,
        attended,
        scaled_a,
        first_low,
        active,
        slope,
        scaled_b,
        output,
        pooled,
    ) = layer(
        tokens,
        segments,
        triple_weight,
        query_bias,
        value_bias,
        mixer_weight,
        mixer_bias,
        norm_gain,
        norm_shift,
        expand_weight,
        expand_bias,
        shrink_weight,
        shrink_bias,
        final_gain,
        final_shift,
    )
    active, slope, expand_weight, shrink_weight, triple_weight = [
        pltpu.with_memory_space_constraint(array, pltpu.HBM)
        for array in (active, slope, expand_weight, shrink_weight, triple_weight)
    ]
    own = pooled.reshape(rows * SEG_ROW, width)
    gathered, (first_t, tokens_t) = gather_rows(own, size, [(turn, first_low), (turn, tokens)])
    loss, dpooled = contrast(gathered, own, pairing, pair_weight, me, size)

    dsecond, dshrunk, sums_b = second_grad(segments, dpooled, scaled_b, stats, final_gain)
    one = Summing(shrink_grad(0, order, dshrunk, active), me, size)
    beside(dshrunk, lambda t: shrink_grad(1, order, t, active), [one], [one], one)

    dexpanded, fan_sums = [], []

    def expand_part(quarter, blocks, starts, ends):
        blocks, part, sums = beside(
            dshrunk,
            lambda t: expand_grad(quarter, order, t, shrink_weight, slope, first_t, blocks),
            starts,
            ends,
        )
        dexpanded.append(part)
        fan_sums.append(sums)
        return blocks

    send = expand_part(0, None, [one], [])
    send = expand_part(1, send, [], [one])
    two = Summing(send, me, size)
    keep = expand_part(2, None, [one], [one])
    two.keep = expand_part(3, keep, [one, two], [one])
    two.moving = lax.optimization_barrier((two.moving, fan_sums[3]))[0]
    two.finish()
    dfirst = beside(
        dsecond, lambda t: first_grad(order, t, expand_weight, dexpanded), [two, one], [one]
    )
    dbranch, dbranch_low, dattended, dots, sums_a = beside(
        dfirst,
        lambda t: branch_grad(t, scaled_a, stats, norm_gain, mixer_weight, attended),
        [one],
        [one, two],
    )
    dmixed, sums_c = [], []
    for row in range(rows):
        part, sums = beside(
            dattended,
            lambda t: attention_grad(row, segments, qkv, t, spread, dots),
            [one, two] if row < 2 else [],
            [two, one] if row < 2 else [],
        )
        dmixed.append(part)
        sums_c.append(sums[0:2])
    send, keep = beside(
        tokens_t,
        lambda t: triple_grad(order, t, attended, dmixed, dbranch_low),
        [one, two],
        [one, two],
    )
    three = Summing(send, me, size)
    three.keep = keep
    fan_sums = jnp.concatenate([part[0:1] for part in fan_sums], axis=0)
    pairs = order[0::2] // 2
    fan_sums = jnp.sum(
        jnp.where(pairs[None, :, None] == jnp.arange(4)[:, None, None], fan_sums[None], 0.0), axis=1
    )
    small = jnp.concatenate([sums_a[0:3], sums_b[0:3], sum(sums_c), fan_sums], axis=0)
    trades = [1 << k for k in range(size.bit_length() - 1)]

    def trade(*bits):
        def work(value):
            for bit in bits:
                if bit in trades:
                    trades.remove(bit)
                    value = value + lax.ppermute(value, AXIS, flip(size, bit, bit))
            return value

        return work

    def slot(starts, ends, work=lambda t: t):
        nonlocal small
        small = beside(small, work, starts, ends)

    def spread_beside(chain, parts, others):
        nonlocal small
        small, *grads = beside(
            small, lambda t: (t, *spread_blocks(places, chain.result, parts)), others, others
        )
        return grads

    slot([two, three], [three])
    tokens_out = beside(
        dbranch, lambda t: token_grad(t, dmixed, triple_weight), [three, one], [one, three, two]
    )
    slot([three, two], [three, two], trade(1))
    while not one.done:
        slot([three, one], [three, one])
    (dshrink,) = spread_beside(one, [((fan, width), 0, (0, 8), fan // 8, 0)], [three, two])
    slot([three, two], [three], trade(8))
    slot([three], [three, two])
    while not two.done:
        chains = [two] if len(three.steps) == 1 else [three, two]
        slot(chains, chains, trade(2))
    chains = [] if len(three.steps) == 1 else [three]
    (dexpand,) = spread_beside(two, [((width, fan), 1, (0, 8), width, 0)], chains)
    while len(three.steps) > 1:
        slot([three], [three], trade(16))
    small = trade(*trades[::-1])(small)
    small, *grads = beside(
        small, lambda t: (t, *settle(4, order, three.next)), [three], [three]
    )
    dtriple, dmixer = settle(0, order, three.result[0], grads)
    return (
        loss,
        output,
        tokens_out,
        dtriple,
        small[6],
        small[7],
        dmixer,
        small[2],
        small[0],
        small[1],
        dexpand,
        small[8:].reshape(-1),
        dshrink,
        small[5],
        small[3],
        small[4],
    )


def solution(mesh):
    wide = P(AXIS, None, None)
    return jax.shard_map(
        on_device,
        mesh=mesh,
        in_specs=(wide, P(AXIS, None)) + (P(),) * 15,
        out_specs=(P(), wide, wide) + (P(),) * 13,
        check_vma=False,
    )
```

```python
import functools

import jax
import jax.numpy as jnp
from jax import lax
from jax.experimental import pallas as pl
from jax.experimental.pallas import tpu as pltpu
from jax.sharding import PartitionSpec as P

HEADS = 12
HEAD_DIM = 64
SEG_ROW = 8
AXIS = "wide"
F32 = jnp.float32
BF16 = jnp.bfloat16

highest = lax.Precision.HIGHEST
scale = 20.0
MIB = 1024 * 1024


def prefixes(width):
    return (width // 12, width // 6, width // 3, 2 * width // 3, width)


def cost(micros):
    return pl.CostEstimate(flops=int(micros * 1.15e9), bytes_accessed=0, transcendentals=0)


def dot(a, b):
    return jnp.dot(a, b, preferred_element_type=F32)


def dot_nt(a, b):
    return lax.dot_general(a, b, (((1,), (1,)), ((), ())), preferred_element_type=F32)


def dot_tn(a, b):
    return lax.dot_general(a, b, (((0,), (0,)), ((), ())), preferred_element_type=F32)


def window(array, low, high):
    first, last = low // 128 * 128, -(-high // 128) * 128
    piece = array[:, first:last]
    if first == low and last == high:
        return piece, first, last
    lane = first + lax.broadcasted_iota(jnp.int32, (1, last - first), 1)
    return jnp.where((lane >= low) & (lane < high), piece, jnp.zeros_like(piece)), first, last


def split(value):
    high = value.astype(BF16)
    return high, (value - high.astype(F32)).astype(BF16)


def flip(size, low, high):
    return [(i, i ^ (high if i & 1 else low)) for i in range(size)]


def bit_of(me, bit):
    return (me // bit) % 2


def gather_rows(block, size, works):
    bit, results = size // 2, []
    while bit:
        pairs = flip(size, bit, bit)
        if len(results) < len(works):
            work, value = works[len(results)]
            block, value = lax.optimization_barrier((block, value))
            other, result = lax.optimization_barrier((lax.ppermute(block, AXIS, pairs), work(value)))
            results.append(result)
        else:
            other = lax.ppermute(block, AXIS, pairs)
        block = jnp.concatenate([block, other], axis=0)
        bit //= 2
    return block, results


def contrast_kernel(
    size, me_ref, gathered, own_ref, cols_ref, rows_ref, load_col_ref, load_row_ref, loss_ref, grad_ref, table, total, aim
):
    me = me_ref[0]
    count, width = table.shape
    share = own_ref.shape[0]
    block = 128
    levels = size.bit_length() - 1
    for place in range(size):
        mask = sum(((place >> k) & 1) << (levels - 1 - k) for k in range(levels))
        owner = me ^ mask
        table[pl.ds(pl.multiple_of(owner * share, share), share), :] = gathered[
            place * share : (place + 1) * share, :
        ]
    cuts = prefixes(width)
    spans = list(zip((0,) + cuts[:-1], cuts))
    lane_ids = lax.broadcasted_iota(jnp.int32, (1, count), 1)

    def place_pairs(i, carry):
        partner, load = carry
        rows = pl.ds(pl.multiple_of(i * block, block), block)
        hit = cols_ref[rows, 0:1] == lane_ids
        partner = partner + jnp.sum(
            jnp.where(hit, cols_ref[rows, 1:2].astype(F32), 0.0), axis=0, keepdims=True
        )
        load = load + jnp.sum(jnp.where(hit, load_col_ref[rows, :], 0.0), axis=0, keepdims=True)
        return partner, load

    zero_row = jnp.zeros((1, count), F32)
    partner_row, load_row = lax.fori_loop(0, count // block, place_pairs, (zero_row, zero_row))
    own_ids = me * share + lax.broadcasted_iota(jnp.int32, (share, 1), 0)
    hit = rows_ref[0:1, :] == own_ids
    partner_own = jnp.sum(jnp.where(hit, rows_ref[1:2, :].astype(F32), 0.0), axis=1, keepdims=True)
    load_own = jnp.sum(jnp.where(hit, load_row_ref[...], 0.0), axis=1, keepdims=True)

    squares = jnp.zeros((count, 1), F32)
    side = jnp.zeros((count, 128), F32)
    for k, (low, high) in enumerate(spans):
        piece, first, last = window(table, low, high)
        wide = piece.astype(F32)
        squares = squares + jnp.sum(wide * wide, axis=1, keepdims=True)
        lane = lax.broadcasted_iota(jnp.int32, (1, 128), 1)
        side = jnp.where(lane == k, squares, side)
    upright = lax.rsqrt(jnp.transpose(side)[0:8, :] + 1e-06) * scale
    inverse_rows = [upright[k : k + 1, :] for k in range(len(cuts))]

    total[...] = jnp.zeros_like(total)
    aim[...] = jnp.zeros_like(aim)

    def add_rows(i, carry):
        start = pl.multiple_of(i * block, block)
        sims = jnp.zeros((block, count), F32)
        squares = jnp.zeros((block, 1), F32)
        row_ids = (start + lax.broadcasted_iota(jnp.int32, (block, 1), 0)).astype(F32)
        chosen = partner_row == row_ids
        for k, (low, high) in enumerate(spans):
            piece, first, last = window(table.at[pl.ds(start, block), :], low, high)
            wide = piece.astype(F32)
            squares = squares + jnp.sum(wide * wide, axis=1, keepdims=True)
            sims = sims + dot_nt(piece, table[:, first:last])
            value = sims * lax.rsqrt(squares + 1e-06) * inverse_rows[k]
            total[k : k + 1, :] += jnp.sum(jnp.exp(value - scale), axis=0, keepdims=True)
            aim[k : k + 1, :] += jnp.sum(jnp.where(chosen, value, 0.0), axis=0, keepdims=True)
        return carry

    lax.fori_loop(0, count // block, add_rows, 0)

    spreads = scale + jnp.log(total[0 : len(cuts), :])
    gaps = jnp.sum(spreads - aim[0 : len(cuts), :], axis=0, keepdims=True)
    loss_ref[...] = jnp.broadcast_to(
        jnp.sum(gaps * load_row, axis=1, keepdims=True) / count, loss_ref.shape
    )

    sims = jnp.zeros((share, count), F32)
    squares = jnp.zeros((share, 1), F32)
    out_hit = (partner_own == lane_ids.astype(F32)).astype(F32)
    in_hit = (partner_row == own_ids.astype(F32)).astype(F32)
    grad_ref[...] = jnp.zeros_like(grad_ref)
    for k, (low, high) in enumerate(spans):
        piece, first, last = window(own_ref, low, high)
        wide = piece.astype(F32)
        squares = squares + jnp.sum(wide * wide, axis=1, keepdims=True)
        inverse = lax.rsqrt(squares + 1e-06)
        sims = sims + dot_nt(piece, table[:, first:last])
        value = sims * inverse * inverse_rows[k]
        spread = scale + jnp.log(jnp.sum(jnp.exp(value - scale), axis=1, keepdims=True))
        dsims = load_own * (jnp.exp(value - spread) - out_hit) + load_row * (
            jnp.exp(value - spreads[k : k + 1, :]) - in_hit
        )
        big, small = split(dsims * inverse_rows[k])
        unit, _, last = window(own_ref, 0, high)
        unit = unit.astype(F32) * inverse
        dunit = dot(big, table[:, :last]) + dot(small, table[:, :last])
        if last != high:
            lane = lax.broadcasted_iota(jnp.int32, (1, last), 1)
            dunit = jnp.where(lane < high, dunit, 0.0)
        along = jnp.sum(dunit * unit, axis=1, keepdims=True)
        grad_ref[:, :last] += inverse * (dunit - unit * along)


def contrast(gathered, own, pairing, pair_weight, me, size):
    share, width = own.shape
    count = share * size
    vmem = pl.BlockSpec(memory_space=pltpu.VMEM)
    loss, grad = pl.pallas_call(
        functools.partial(contrast_kernel, size),
        out_shape=(
            jax.ShapeDtypeStruct((8, 128), F32),
            jax.ShapeDtypeStruct((share, width), F32),
        ),
        in_specs=[pl.BlockSpec(memory_space=pltpu.SMEM)] + [vmem] * 6,
        out_specs=(vmem, vmem),
        scratch_shapes=[
            pltpu.VMEM((count, width), BF16),
            pltpu.VMEM((8, count), F32),
            pltpu.VMEM((8, count), F32),
        ],
        compiler_params=pltpu.CompilerParams(vmem_limit_bytes=16 * MIB),
        cost_estimate=cost(6),
        name="contrast",
    )(
        me.reshape(1),
        gathered,
        own,
        pairing,
        pairing.T,
        pair_weight[:, None],
        pair_weight[None, :],
    )
    return loss[0, 0], grad


def attention_windows(length):
    block = 128
    return [
        (i, max(0, i - block), min(length, i + 2 * block)) for i in range(0, length, block)
    ]


def segment_column(seg_row):
    wide = jnp.broadcast_to(seg_row.astype(F32), (128, seg_row.shape[1]))
    return jnp.transpose(wide)[:, 0:1].astype(jnp.int32)


def both_heads(pair):
    left = lax.broadcasted_iota(jnp.int32, (1, 128), 1) < HEAD_DIM
    zero = jnp.zeros((), pair.dtype)
    return jnp.concatenate([jnp.where(left, pair, zero), jnp.where(left, zero, pair)], axis=0)


def layer_kernel(
    tokens,
    segments,
    triple_hbm,
    query_bias,
    value_bias,
    mixer_hbm,
    mixer_bias,
    norm_gain,
    norm_shift,
    expand_hbm,
    expand_bias,
    shrink_hbm,
    shrink_bias,
    final_gain,
    final_shift,
    qkv,
    spread,
    stats,
    attended,
    scaled_a,
    first_low,
    active,
    slope,
    scaled_b,
    output,
    pooled,
    triple,
    mixer,
    expand,
    shrink,
    bias,
    joined,
    first,
    total,
    sems,
):
    step = pl.program_id(0)
    length, width = tokens.shape[1:]
    fan = expand.shape[1]
    held = (triple, mixer, expand, shrink)
    copies = [
        pltpu.make_async_copy(src, dst, sems.at[k])
        for k, (src, dst) in enumerate(zip((triple_hbm, mixer_hbm, expand_hbm, shrink_hbm), held))
    ]

    @pl.when(step == 0)
    def _():
        for copy in copies:
            copy.start()
        copies[0].wait()

    seg_row = segments[pl.ds(step, 1), :]
    seg_col = segment_column(seg_row)
    windows = attention_windows(length)
    for k, (at, low, high) in enumerate(windows):
        same = seg_col[low:high, :] == seg_row[:, at : at + 128]
        bias[k, : high - low, :] = jnp.where(same, 0.0, -1e30)

    chunk = width
    x = tokens[0]
    mixed = dot(x, triple[:, 0:chunk]) + query_bias[...][None, :]
    qkv[0, :, 0:chunk] = (mixed.astype(BF16).astype(F32) * 0.125).astype(BF16)
    qkv[0, :, chunk : 2 * chunk] = dot(x, triple[:, chunk : 2 * chunk]).astype(BF16)
    qkv[0, :, 2 * chunk :] = (dot(x, triple[:, 2 * chunk :]) + value_bias[...][None, :]).astype(BF16)

    left = lax.broadcasted_iota(jnp.int32, (1, 128), 1) < HEAD_DIM
    spread[...] = jnp.zeros_like(spread)
    for k, (at, low, high) in enumerate(windows):
        wall = bias[k, : high - low, :]
        wall = jnp.concatenate([wall, wall], axis=1)
        for p in range(width // 128):
            cols = slice(p * 128, p * 128 + 128)
            query = both_heads(qkv[0, at : at + 128, cols])
            keys = qkv[0, low:high, width + p * 128 : width + p * 128 + 128]
            scores = dot_nt(keys, query) + wall
            top = jnp.max(scores, axis=0, keepdims=True)
            expo = jnp.exp(scores - top)
            amount = jnp.sum(expo, axis=0, keepdims=True)
            values = qkv[0, low:high, 2 * width + p * 128 : 2 * width + p * 128 + 128]
            share = jnp.transpose(jnp.broadcast_to(1.0 / amount, (128, amount.shape[1])))
            found = dot_tn(expo.astype(BF16), values) * share
            joined[at : at + 128, cols] = jnp.where(left, found[:128], found[128:]).astype(BF16)
            marks = top + jnp.log(amount)
            spread[0, 2 * p : 2 * p + 1, at : at + 128] = marks[:, :128]
            spread[0, 2 * p + 1 : 2 * p + 2, at : at + 128] = marks[:, 128:]

    attended[0] = jnp.transpose(joined[...])

    @pl.when(step == 0)
    def _():
        copies[1].wait()

    summed = tokens[0].astype(F32) + (dot(joined[...], mixer[...]) + mixer_bias[...][None, :])
    centre = summed - jnp.mean(summed, axis=1, keepdims=True)
    inverse = lax.rsqrt(jnp.mean(centre * centre, axis=1, keepdims=True) + 1e-05)
    scaled = centre * inverse
    scaled_a[0] = scaled.astype(BF16)
    inverse_a = inverse
    value = scaled * norm_gain[...][None, :] + norm_shift[...][None, :]
    first[...] = value
    first_low[0] = value.astype(BF16)

    @pl.when(step == 0)
    def _():
        copies[2].wait()
        copies[3].wait()

    part = 1024
    for j in range(fan // part):
        cols = slice(j * part, (j + 1) * part)
        value = dot(first_low[0], expand[:, cols]) + expand_bias[cols][None, :]
        gauss = jnp.exp(value * value * -0.5)
        near = 1.0 / (1.0 + 0.3275911 * 0.7071067811865476 * jnp.abs(value))
        poly = near * (
            0.5 * 0.254829592
            + near
            * (
                0.5 * -0.284496736
                + near * (0.5 * 1.421413741 + near * (0.5 * -1.453152027 + near * (0.5 * 1.061405429)))
            )
        )
        tail = poly * gauss
        below = jnp.where(value < 0, tail, 1.0 - tail)
        rounded = (value * below).astype(BF16)
        active[0, :, cols] = rounded
        slope[0, :, cols] = (below + value * (gauss * 0.3989422804014327)).astype(BF16)
        product = dot(rounded, shrink[cols, :])
        if j == 0:
            total[...] = product
        else:
            total[...] += product

    summed = first[...] + (total[...] + shrink_bias[...][None, :])
    centre = summed - jnp.mean(summed, axis=1, keepdims=True)
    inverse = lax.rsqrt(jnp.mean(centre * centre, axis=1, keepdims=True) + 1e-05)
    scaled = centre * inverse
    scaled_b[0] = scaled.astype(BF16)
    lane = lax.broadcasted_iota(jnp.int32, (1, 128), 1)
    stats[0] = jnp.where(lane == 0, inverse_a, inverse)
    final = scaled * final_gain[...][None, :] + final_shift[...][None, :]
    output[0] = final.astype(BF16)
    member = (
        lax.broadcasted_iota(jnp.int32, (SEG_ROW, length), 0) == seg_row
    ).astype(F32)
    counts = jnp.sum(member, axis=1, keepdims=True)
    gathered = jnp.dot(member, final, preferred_element_type=F32, precision=highest)
    pooled[0] = (gathered / counts).astype(BF16)


def layer(tokens, segments, triple_weight, query_bias, value_bias, mixer_weight, mixer_bias, norm_gain, norm_shift, expand_weight, expand_bias, shrink_weight, shrink_bias, final_gain, final_shift):
    rows, length, width = tokens.shape
    fan = expand_weight.shape[1]

    def by_row(*shape):
        return pl.BlockSpec((1,) + shape, lambda r: (r,) + (0,) * len(shape))

    def whole(size):
        return pl.BlockSpec((size,), lambda r: (0,))

    hbm = pl.BlockSpec(memory_space=pl.ANY)
    outs = (
        ((length, 3 * width), BF16),
        ((16, length), F32),
        ((length, 128), F32),
        ((width, length), BF16),
        ((length, width), BF16),
        ((length, width), BF16),
        ((length, fan), BF16),
        ((length, fan), BF16),
        ((length, width), BF16),
        ((length, width), BF16),
        ((SEG_ROW, width), BF16),
    )
    weights = (triple_weight, mixer_weight, expand_weight, shrink_weight)
    return pl.pallas_call(
        layer_kernel,
        grid=(rows,),
        out_shape=tuple(jax.ShapeDtypeStruct((rows,) + shape, kind) for shape, kind in outs),
        in_specs=[
            by_row(length, width),
            pl.BlockSpec((rows, length), lambda r: (0, 0)),
            hbm,
            whole(width),
            whole(width),
            hbm,
            whole(width),
            whole(width),
            whole(width),
            hbm,
            whole(fan),
            hbm,
            whole(width),
            whole(width),
            whole(width),
        ],
        out_specs=tuple(by_row(*shape) for shape, _ in outs),
        scratch_shapes=[pltpu.VMEM(w.shape, BF16) for w in weights]
        + [
            pltpu.VMEM((length // 128, 384, 128), F32),
            pltpu.VMEM((length, width), BF16),
            pltpu.VMEM((length, width), F32),
            pltpu.VMEM((length, width), F32),
            pltpu.SemaphoreType.DMA((4,)),
        ],
        compiler_params=pltpu.CompilerParams(vmem_limit_bytes=56 * MIB),
        cost_estimate=cost(50),
        name="layer",
    )(
        tokens,
        segments,
        triple_weight,
        query_bias,
        value_bias,
        mixer_weight,
        mixer_bias,
        norm_gain,
        norm_shift,
        expand_weight,
        expand_bias,
        shrink_weight,
        shrink_bias,
        final_gain,
        final_shift,
    )


def fixed(shape):
    return pl.BlockSpec(shape, lambda *_: (0,) * len(shape), pipeline_mode=pl.Buffered(1))


def second_grad_kernel(segments, dpooled, scaled, stats, gain, dsecond, dshrunk, sums):
    r = pl.program_id(0)
    length = scaled.shape[1]
    scale_row = gain[...][None, :]
    member = (
        lax.broadcasted_iota(jnp.int32, (SEG_ROW, length), 0) == segments[pl.ds(r, 1), :]
    ).astype(F32)
    counts = jnp.sum(member, axis=1, keepdims=True)
    inner = dpooled[...] / counts * scale_row
    table = jnp.concatenate(split(inner), axis=0)
    member = jnp.concatenate([member, member], axis=0).astype(BF16)
    inner = dot_tn(member, table)
    norm = scaled[0].astype(F32)
    product = inner * norm
    value = stats[0][:, 127:128] * (
        inner
        - jnp.mean(inner, axis=1, keepdims=True)
        - norm * jnp.mean(product, axis=1, keepdims=True)
    )
    low = value.astype(BF16)
    dsecond[0] = value
    dshrunk[0] = low

    @pl.when(r == 0)
    def _():
        sums[...] = jnp.zeros_like(sums)

    sums[0:1, :] += jnp.sum(product, axis=0, keepdims=True) / scale_row
    sums[1:2, :] += jnp.sum(dpooled[...], axis=0, keepdims=True)
    sums[2:3, :] += jnp.sum(low.astype(F32), axis=0, keepdims=True)


def second_grad(segments, dpooled, scaled, stats, gain):
    rows, length, width = scaled.shape

    def by_row(*shape):
        return pl.BlockSpec((1,) + shape, lambda r: (r,) + (0,) * len(shape))

    return pl.pallas_call(
        second_grad_kernel,
        grid=(rows,),
        in_specs=[
            fixed(segments.shape),
            pl.BlockSpec((SEG_ROW, width), lambda r: (r, 0)),
            by_row(length, width),
            by_row(length, 128),
            fixed(gain.shape),
        ],
        out_specs=(by_row(length, width), by_row(length, width), fixed((8, width))),
        out_shape=(
            jax.ShapeDtypeStruct((rows, length, width), F32),
            jax.ShapeDtypeStruct((rows, length, width), BF16),
            jax.ShapeDtypeStruct((8, width), F32),
        ),
        compiler_params=pltpu.CompilerParams(vmem_limit_bytes=16 * MIB),
        cost_estimate=cost(3),
        name="second_grad",
    )(segments, dpooled, scaled, stats, gain)


def put_pair(out, order, g, value, along=1):
    turned = order[2 * g] % 2
    cut = value.shape[along] // 2
    value = value.astype(BF16)
    out[turned] = value[:cut] if along == 0 else value[:, :cut]
    out[1 - turned] = value[cut:] if along == 0 else value[:, cut:]


def put_half(g, send, keep, put):
    @pl.when(g < 2)
    def _():
        put(send)

    @pl.when(g >= 2)
    def _():
        put(keep)


def half_specs(height, width):
    return (
        pl.BlockSpec((2, height, width), lambda g, order: (jnp.minimum(g, 1), 0, 0)),
        pl.BlockSpec((2, height, width), lambda g, order: (jnp.maximum(g - 2, 0), 0, 0)),
    )


def shrink_grad_kernel(half, order, dshrunk, active, out):
    rows, length, width = dshrunk.shape
    value = dot_tn(
        active[...].reshape(rows * length, active.shape[2]), dshrunk[...].reshape(rows * length, width)
    )
    put_pair(out, order, 2 * half + pl.program_id(0), value, 0)


def shrink_grad(half, order, dshrunk, active):
    rows, length, width = dshrunk.shape
    part = active.shape[2] // 4
    return pl.pallas_call(
        functools.partial(shrink_grad_kernel, half),
        grid_spec=pltpu.PrefetchScalarGridSpec(
            num_scalar_prefetch=1,
            grid=(2,),
            in_specs=[
                fixed(dshrunk.shape),
                pl.BlockSpec(
                    (rows, length, part), lambda g, order: (0, 0, order[4 * half + 2 * g] // 2)
                ),
            ],
            out_specs=pl.BlockSpec((2, part // 2, width), lambda g, order: (g, 0, 0)),
        ),
        out_shape=jax.ShapeDtypeStruct((4, part // 2, width), BF16),
        compiler_params=pltpu.CompilerParams(vmem_limit_bytes=20 * MIB),
        cost_estimate=cost(4),
        name="shrink_grad",
    )(order, dshrunk, active)


def expand_grad_kernel(first, order, dshrunk, shrink, slope, turned, *refs):
    out, dexpanded, sums = refs[-3:]
    rows, length, width = dshrunk.shape
    part = slope.shape[2]
    dactive = dot_nt(dshrunk[...].reshape(rows * length, width), shrink[...])
    low = (dactive * slope[...].reshape(rows * length, part).astype(F32)).astype(BF16)
    g = pl.program_id(0)
    sums[pl.ds(g, 1), :] = jnp.sum(low.astype(F32), axis=0, keepdims=True)
    put_pair(out, order, first + g, dot(turned[...], low))
    dexpanded[...] = low.reshape(rows, length, part)


def expand_grad(first, count, order, dshrunk, shrink_weight, slope, turned, blocks=None):
    rows, length, width = dshrunk.shape
    part = slope.shape[2] // 4
    pair = lambda g, order: order[2 * (first + g)] // 2
    given = [] if blocks is None else [blocks]
    return pl.pallas_call(
        functools.partial(expand_grad_kernel, first),
        grid_spec=pltpu.PrefetchScalarGridSpec(
            num_scalar_prefetch=1,
            grid=(count,),
            in_specs=[
                fixed(dshrunk.shape),
                pl.BlockSpec((part, width), lambda g, order: (pair(g, order), 0)),
                pl.BlockSpec((rows, length, part), lambda g, order: (0, 0, pair(g, order))),
                fixed(turned.shape),
            ]
            + [pl.BlockSpec(memory_space=pl.ANY) for _ in given],
            out_specs=(
                pl.BlockSpec((2, width, part // 2), lambda g, order: (first % 2 + g, 0, 0)),
                pl.BlockSpec((rows, length, part), lambda g, order: (0, 0, g)),
                fixed((8, part)),
            ),
        ),
        out_shape=(
            jax.ShapeDtypeStruct((4, width, part // 2), BF16),
            jax.ShapeDtypeStruct((rows, length, count * part), BF16),
            jax.ShapeDtypeStruct((8, part), F32),
        ),
        input_output_aliases={5: 0} if given else {},
        compiler_params=pltpu.CompilerParams(vmem_limit_bytes=24 * MIB),
        cost_estimate=cost(4),
        name="expand_grad",
    )(order, dshrunk, shrink_weight, slope, turned, *given)


def first_grad_kernel(order, dsecond, expand, *refs):
    *parts, out = refs
    width = dsecond.shape[2]
    value = dsecond[0]
    q = 0
    for part in parts:
        for k in range(part.shape[2] // width):
            columns = pl.ds(pl.multiple_of(order[2 * q] // 2 * width, 128), width)
            value = value + dot_nt(part[0, :, k * width : (k + 1) * width], expand[:, columns])
            q += 1
    out[0] = value


def first_grad(order, dsecond, expand_weight, parts):
    rows, length, width = dsecond.shape
    block = pl.BlockSpec((1, length, width), lambda r, order: (r, 0, 0))
    return pl.pallas_call(
        first_grad_kernel,
        grid_spec=pltpu.PrefetchScalarGridSpec(
            num_scalar_prefetch=1,
            grid=(rows,),
            in_specs=[block, fixed(expand_weight.shape)]
            + [pl.BlockSpec((1,) + part.shape[1:], lambda r, order: (r, 0, 0)) for part in parts],
            out_specs=block,
        ),
        out_shape=jax.ShapeDtypeStruct(dsecond.shape, F32),
        compiler_params=pltpu.CompilerParams(vmem_limit_bytes=28 * MIB),
        cost_estimate=cost(5.5),
        name="first_grad",
    )(order, dsecond, expand_weight, *parts)


def turn_kernel(value, out):
    out[...] = jnp.transpose(value[0])


def turn(value):
    rows, length, width = value.shape
    return pl.pallas_call(
        turn_kernel,
        grid=(rows,),
        in_specs=[pl.BlockSpec((1, length, width), lambda r: (r, 0, 0))],
        out_specs=pl.BlockSpec((width, length), lambda r: (0, r)),
        out_shape=jax.ShapeDtypeStruct((width, rows * length), value.dtype),
        compiler_params=pltpu.CompilerParams(vmem_limit_bytes=10 * MIB),
        cost_estimate=cost(1.5),
        name="turn",
    )(value)


def branch_grad_kernel(
    given, scaled, stats, gain, mixer, attended, dbranch, dbranch_low, dattended, dots, sums
):
    r = pl.program_id(0)
    width = given.shape[2]
    dfirst = given[0]
    inner = dfirst * gain[...][None, :]
    norm = scaled[0].astype(F32)
    value = stats[0][:, 0:1] * (
        inner
        - jnp.mean(inner, axis=1, keepdims=True)
        - norm * jnp.mean(inner * norm, axis=1, keepdims=True)
    )
    low = value.astype(BF16)
    dbranch[0] = value
    dbranch_low[0] = low

    @pl.when(r == 0)
    def _():
        sums[...] = jnp.zeros_like(sums)

    sums[0:1, :] += jnp.sum(dfirst * norm, axis=0, keepdims=True)
    sums[1:2, :] += jnp.sum(dfirst, axis=0, keepdims=True)
    sums[2:3, :] += jnp.sum(low.astype(F32), axis=0, keepdims=True)
    dattended[0] = dot_nt(low, mixer[...]).astype(BF16)
    turned = dot_nt(mixer[...], low).astype(BF16)
    product = turned.astype(F32) * attended[0].astype(F32)
    dots[...] = jnp.zeros_like(dots)
    for h in range(width // HEAD_DIM):
        dots[0, h : h + 1, :] = jnp.sum(
            product[h * HEAD_DIM : (h + 1) * HEAD_DIM, :], axis=0, keepdims=True
        )


def branch_grad(dfirst, scaled, stats, gain, mixer_weight, attended):
    rows, length, width = dfirst.shape

    def by_row(*shape):
        return pl.BlockSpec((1,) + shape, lambda r: (r,) + (0,) * len(shape))

    wide, low = by_row(length, width), by_row(length, width)
    return pl.pallas_call(
        branch_grad_kernel,
        grid=(rows,),
        in_specs=[
            wide,
            low,
            by_row(length, 128),
            fixed(gain.shape),
            fixed(mixer_weight.shape),
            by_row(width, length),
        ],
        out_specs=(wide, low, low, by_row(16, length), fixed((8, width))),
        out_shape=(
            jax.ShapeDtypeStruct((rows, length, width), F32),
            jax.ShapeDtypeStruct((rows, length, width), BF16),
            jax.ShapeDtypeStruct((rows, length, width), BF16),
            jax.ShapeDtypeStruct((rows, 16, length), F32),
            jax.ShapeDtypeStruct((8, width), F32),
        ),
        compiler_params=pltpu.CompilerParams(vmem_limit_bytes=28 * MIB),
        cost_estimate=cost(5.5),
        name="branch_grad",
    )(dfirst, scaled, stats, gain, mixer_weight, attended)


def attention_grad_kernel(row, segments, qkv, dattended, spread, dots, dmixed, sums, bias, dkeys, dvalues):
    r = row
    length, width = dattended.shape[1:]
    seg_row = segments[r : r + 1, :]
    seg_col = segment_column(seg_row)
    windows = attention_windows(length)
    for k, (at, low, high) in enumerate(windows):
        same = seg_col[low:high, :] == seg_row[:, at : at + 128]
        bias[k, : high - low, :] = jnp.where(same, 0.0, -1e30)
    dkeys[...] = jnp.zeros_like(dkeys)
    dvalues[...] = jnp.zeros_like(dvalues)
    left = lax.broadcasted_iota(jnp.int32, (1, 128), 1) < HEAD_DIM
    for k, (at, low, high) in enumerate(windows):
        wall = bias[k, : high - low, :]
        wall = jnp.concatenate([wall, wall], axis=1)
        for p in range(width // 128):
            cols = slice(p * 128, p * 128 + 128)
            query = both_heads(qkv[0, at : at + 128, cols])
            keys = qkv[0, low:high, width + p * 128 : width + p * 128 + 128]
            values = qkv[0, low:high, 2 * width + p * 128 : 2 * width + p * 128 + 128]
            grad = both_heads(dattended[0, at : at + 128, cols])
            lse, delta = [
                jnp.concatenate(
                    [ref[0, 2 * p : 2 * p + 1, at : at + 128], ref[0, 2 * p + 1 : 2 * p + 2, at : at + 128]],
                    axis=1,
                )
                for ref in (spread, dots)
            ]
            probs = jnp.exp(dot_nt(keys, query) + wall - lse)
            dscores = (probs * (dot_nt(values, grad) - delta)).astype(BF16)
            dvalues[low:high, cols] += dot(probs.astype(BF16), grad)
            dkeys[low:high, cols] += dot(dscores, query)
            dquery = dot_tn(dscores, keys)
            dmixed[0, at : at + 128, cols] = (
                jnp.where(left, dquery[:128], dquery[128:]) * 0.125
            ).astype(BF16)
    dmixed[0, :, width : 2 * width] = dkeys[...].astype(BF16)
    dmixed[0, :, 2 * width :] = dvalues[...].astype(BF16)

    sums[...] = jnp.zeros_like(sums)
    sums[0:1, :] = jnp.sum(dmixed[0, :, :width].astype(F32), axis=0, keepdims=True)
    sums[1:2, :] = jnp.sum(dmixed[0, :, 2 * width :].astype(F32), axis=0, keepdims=True)


def attention_grad(row, segments, qkv, dattended, spread, dots):
    rows, length, width = dattended.shape

    def by_row(*shape):
        return pl.BlockSpec((1,) + shape, lambda _: (row,) + (0,) * len(shape))

    return pl.pallas_call(
        functools.partial(attention_grad_kernel, row),
        grid=(1,),
        in_specs=[
            fixed(segments.shape),
            by_row(length, 3 * width),
            by_row(length, width),
            by_row(16, length),
            by_row(16, length),
        ],
        out_specs=(fixed((1, length, 3 * width)), fixed((8, width))),
        out_shape=(
            jax.ShapeDtypeStruct((1, length, 3 * width), BF16),
            jax.ShapeDtypeStruct((8, width), F32),
        ),
        scratch_shapes=[
            pltpu.VMEM((length // 128, 384, 128), F32),
            pltpu.VMEM((length, width), F32),
            pltpu.VMEM((length, width), F32),
        ],
        compiler_params=pltpu.CompilerParams(vmem_limit_bytes=20 * MIB),
        cost_estimate=cost(8),
        name="attention_grad",
    )(segments, qkv, dattended, spread, dots)


def triple_grad_kernel(order, turned, attended, dbranch, *refs):
    *dmixed, send, keep = refs
    g = pl.program_id(0)
    rows, length = dbranch.shape[:2]
    pair = order[2 * g] // 2

    @pl.when(pair < 3)
    def _():
        value = dot(turned[:, :length], dmixed[0][0])
        for r in range(1, rows):
            value = value + dot(turned[:, r * length : (r + 1) * length], dmixed[r][0])
        put_half(g, send, keep, lambda out: put_pair(out, order, g, value))

    @pl.when(pair >= 3)
    def _():
        value = dot(attended[0], dbranch[0])
        for r in range(1, rows):
            value = value + dot(attended[r], dbranch[r])
        put_half(g, send, keep, lambda out: put_pair(out, order, g, value))


def triple_grad(order, turned, attended, dmixed, dbranch):
    rows, length, width = dbranch.shape
    shape = jax.ShapeDtypeStruct((4, width, width // 2), BF16)
    return pl.pallas_call(
        triple_grad_kernel,
        grid_spec=pltpu.PrefetchScalarGridSpec(
            num_scalar_prefetch=1,
            grid=(4,),
            in_specs=[fixed(turned.shape), fixed(attended.shape), fixed(dbranch.shape)]
            + [
                pl.BlockSpec(
                    (1, length, width), lambda g, order: (0, 0, jnp.minimum(order[2 * g] // 2, 2))
                )
                for _ in dmixed
            ],
            out_specs=half_specs(width, width // 2),
        ),
        out_shape=(shape, shape),
        compiler_params=pltpu.CompilerParams(vmem_limit_bytes=22 * MIB),
        cost_estimate=cost(7),
        name="triple_grad",
    )(order, turned, attended, dbranch, *dmixed)


def token_grad_kernel(dbranch, triple, *refs):
    *dmixed, out = refs
    r = pl.program_id(0)
    for k, ref in enumerate(dmixed):

        @pl.when(r == k)
        def _():
            out[0] = dbranch[0] + dot_nt(ref[0], triple[...])


def token_grad(dbranch, dmixed, triple_weight):
    rows, length, width = dbranch.shape
    return pl.pallas_call(
        token_grad_kernel,
        grid=(rows,),
        in_specs=[pl.BlockSpec((1, length, width), lambda r: (r, 0, 0)), fixed(triple_weight.shape)]
        + [fixed(part.shape) for part in dmixed],
        out_specs=pl.BlockSpec((1, length, width), lambda r: (r, 0, 0)),
        out_shape=jax.ShapeDtypeStruct(dbranch.shape, F32),
        compiler_params=pltpu.CompilerParams(vmem_limit_bytes=24 * MIB),
        cost_estimate=cost(5.5),
        name="token_grad",
    )(dbranch, triple_weight, *dmixed)


def block_order(me):
    core = bit_of(me, 1)
    one, two = bit_of(me, 2), bit_of(me, 4)
    near, far = jnp.where(core == 0, one, two), jnp.where(core == 0, two, one)
    order = []
    for owner, high, low in ((1 - core, far, near), (core, near, far)):
        for a in (1, 0):
            for b in (1, 0):
                order.append(owner * 4 + (high ^ a) * 2 + (low ^ b))
    order = jnp.stack(order).astype(jnp.int32)
    places = jnp.sum(
        jnp.where(order[None, :] == jnp.arange(8)[:, None], jnp.arange(8)[None, :], 0), axis=1
    ).astype(jnp.int32)
    return order, places


def beside(value, work, starts=(), ends=(), rest=None):
    value, nexts = lax.optimization_barrier((value, [chain.next for chain in starts]))
    for chain, array in zip(starts, nexts):
        chain.next = array
        chain.start()
    result = work(value)
    result, moving = lax.optimization_barrier((result, [chain.moving for chain in ends]))
    if rest is not None:
        rest.keep = result
    for chain, array in zip(ends, moving):
        chain.moving = array
        chain.finish()
    return result


class Summing:
    def __init__(self, send, me, size, whole=True):
        self.me, self.size = me, size
        self.next, self.moving = send, None
        rest = [1 << k for k in range(3, size.bit_length() - 1)]
        steps = [(k, flip(size, *bits)) for k, bits in enumerate(((1, 1), (2, 4), (4, 2)))]
        self.steps = steps + [("halve", bit) for bit in rest]
        if whole:
            self.steps += [("double", bit) for bit in rest[::-1]]
            self.steps += [("join", pairs) for _, pairs in steps[::-1]]

    @property
    def done(self):
        return not self.steps

    def start(self):
        kind, detail = self.steps[0]
        pairs = flip(self.size, detail, detail) if kind in ("halve", "double") else detail
        self.moving = lax.ppermute(self.next, AXIS, pairs)

    def finish(self):
        kind, detail = self.steps.pop(0)
        got = self.moving
        f32 = lambda t: t.astype(F32)
        if kind == 0:
            self.first = got
            self.next = (f32(self.keep[0:2]) + f32(got[0:2])).astype(BF16)
        elif kind == 1:
            self.second = got
            self.next = (f32(self.keep[2:3]) + f32(self.first[2:3]) + f32(got[0:1])).astype(BF16)
        elif kind == 2:
            own = f32(self.keep[3]) + f32(self.first[3]) + f32(self.second[1]) + f32(got[0])
            self.cut(own)
        elif kind == "halve":
            self.cut(self.own + f32(got))
        elif kind == "double":
            mine = bit_of(self.me, detail)
            self.next = jnp.where(
                mine == 0,
                jnp.concatenate([self.next, got], axis=0),
                jnp.concatenate([got, self.next], axis=0),
            )
            self.lift()
        elif len(self.steps):
            self.next = jnp.concatenate([got, self.next], axis=0)
        else:
            self.result = (got, self.next)

    def cut(self, own):
        kind, detail = self.steps[0] if self.steps else (None, None)
        if kind == "halve":
            mine = bit_of(self.me, detail)
            half = own.shape[0] // 2
            self.own = lax.dynamic_slice_in_dim(own, mine * half, half, 0)
            own = lax.dynamic_slice_in_dim(own, (1 - mine) * half, half, 0)
        self.next = own.astype(BF16)
        self.lift()

    def lift(self):
        if self.steps and self.steps[0][0] == "join":
            self.next = self.next[None]


def spread_kernel(ranges, places, *refs):
    outs = refs[2 * len(ranges) :]
    b = pl.program_id(0)
    half = pl.num_programs(0) // 2

    def store(out, value):
        value = value.astype(F32)
        height, width = out.shape
        if value.shape[1] == width:
            out[...] = value
        else:
            out[:, : width // 2] = value[:height]
            out[:, width // 2 :] = value[height:]

    for k, (low, high) in enumerate(ranges):
        here = (b >= low) & (b < high)

        @pl.when(here & (places[b] < half))
        def _():
            store(outs[k], refs[2 * k][0])

        @pl.when(here & (places[b] >= half))
        def _():
            store(outs[k], refs[2 * k + 1][0])


def spread_blocks(places, halves, parts):
    got, own = halves
    half, _, width = got.shape
    in_specs, out_specs, shapes = [], [], []

    def spec(shape, index):
        return pl.BlockSpec(shape, index)

    for shape, along, (low, high), height, skip in parts:
        at = lambda b, low=low, high=high: jnp.clip(b, low, high - 1)
        block = (1, height, width)
        in_specs.append(
            spec(block, lambda b, p, at=at, skip=skip: (jnp.minimum(p[at(b)], half - 1), skip, 0))
        )
        in_specs.append(
            spec(block, lambda b, p, at=at, skip=skip: (jnp.maximum(p[at(b)] - half, 0), skip, 0))
        )
        count = high - low
        if along == 0:
            out = (shape[0] // count, shape[1])
            out_specs.append(spec(out, lambda b, p, at=at, low=low: (at(b) - low, 0)))
        else:
            out = (shape[0], shape[1] // count)
            out_specs.append(spec(out, lambda b, p, at=at, low=low: (0, at(b) - low)))
        shapes.append(jax.ShapeDtypeStruct(shape, F32))
    return pl.pallas_call(
        functools.partial(spread_kernel, [part[2] for part in parts]),
        grid_spec=pltpu.PrefetchScalarGridSpec(
            num_scalar_prefetch=1, grid=(2 * half,), in_specs=in_specs, out_specs=tuple(out_specs)
        ),
        out_shape=tuple(shapes),
        compiler_params=pltpu.CompilerParams(vmem_limit_bytes=20 * MIB),
        cost_estimate=cost(5),
        name="spread_blocks",
    )(places, *(half for _ in parts for half in (got, own)))


def settle_kernel(first, order, half, *refs):
    triple, mixer, wide, sems = refs[-4:]
    width = wide.shape[2]
    split_at = triple.shape[1] // width
    copies = []
    for k in range(4):
        slot, label = k % 2, order[first + k]
        if k >= 2:
            copies[k - 2].wait()
        wide[slot] = half[k].astype(F32)

        @pl.when(label < split_at)
        def _():
            at = pl.multiple_of(label * width, 128)
            pltpu.make_async_copy(wide.at[slot], triple.at[:, pl.ds(at, width)], sems.at[slot]).start()

        @pl.when(label >= split_at)
        def _():
            at = pl.multiple_of((label - split_at) * width, 128)
            pltpu.make_async_copy(wide.at[slot], mixer.at[:, pl.ds(at, width)], sems.at[slot]).start()

        copies.append(pltpu.make_async_copy(wide.at[slot], mixer.at[:, pl.ds(0, width)], sems.at[slot]))
    copies[2].wait()
    copies[3].wait()


def settle(first, order, half, grads=None):
    _, height, width = half.shape
    shapes = (
        jax.ShapeDtypeStruct((height, 3 * height), F32),
        jax.ShapeDtypeStruct((height, height), F32),
    )
    given = [] if grads is None else list(grads)
    far = pl.BlockSpec(memory_space=pl.ANY)
    return pl.pallas_call(
        functools.partial(settle_kernel, first),
        grid_spec=pltpu.PrefetchScalarGridSpec(
            num_scalar_prefetch=1,
            grid=(1,),
            in_specs=[fixed(half.shape)] + [far] * len(given),
            out_specs=(far, far),
            scratch_shapes=[pltpu.VMEM((2, height, width), F32), pltpu.SemaphoreType.DMA((2,))],
        ),
        out_shape=shapes,
        input_output_aliases={2: 0, 3: 1} if given else {},
        compiler_params=pltpu.CompilerParams(vmem_limit_bytes=12 * MIB),
        cost_estimate=cost(3),
        name="settle",
    )(order, half, *given)


def on_device(
    tokens,
    segments,
    pairing,
    pair_weight,
    triple_weight,
    query_bias,
    value_bias,
    mixer_weight,
    mixer_bias,
    norm_gain,
    norm_shift,
    expand_weight,
    expand_bias,
    shrink_weight,
    shrink_bias,
    final_gain,
    final_shift,
):
    rows, length, width = tokens.shape
    fan = expand_weight.shape[1]
    size = lax.axis_size(AXIS)
    me = lax.axis_index(AXIS)
    order, places = block_order(me)
    (
        qkv,
        spread,
        stats,
        attended,
        scaled_a,
        first_low,
        active,
        slope,
        scaled_b,
        output,
        pooled,
    ) = layer(
        tokens,
        segments,
        triple_weight,
        query_bias,
        value_bias,
        mixer_weight,
        mixer_bias,
        norm_gain,
        norm_shift,
        expand_weight,
        expand_bias,
        shrink_weight,
        shrink_bias,
        final_gain,
        final_shift,
    )
    active, slope, expand_weight, shrink_weight, triple_weight = [
        pltpu.with_memory_space_constraint(array, pltpu.HBM)
        for array in (active, slope, expand_weight, shrink_weight, triple_weight)
    ]
    own = pooled.reshape(rows * SEG_ROW, width)
    gathered, (first_t, tokens_t) = gather_rows(own, size, [(turn, first_low), (turn, tokens)])
    loss, dpooled = contrast(gathered, own, pairing, pair_weight, me, size)

    dsecond, dshrunk, sums_b = second_grad(segments, dpooled, scaled_b, stats, final_gain)
    one = Summing(shrink_grad(0, order, dshrunk, active), me, size)
    beside(dshrunk, lambda t: shrink_grad(1, order, t, active), [one], [one], one)

    dexpanded, fan_sums = [], []

    def expand_part(first, count, blocks, starts, ends):
        blocks, part, sums = beside(
            dshrunk,
            lambda t: expand_grad(first, count, order, t, shrink_weight, slope, first_t, blocks),
            starts,
            ends,
        )
        dexpanded.append(part)
        fan_sums.append(sums[:count])
        return blocks

    send = expand_part(0, 2, None, [one], [one])
    two = Summing(send, me, size)
    keep = expand_part(2, 1, None, [one], [one])
    two.keep = expand_part(3, 1, keep, [one, two], [one])
    two.moving = lax.optimization_barrier((two.moving, fan_sums[-1]))[0]
    two.finish()
    dfirst = beside(
        dsecond, lambda t: first_grad(order, t, expand_weight, dexpanded), [two, one], [one]
    )
    dbranch, dbranch_low, dattended, dots, sums_a = beside(
        dfirst,
        lambda t: branch_grad(t, scaled_a, stats, norm_gain, mixer_weight, attended),
        [one],
        [one, two],
    )
    dmixed, sums_c = [], []
    for row in range(rows):
        part, sums = beside(
            dattended,
            lambda t: attention_grad(row, segments, qkv, t, spread, dots),
            [one, two] if row < 2 else [],
            [two, one] if row < 2 else [],
        )
        dmixed.append(part)
        sums_c.append(sums[0:2])
    send, keep = beside(
        tokens_t,
        lambda t: triple_grad(order, t, attended, dmixed, dbranch_low),
        [one, two],
        [one, two],
    )
    three = Summing(send, me, size)
    three.keep = keep
    fan_sums = jnp.concatenate(fan_sums, axis=0)
    pairs = order[0::2] // 2
    fan_sums = jnp.sum(
        jnp.where(pairs[None, :, None] == jnp.arange(4)[:, None, None], fan_sums[None], 0.0), axis=1
    )
    small = jnp.concatenate([sums_a[0:3], sums_b[0:3], sum(sums_c), fan_sums], axis=0)
    trades = [1 << k for k in range(size.bit_length() - 1)]

    def trade(*bits):
        def work(value):
            for bit in bits:
                if bit in trades:
                    trades.remove(bit)
                    value = value + lax.ppermute(value, AXIS, flip(size, bit, bit))
            return value

        return work

    def slot(starts, ends, work=lambda t: t):
        nonlocal small
        small = beside(small, work, starts, ends)

    def spread_beside(chain, parts, others):
        nonlocal small
        small, *grads = beside(
            small, lambda t: (t, *spread_blocks(places, chain.result, parts)), others, others
        )
        return grads

    slot([two, three], [three])
    tokens_out = beside(
        dbranch, lambda t: token_grad(t, dmixed, triple_weight), [three, one], [one, three, two]
    )
    slot([three, two], [three, two], trade(1))
    while not one.done:
        slot([three, one], [three, one])
    (dshrink,) = spread_beside(one, [((fan, width), 0, (0, 8), fan // 8, 0)], [three, two])
    slot([three, two], [three], trade(8))
    slot([three], [three, two])
    while not two.done:
        chains = [two] if len(three.steps) == 1 else [three, two]
        slot(chains, chains, trade(2))
    chains = [] if len(three.steps) == 1 else [three]
    (dexpand,) = spread_beside(two, [((width, fan), 1, (0, 8), width, 0)], chains)
    while len(three.steps) > 1:
        slot([three], [three], trade(16, 4))
    small = trade(*trades[::-1])(small)
    small, *grads = beside(
        small, lambda t: (t, *settle(4, order, three.next)), [three], [three]
    )
    dtriple, dmixer = settle(0, order, three.result[0], grads)
    return (
        loss,
        output,
        tokens_out,
        dtriple,
        small[6],
        small[7],
        dmixer,
        small[2],
        small[0],
        small[1],
        dexpand,
        small[8:].reshape(-1),
        dshrink,
        small[5],
        small[3],
        small[4],
    )


def solution(mesh):
    wide = P(AXIS, None, None)
    return jax.shard_map(
        on_device,
        mesh=mesh,
        in_specs=(wide, P(AXIS, None)) + (P(),) * 15,
        out_specs=(P(), wide, wide) + (P(),) * 13,
        check_vma=False,
    )
```

```python
import functools

import jax
import jax.numpy as jnp
from jax import lax
from jax.experimental import pallas as pl
from jax.experimental.pallas import tpu as pltpu
from jax.sharding import PartitionSpec as P

HEADS = 12
HEAD_DIM = 64
SEG_ROW = 8
AXIS = "wide"
F32 = jnp.float32
BF16 = jnp.bfloat16

highest = lax.Precision.HIGHEST
scale = 20.0
MIB = 1024 * 1024


def prefixes(width):
    return (width // 12, width // 6, width // 3, 2 * width // 3, width)


def cost(micros):
    return pl.CostEstimate(flops=int(micros * 1.15e9), bytes_accessed=0, transcendentals=0)


def dot(a, b):
    return jnp.dot(a, b, preferred_element_type=F32)


def dot_nt(a, b):
    return lax.dot_general(a, b, (((1,), (1,)), ((), ())), preferred_element_type=F32)


def dot_tn(a, b):
    return lax.dot_general(a, b, (((0,), (0,)), ((), ())), preferred_element_type=F32)


def window(array, low, high):
    first, last = low // 128 * 128, -(-high // 128) * 128
    piece = array[:, first:last]
    if first == low and last == high:
        return piece, first, last
    lane = first + lax.broadcasted_iota(jnp.int32, (1, last - first), 1)
    return jnp.where((lane >= low) & (lane < high), piece, jnp.zeros_like(piece)), first, last


def split(value):
    high = value.astype(BF16)
    return high, (value - high.astype(F32)).astype(BF16)


def flip(size, low, high):
    return [(i, i ^ (high if i & 1 else low)) for i in range(size)]


def bit_of(me, bit):
    return (me // bit) % 2


def gather_rows(block, size, works):
    bit, results = size // 2, []
    while bit:
        pairs = flip(size, bit, bit)
        if len(results) < len(works):
            work, value = works[len(results)]
            block, value = lax.optimization_barrier((block, value))
            other, result = lax.optimization_barrier((lax.ppermute(block, AXIS, pairs), work(value)))
            results.append(result)
        else:
            other = lax.ppermute(block, AXIS, pairs)
        block = jnp.concatenate([block, other], axis=0)
        bit //= 2
    return block, results


def contrast_kernel(
    size, me_ref, gathered, own_ref, cols_ref, rows_ref, load_col_ref, load_row_ref, loss_ref, grad_ref, table, total, aim
):
    me = me_ref[0]
    count, width = table.shape
    share = own_ref.shape[0]
    block = 128
    levels = size.bit_length() - 1
    for place in range(size):
        mask = sum(((place >> k) & 1) << (levels - 1 - k) for k in range(levels))
        owner = me ^ mask
        table[pl.ds(pl.multiple_of(owner * share, share), share), :] = gathered[
            place * share : (place + 1) * share, :
        ]
    cuts = prefixes(width)
    spans = list(zip((0,) + cuts[:-1], cuts))
    lane_ids = lax.broadcasted_iota(jnp.int32, (1, count), 1)

    def place_pairs(i, carry):
        partner, load = carry
        rows = pl.ds(pl.multiple_of(i * block, block), block)
        hit = cols_ref[rows, 0:1] == lane_ids
        partner = partner + jnp.sum(
            jnp.where(hit, cols_ref[rows, 1:2].astype(F32), 0.0), axis=0, keepdims=True
        )
        load = load + jnp.sum(jnp.where(hit, load_col_ref[rows, :], 0.0), axis=0, keepdims=True)
        return partner, load

    zero_row = jnp.zeros((1, count), F32)
    partner_row, load_row = lax.fori_loop(0, count // block, place_pairs, (zero_row, zero_row))
    own_ids = me * share + lax.broadcasted_iota(jnp.int32, (share, 1), 0)
    hit = rows_ref[0:1, :] == own_ids
    partner_own = jnp.sum(jnp.where(hit, rows_ref[1:2, :].astype(F32), 0.0), axis=1, keepdims=True)
    load_own = jnp.sum(jnp.where(hit, load_row_ref[...], 0.0), axis=1, keepdims=True)

    squares = jnp.zeros((count, 1), F32)
    side = jnp.zeros((count, 128), F32)
    for k, (low, high) in enumerate(spans):
        piece, first, last = window(table, low, high)
        wide = piece.astype(F32)
        squares = squares + jnp.sum(wide * wide, axis=1, keepdims=True)
        lane = lax.broadcasted_iota(jnp.int32, (1, 128), 1)
        side = jnp.where(lane == k, squares, side)
    upright = lax.rsqrt(jnp.transpose(side)[0:8, :] + 1e-06) * scale
    inverse_rows = [upright[k : k + 1, :] for k in range(len(cuts))]

    total[...] = jnp.zeros_like(total)
    aim[...] = jnp.zeros_like(aim)

    def add_rows(i, carry):
        start = pl.multiple_of(i * block, block)
        sims = jnp.zeros((block, count), F32)
        squares = jnp.zeros((block, 1), F32)
        row_ids = (start + lax.broadcasted_iota(jnp.int32, (block, 1), 0)).astype(F32)
        chosen = partner_row == row_ids
        for k, (low, high) in enumerate(spans):
            piece, first, last = window(table.at[pl.ds(start, block), :], low, high)
            wide = piece.astype(F32)
            squares = squares + jnp.sum(wide * wide, axis=1, keepdims=True)
            sims = sims + dot_nt(piece, table[:, first:last])
            value = sims * lax.rsqrt(squares + 1e-06) * inverse_rows[k]
            total[k : k + 1, :] += jnp.sum(jnp.exp(value - scale), axis=0, keepdims=True)
            aim[k : k + 1, :] += jnp.sum(jnp.where(chosen, value, 0.0), axis=0, keepdims=True)
        return carry

    lax.fori_loop(0, count // block, add_rows, 0)

    spreads = scale + jnp.log(total[0 : len(cuts), :])
    gaps = jnp.sum(spreads - aim[0 : len(cuts), :], axis=0, keepdims=True)
    loss_ref[...] = jnp.broadcast_to(
        jnp.sum(gaps * load_row, axis=1, keepdims=True) / count, loss_ref.shape
    )

    sims = jnp.zeros((share, count), F32)
    squares = jnp.zeros((share, 1), F32)
    out_hit = (partner_own == lane_ids.astype(F32)).astype(F32)
    in_hit = (partner_row == own_ids.astype(F32)).astype(F32)
    grad_ref[...] = jnp.zeros_like(grad_ref)
    for k, (low, high) in enumerate(spans):
        piece, first, last = window(own_ref, low, high)
        wide = piece.astype(F32)
        squares = squares + jnp.sum(wide * wide, axis=1, keepdims=True)
        inverse = lax.rsqrt(squares + 1e-06)
        sims = sims + dot_nt(piece, table[:, first:last])
        value = sims * inverse * inverse_rows[k]
        spread = scale + jnp.log(jnp.sum(jnp.exp(value - scale), axis=1, keepdims=True))
        dsims = load_own * (jnp.exp(value - spread) - out_hit) + load_row * (
            jnp.exp(value - spreads[k : k + 1, :]) - in_hit
        )
        big, small = split(dsims * inverse_rows[k])
        unit, _, last = window(own_ref, 0, high)
        unit = unit.astype(F32) * inverse
        dunit = dot(big, table[:, :last]) + dot(small, table[:, :last])
        if last != high:
            lane = lax.broadcasted_iota(jnp.int32, (1, last), 1)
            dunit = jnp.where(lane < high, dunit, 0.0)
        along = jnp.sum(dunit * unit, axis=1, keepdims=True)
        grad_ref[:, :last] += inverse * (dunit - unit * along)


def contrast(gathered, own, pairing, pair_weight, me, size):
    share, width = own.shape
    count = share * size
    vmem = pl.BlockSpec(memory_space=pltpu.VMEM)
    loss, grad = pl.pallas_call(
        functools.partial(contrast_kernel, size),
        out_shape=(
            jax.ShapeDtypeStruct((8, 128), F32),
            jax.ShapeDtypeStruct((share, width), F32),
        ),
        in_specs=[pl.BlockSpec(memory_space=pltpu.SMEM)] + [vmem] * 6,
        out_specs=(vmem, vmem),
        scratch_shapes=[
            pltpu.VMEM((count, width), BF16),
            pltpu.VMEM((8, count), F32),
            pltpu.VMEM((8, count), F32),
        ],
        compiler_params=pltpu.CompilerParams(vmem_limit_bytes=16 * MIB),
        cost_estimate=cost(6),
        name="contrast",
    )(
        me.reshape(1),
        gathered,
        own,
        pairing,
        pairing.T,
        pair_weight[:, None],
        pair_weight[None, :],
    )
    return loss[0, 0], grad


def attention_windows(length):
    block = 128
    return [
        (i, max(0, i - block), min(length, i + 2 * block)) for i in range(0, length, block)
    ]


def segment_column(seg_row):
    wide = jnp.broadcast_to(seg_row.astype(F32), (128, seg_row.shape[1]))
    return jnp.transpose(wide)[:, 0:1].astype(jnp.int32)


def both_heads(pair):
    left = lax.broadcasted_iota(jnp.int32, (1, 128), 1) < HEAD_DIM
    zero = jnp.zeros((), pair.dtype)
    return jnp.concatenate([jnp.where(left, pair, zero), jnp.where(left, zero, pair)], axis=0)


def layer_kernel(
    tokens,
    segments,
    triple_hbm,
    query_bias,
    value_bias,
    mixer_hbm,
    mixer_bias,
    norm_gain,
    norm_shift,
    expand_hbm,
    expand_bias,
    shrink_hbm,
    shrink_bias,
    final_gain,
    final_shift,
    qkv,
    spread,
    stats,
    attended,
    scaled_a,
    first_low,
    active,
    slope,
    scaled_b,
    output,
    pooled,
    triple,
    mixer,
    expand,
    shrink,
    bias,
    joined,
    first,
    total,
    sems,
):
    step = pl.program_id(0)
    length, width = tokens.shape[1:]
    fan = expand.shape[1]
    held = (triple, mixer, expand, shrink)
    copies = [
        pltpu.make_async_copy(src, dst, sems.at[k])
        for k, (src, dst) in enumerate(zip((triple_hbm, mixer_hbm, expand_hbm, shrink_hbm), held))
    ]

    @pl.when(step == 0)
    def _():
        for copy in copies:
            copy.start()
        copies[0].wait()

    seg_row = segments[pl.ds(step, 1), :]
    seg_col = segment_column(seg_row)
    windows = attention_windows(length)
    for k, (at, low, high) in enumerate(windows):
        same = seg_col[low:high, :] == seg_row[:, at : at + 128]
        bias[k, : high - low, :] = jnp.where(same, 0.0, -1e30)

    chunk = width
    x = tokens[0]
    mixed = dot(x, triple[:, 0:chunk]) + query_bias[...][None, :]
    qkv[0, :, 0:chunk] = (mixed.astype(BF16).astype(F32) * 0.125).astype(BF16)
    qkv[0, :, chunk : 2 * chunk] = dot(x, triple[:, chunk : 2 * chunk]).astype(BF16)
    qkv[0, :, 2 * chunk :] = (dot(x, triple[:, 2 * chunk :]) + value_bias[...][None, :]).astype(BF16)

    left = lax.broadcasted_iota(jnp.int32, (1, 128), 1) < HEAD_DIM
    spread[...] = jnp.zeros_like(spread)
    for k, (at, low, high) in enumerate(windows):
        wall = bias[k, : high - low, :]
        wall = jnp.concatenate([wall, wall], axis=1)
        for p in range(width // 128):
            cols = slice(p * 128, p * 128 + 128)
            query = both_heads(qkv[0, at : at + 128, cols])
            keys = qkv[0, low:high, width + p * 128 : width + p * 128 + 128]
            scores = dot_nt(keys, query) + wall
            top = jnp.max(scores, axis=0, keepdims=True)
            expo = jnp.exp(scores - top)
            amount = jnp.sum(expo, axis=0, keepdims=True)
            values = qkv[0, low:high, 2 * width + p * 128 : 2 * width + p * 128 + 128]
            share = jnp.transpose(jnp.broadcast_to(1.0 / amount, (128, amount.shape[1])))
            found = dot_tn(expo.astype(BF16), values) * share
            joined[at : at + 128, cols] = jnp.where(left, found[:128], found[128:]).astype(BF16)
            marks = top + jnp.log(amount)
            spread[0, 2 * p : 2 * p + 1, at : at + 128] = marks[:, :128]
            spread[0, 2 * p + 1 : 2 * p + 2, at : at + 128] = marks[:, 128:]

    attended[0] = jnp.transpose(joined[...])

    @pl.when(step == 0)
    def _():
        copies[1].wait()

    summed = tokens[0].astype(F32) + (dot(joined[...], mixer[...]) + mixer_bias[...][None, :])
    centre = summed - jnp.mean(summed, axis=1, keepdims=True)
    inverse = lax.rsqrt(jnp.mean(centre * centre, axis=1, keepdims=True) + 1e-05)
    scaled = centre * inverse
    scaled_a[0] = scaled.astype(BF16)
    inverse_a = inverse
    value = scaled * norm_gain[...][None, :] + norm_shift[...][None, :]
    first[...] = value
    first_low[0] = value.astype(BF16)

    @pl.when(step == 0)
    def _():
        copies[2].wait()
        copies[3].wait()

    part = 1024
    for j in range(fan // part):
        cols = slice(j * part, (j + 1) * part)
        value = dot(first_low[0], expand[:, cols]) + expand_bias[cols][None, :]
        gauss = jnp.exp(value * value * -0.5)
        near = 1.0 / (1.0 + 0.3275911 * 0.7071067811865476 * jnp.abs(value))
        poly = near * (
            0.5 * 0.254829592
            + near
            * (
                0.5 * -0.284496736
                + near * (0.5 * 1.421413741 + near * (0.5 * -1.453152027 + near * (0.5 * 1.061405429)))
            )
        )
        tail = poly * gauss
        below = jnp.where(value < 0, tail, 1.0 - tail)
        rounded = (value * below).astype(BF16)
        active[0, :, cols] = rounded
        slope[0, :, cols] = (below + value * (gauss * 0.3989422804014327)).astype(BF16)
        product = dot(rounded, shrink[cols, :])
        if j == 0:
            total[...] = product
        else:
            total[...] += product

    summed = first[...] + (total[...] + shrink_bias[...][None, :])
    centre = summed - jnp.mean(summed, axis=1, keepdims=True)
    inverse = lax.rsqrt(jnp.mean(centre * centre, axis=1, keepdims=True) + 1e-05)
    scaled = centre * inverse
    scaled_b[0] = scaled.astype(BF16)
    lane = lax.broadcasted_iota(jnp.int32, (1, 128), 1)
    stats[0] = jnp.where(lane == 0, inverse_a, inverse)
    final = scaled * final_gain[...][None, :] + final_shift[...][None, :]
    output[0] = final.astype(BF16)
    member = (
        lax.broadcasted_iota(jnp.int32, (SEG_ROW, length), 0) == seg_row
    ).astype(F32)
    counts = jnp.sum(member, axis=1, keepdims=True)
    gathered = jnp.dot(member, final, preferred_element_type=F32, precision=highest)
    pooled[0] = (gathered / counts).astype(BF16)


def layer(tokens, segments, triple_weight, query_bias, value_bias, mixer_weight, mixer_bias, norm_gain, norm_shift, expand_weight, expand_bias, shrink_weight, shrink_bias, final_gain, final_shift):
    rows, length, width = tokens.shape
    fan = expand_weight.shape[1]

    def by_row(*shape):
        return pl.BlockSpec((1,) + shape, lambda r: (r,) + (0,) * len(shape))

    def whole(size):
        return pl.BlockSpec((size,), lambda r: (0,))

    hbm = pl.BlockSpec(memory_space=pl.ANY)
    outs = (
        ((length, 3 * width), BF16),
        ((16, length), F32),
        ((length, 128), F32),
        ((width, length), BF16),
        ((length, width), BF16),
        ((length, width), BF16),
        ((length, fan), BF16),
        ((length, fan), BF16),
        ((length, width), BF16),
        ((length, width), BF16),
        ((SEG_ROW, width), BF16),
    )
    weights = (triple_weight, mixer_weight, expand_weight, shrink_weight)
    return pl.pallas_call(
        layer_kernel,
        grid=(rows,),
        out_shape=tuple(jax.ShapeDtypeStruct((rows,) + shape, kind) for shape, kind in outs),
        in_specs=[
            by_row(length, width),
            pl.BlockSpec((rows, length), lambda r: (0, 0)),
            hbm,
            whole(width),
            whole(width),
            hbm,
            whole(width),
            whole(width),
            whole(width),
            hbm,
            whole(fan),
            hbm,
            whole(width),
            whole(width),
            whole(width),
        ],
        out_specs=tuple(by_row(*shape) for shape, _ in outs),
        scratch_shapes=[pltpu.VMEM(w.shape, BF16) for w in weights]
        + [
            pltpu.VMEM((length // 128, 384, 128), F32),
            pltpu.VMEM((length, width), BF16),
            pltpu.VMEM((length, width), F32),
            pltpu.VMEM((length, width), F32),
            pltpu.SemaphoreType.DMA((4,)),
        ],
        compiler_params=pltpu.CompilerParams(vmem_limit_bytes=56 * MIB),
        cost_estimate=cost(50),
        name="layer",
    )(
        tokens,
        segments,
        triple_weight,
        query_bias,
        value_bias,
        mixer_weight,
        mixer_bias,
        norm_gain,
        norm_shift,
        expand_weight,
        expand_bias,
        shrink_weight,
        shrink_bias,
        final_gain,
        final_shift,
    )


def fixed(shape):
    return pl.BlockSpec(shape, lambda *_: (0,) * len(shape), pipeline_mode=pl.Buffered(1))


def second_grad_kernel(segments, dpooled, scaled, stats, gain, dsecond, dshrunk, sums):
    r = pl.program_id(0)
    length = scaled.shape[1]
    scale_row = gain[...][None, :]
    member = (
        lax.broadcasted_iota(jnp.int32, (SEG_ROW, length), 0) == segments[pl.ds(r, 1), :]
    ).astype(F32)
    counts = jnp.sum(member, axis=1, keepdims=True)
    inner = dpooled[...] / counts * scale_row
    table = jnp.concatenate(split(inner), axis=0)
    member = jnp.concatenate([member, member], axis=0).astype(BF16)
    inner = dot_tn(member, table)
    norm = scaled[0].astype(F32)
    product = inner * norm
    value = stats[0][:, 127:128] * (
        inner
        - jnp.mean(inner, axis=1, keepdims=True)
        - norm * jnp.mean(product, axis=1, keepdims=True)
    )
    low = value.astype(BF16)
    dsecond[0] = value
    dshrunk[0] = low

    @pl.when(r == 0)
    def _():
        sums[...] = jnp.zeros_like(sums)

    sums[0:1, :] += jnp.sum(product, axis=0, keepdims=True) / scale_row
    sums[1:2, :] += jnp.sum(dpooled[...], axis=0, keepdims=True)
    sums[2:3, :] += jnp.sum(low.astype(F32), axis=0, keepdims=True)


def second_grad(segments, dpooled, scaled, stats, gain):
    rows, length, width = scaled.shape

    def by_row(*shape):
        return pl.BlockSpec((1,) + shape, lambda r: (r,) + (0,) * len(shape))

    return pl.pallas_call(
        second_grad_kernel,
        grid=(rows,),
        in_specs=[
            fixed(segments.shape),
            pl.BlockSpec((SEG_ROW, width), lambda r: (r, 0)),
            by_row(length, width),
            by_row(length, 128),
            fixed(gain.shape),
        ],
        out_specs=(by_row(length, width), by_row(length, width), fixed((8, width))),
        out_shape=(
            jax.ShapeDtypeStruct((rows, length, width), F32),
            jax.ShapeDtypeStruct((rows, length, width), BF16),
            jax.ShapeDtypeStruct((8, width), F32),
        ),
        compiler_params=pltpu.CompilerParams(vmem_limit_bytes=16 * MIB),
        cost_estimate=cost(3),
        name="second_grad",
    )(segments, dpooled, scaled, stats, gain)


def put_pair(out, order, g, value, along=1):
    turned = order[2 * g] % 2
    cut = value.shape[along] // 2
    value = value.astype(BF16)
    out[turned] = value[:cut] if along == 0 else value[:, :cut]
    out[1 - turned] = value[cut:] if along == 0 else value[:, cut:]


def put_half(g, send, keep, put):
    @pl.when(g < 2)
    def _():
        put(send)

    @pl.when(g >= 2)
    def _():
        put(keep)


def half_specs(height, width):
    return (
        pl.BlockSpec((2, height, width), lambda g, order: (jnp.minimum(g, 1), 0, 0)),
        pl.BlockSpec((2, height, width), lambda g, order: (jnp.maximum(g - 2, 0), 0, 0)),
    )


def shrink_grad_kernel(half, order, dshrunk, active, out):
    rows, length, width = dshrunk.shape
    value = dot_tn(
        active[...].reshape(rows * length, active.shape[2]), dshrunk[...].reshape(rows * length, width)
    )
    put_pair(out, order, 2 * half + pl.program_id(0), value, 0)


def shrink_grad(half, order, dshrunk, active):
    rows, length, width = dshrunk.shape
    part = active.shape[2] // 4
    return pl.pallas_call(
        functools.partial(shrink_grad_kernel, half),
        grid_spec=pltpu.PrefetchScalarGridSpec(
            num_scalar_prefetch=1,
            grid=(2,),
            in_specs=[
                fixed(dshrunk.shape),
                pl.BlockSpec(
                    (rows, length, part), lambda g, order: (0, 0, order[4 * half + 2 * g] // 2)
                ),
            ],
            out_specs=pl.BlockSpec((2, part // 2, width), lambda g, order: (g, 0, 0)),
        ),
        out_shape=jax.ShapeDtypeStruct((4, part // 2, width), BF16),
        compiler_params=pltpu.CompilerParams(vmem_limit_bytes=20 * MIB),
        cost_estimate=cost(4),
        name="shrink_grad",
    )(order, dshrunk, active)


def expand_grad_kernel(first, order, dshrunk, shrink, slope, turned, *refs):
    out, dexpanded, sums = refs[-3:]
    rows, length, width = dshrunk.shape
    part = slope.shape[2]
    dactive = dot_nt(dshrunk[...].reshape(rows * length, width), shrink[...])
    low = (dactive * slope[...].reshape(rows * length, part).astype(F32)).astype(BF16)
    g = pl.program_id(0)
    sums[pl.ds(g, 1), :] = jnp.sum(low.astype(F32), axis=0, keepdims=True)
    put_pair(out, order, first + g, dot(turned[...], low))
    dexpanded[...] = low.reshape(rows, length, part)


def expand_grad(first, count, order, dshrunk, shrink_weight, slope, turned, blocks=None):
    rows, length, width = dshrunk.shape
    part = slope.shape[2] // 4
    pair = lambda g, order: order[2 * (first + g)] // 2
    given = [] if blocks is None else [blocks]
    return pl.pallas_call(
        functools.partial(expand_grad_kernel, first),
        grid_spec=pltpu.PrefetchScalarGridSpec(
            num_scalar_prefetch=1,
            grid=(count,),
            in_specs=[
                fixed(dshrunk.shape),
                pl.BlockSpec((part, width), lambda g, order: (pair(g, order), 0)),
                pl.BlockSpec((rows, length, part), lambda g, order: (0, 0, pair(g, order))),
                fixed(turned.shape),
            ]
            + [pl.BlockSpec(memory_space=pl.ANY) for _ in given],
            out_specs=(
                pl.BlockSpec((2, width, part // 2), lambda g, order: (first % 2 + g, 0, 0)),
                pl.BlockSpec((rows, length, part), lambda g, order: (0, 0, g)),
                fixed((8, part)),
            ),
        ),
        out_shape=(
            jax.ShapeDtypeStruct((4, width, part // 2), BF16),
            jax.ShapeDtypeStruct((rows, length, count * part), BF16),
            jax.ShapeDtypeStruct((8, part), F32),
        ),
        input_output_aliases={5: 0} if given else {},
        compiler_params=pltpu.CompilerParams(vmem_limit_bytes=24 * MIB),
        cost_estimate=cost(4),
        name="expand_grad",
    )(order, dshrunk, shrink_weight, slope, turned, *given)


def first_grad_kernel(order, dsecond, expand, *refs):
    *parts, out = refs
    width = dsecond.shape[2]
    value = dsecond[0]
    q = 0
    for part in parts:
        for k in range(part.shape[2] // width):
            columns = pl.ds(pl.multiple_of(order[2 * q] // 2 * width, 128), width)
            value = value + dot_nt(part[0, :, k * width : (k + 1) * width], expand[:, columns])
            q += 1
    out[0] = value


def first_grad(order, dsecond, expand_weight, parts):
    rows, length, width = dsecond.shape
    block = pl.BlockSpec((1, length, width), lambda r, order: (r, 0, 0))
    return pl.pallas_call(
        first_grad_kernel,
        grid_spec=pltpu.PrefetchScalarGridSpec(
            num_scalar_prefetch=1,
            grid=(rows,),
            in_specs=[block, fixed(expand_weight.shape)]
            + [pl.BlockSpec((1,) + part.shape[1:], lambda r, order: (r, 0, 0)) for part in parts],
            out_specs=block,
        ),
        out_shape=jax.ShapeDtypeStruct(dsecond.shape, F32),
        compiler_params=pltpu.CompilerParams(vmem_limit_bytes=28 * MIB),
        cost_estimate=cost(5.5),
        name="first_grad",
    )(order, dsecond, expand_weight, *parts)


def turn_kernel(value, out):
    out[...] = jnp.transpose(value[0])


def turn(value):
    rows, length, width = value.shape
    return pl.pallas_call(
        turn_kernel,
        grid=(rows,),
        in_specs=[pl.BlockSpec((1, length, width), lambda r: (r, 0, 0))],
        out_specs=pl.BlockSpec((width, length), lambda r: (0, r)),
        out_shape=jax.ShapeDtypeStruct((width, rows * length), value.dtype),
        compiler_params=pltpu.CompilerParams(vmem_limit_bytes=10 * MIB),
        cost_estimate=cost(1.5),
        name="turn",
    )(value)


def branch_grad_kernel(
    given, scaled, stats, gain, mixer, attended, dbranch, dbranch_low, dattended, dots, sums
):
    r = pl.program_id(0)
    width = given.shape[2]
    dfirst = given[0]
    inner = dfirst * gain[...][None, :]
    norm = scaled[0].astype(F32)
    value = stats[0][:, 0:1] * (
        inner
        - jnp.mean(inner, axis=1, keepdims=True)
        - norm * jnp.mean(inner * norm, axis=1, keepdims=True)
    )
    low = value.astype(BF16)
    dbranch[0] = value
    dbranch_low[0] = low

    @pl.when(r == 0)
    def _():
        sums[...] = jnp.zeros_like(sums)

    sums[0:1, :] += jnp.sum(dfirst * norm, axis=0, keepdims=True)
    sums[1:2, :] += jnp.sum(dfirst, axis=0, keepdims=True)
    sums[2:3, :] += jnp.sum(low.astype(F32), axis=0, keepdims=True)
    dattended[0] = dot_nt(low, mixer[...]).astype(BF16)
    turned = dot_nt(mixer[...], low).astype(BF16)
    product = turned.astype(F32) * attended[0].astype(F32)
    dots[...] = jnp.zeros_like(dots)
    for h in range(width // HEAD_DIM):
        dots[0, h : h + 1, :] = jnp.sum(
            product[h * HEAD_DIM : (h + 1) * HEAD_DIM, :], axis=0, keepdims=True
        )


def branch_grad(dfirst, scaled, stats, gain, mixer_weight, attended):
    rows, length, width = dfirst.shape

    def by_row(*shape):
        return pl.BlockSpec((1,) + shape, lambda r: (r,) + (0,) * len(shape))

    wide, low = by_row(length, width), by_row(length, width)
    return pl.pallas_call(
        branch_grad_kernel,
        grid=(rows,),
        in_specs=[
            wide,
            low,
            by_row(length, 128),
            fixed(gain.shape),
            fixed(mixer_weight.shape),
            by_row(width, length),
        ],
        out_specs=(wide, low, low, by_row(16, length), fixed((8, width))),
        out_shape=(
            jax.ShapeDtypeStruct((rows, length, width), F32),
            jax.ShapeDtypeStruct((rows, length, width), BF16),
            jax.ShapeDtypeStruct((rows, length, width), BF16),
            jax.ShapeDtypeStruct((rows, 16, length), F32),
            jax.ShapeDtypeStruct((8, width), F32),
        ),
        compiler_params=pltpu.CompilerParams(vmem_limit_bytes=28 * MIB),
        cost_estimate=cost(5.5),
        name="branch_grad",
    )(dfirst, scaled, stats, gain, mixer_weight, attended)


def attention_grad_kernel(row, segments, qkv, dattended, spread, dots, dmixed, sums, bias, dkeys, dvalues):
    r = row
    length, width = dattended.shape[1:]
    seg_row = segments[r : r + 1, :]
    seg_col = segment_column(seg_row)
    windows = attention_windows(length)
    for k, (at, low, high) in enumerate(windows):
        same = seg_col[low:high, :] == seg_row[:, at : at + 128]
        bias[k, : high - low, :] = jnp.where(same, 0.0, -1e30)
    dkeys[...] = jnp.zeros_like(dkeys)
    dvalues[...] = jnp.zeros_like(dvalues)
    left = lax.broadcasted_iota(jnp.int32, (1, 128), 1) < HEAD_DIM
    for k, (at, low, high) in enumerate(windows):
        wall = bias[k, : high - low, :]
        wall = jnp.concatenate([wall, wall], axis=1)
        for p in range(width // 128):
            cols = slice(p * 128, p * 128 + 128)
            query = both_heads(qkv[0, at : at + 128, cols])
            keys = qkv[0, low:high, width + p * 128 : width + p * 128 + 128]
            values = qkv[0, low:high, 2 * width + p * 128 : 2 * width + p * 128 + 128]
            grad = both_heads(dattended[0, at : at + 128, cols])
            lse, delta = [
                jnp.concatenate(
                    [ref[0, 2 * p : 2 * p + 1, at : at + 128], ref[0, 2 * p + 1 : 2 * p + 2, at : at + 128]],
                    axis=1,
                )
                for ref in (spread, dots)
            ]
            probs = jnp.exp(dot_nt(keys, query) + wall - lse)
            dscores = (probs * (dot_nt(values, grad) - delta)).astype(BF16)
            dvalues[low:high, cols] += dot(probs.astype(BF16), grad)
            dkeys[low:high, cols] += dot(dscores, query)
            dquery = dot_tn(dscores, keys)
            dmixed[0, at : at + 128, cols] = (
                jnp.where(left, dquery[:128], dquery[128:]) * 0.125
            ).astype(BF16)
    dmixed[0, :, width : 2 * width] = dkeys[...].astype(BF16)
    dmixed[0, :, 2 * width :] = dvalues[...].astype(BF16)

    sums[...] = jnp.zeros_like(sums)
    sums[0:1, :] = jnp.sum(dmixed[0, :, :width].astype(F32), axis=0, keepdims=True)
    sums[1:2, :] = jnp.sum(dmixed[0, :, 2 * width :].astype(F32), axis=0, keepdims=True)


def attention_grad(row, segments, qkv, dattended, spread, dots):
    rows, length, width = dattended.shape

    def by_row(*shape):
        return pl.BlockSpec((1,) + shape, lambda _: (row,) + (0,) * len(shape))

    return pl.pallas_call(
        functools.partial(attention_grad_kernel, row),
        grid=(1,),
        in_specs=[
            fixed(segments.shape),
            by_row(length, 3 * width),
            by_row(length, width),
            by_row(16, length),
            by_row(16, length),
        ],
        out_specs=(fixed((1, length, 3 * width)), fixed((8, width))),
        out_shape=(
            jax.ShapeDtypeStruct((1, length, 3 * width), BF16),
            jax.ShapeDtypeStruct((8, width), F32),
        ),
        scratch_shapes=[
            pltpu.VMEM((length // 128, 384, 128), F32),
            pltpu.VMEM((length, width), F32),
            pltpu.VMEM((length, width), F32),
        ],
        compiler_params=pltpu.CompilerParams(vmem_limit_bytes=20 * MIB),
        cost_estimate=cost(8),
        name="attention_grad",
    )(segments, qkv, dattended, spread, dots)


def triple_grad_kernel(order, turned, attended, dbranch, *refs):
    *dmixed, send, keep = refs
    g = pl.program_id(0)
    rows, length = dbranch.shape[:2]
    pair = order[2 * g] // 2

    @pl.when(pair < 3)
    def _():
        value = dot(turned[:, :length], dmixed[0][0])
        for r in range(1, rows):
            value = value + dot(turned[:, r * length : (r + 1) * length], dmixed[r][0])
        put_half(g, send, keep, lambda out: put_pair(out, order, g, value))

    @pl.when(pair >= 3)
    def _():
        value = dot(attended[0], dbranch[0])
        for r in range(1, rows):
            value = value + dot(attended[r], dbranch[r])
        put_half(g, send, keep, lambda out: put_pair(out, order, g, value))


def triple_grad(order, turned, attended, dmixed, dbranch):
    rows, length, width = dbranch.shape
    shape = jax.ShapeDtypeStruct((4, width, width // 2), BF16)
    return pl.pallas_call(
        triple_grad_kernel,
        grid_spec=pltpu.PrefetchScalarGridSpec(
            num_scalar_prefetch=1,
            grid=(4,),
            in_specs=[fixed(turned.shape), fixed(attended.shape), fixed(dbranch.shape)]
            + [
                pl.BlockSpec(
                    (1, length, width), lambda g, order: (0, 0, jnp.minimum(order[2 * g] // 2, 2))
                )
                for _ in dmixed
            ],
            out_specs=half_specs(width, width // 2),
        ),
        out_shape=(shape, shape),
        compiler_params=pltpu.CompilerParams(vmem_limit_bytes=22 * MIB),
        cost_estimate=cost(7),
        name="triple_grad",
    )(order, turned, attended, dbranch, *dmixed)


def token_grad_kernel(dbranch, triple, *refs):
    *dmixed, out = refs
    r = pl.program_id(0)
    for k, ref in enumerate(dmixed):

        @pl.when(r == k)
        def _():
            out[0] = dbranch[0] + dot_nt(ref[0], triple[...])


def token_grad(dbranch, dmixed, triple_weight):
    rows, length, width = dbranch.shape
    return pl.pallas_call(
        token_grad_kernel,
        grid=(rows,),
        in_specs=[pl.BlockSpec((1, length, width), lambda r: (r, 0, 0)), fixed(triple_weight.shape)]
        + [fixed(part.shape) for part in dmixed],
        out_specs=pl.BlockSpec((1, length, width), lambda r: (r, 0, 0)),
        out_shape=jax.ShapeDtypeStruct(dbranch.shape, F32),
        compiler_params=pltpu.CompilerParams(vmem_limit_bytes=24 * MIB),
        cost_estimate=cost(5.5),
        name="token_grad",
    )(dbranch, triple_weight, *dmixed)


def block_order(me):
    core = bit_of(me, 1)
    one, two = bit_of(me, 2), bit_of(me, 4)
    near, far = jnp.where(core == 0, one, two), jnp.where(core == 0, two, one)
    order = []
    for owner, high, low in ((1 - core, far, near), (core, near, far)):
        for a in (1, 0):
            for b in (1, 0):
                order.append(owner * 4 + (high ^ a) * 2 + (low ^ b))
    order = jnp.stack(order).astype(jnp.int32)
    places = jnp.sum(
        jnp.where(order[None, :] == jnp.arange(8)[:, None], jnp.arange(8)[None, :], 0), axis=1
    ).astype(jnp.int32)
    return order, places


def beside(value, work, starts=(), ends=(), rest=None):
    value, nexts = lax.optimization_barrier((value, [chain.next for chain in starts]))
    for chain, array in zip(starts, nexts):
        chain.next = array
        chain.start()
    result = work(value)
    result, moving = lax.optimization_barrier((result, [chain.moving for chain in ends]))
    if rest is not None:
        rest.keep = result
    for chain, array in zip(ends, moving):
        chain.moving = array
        chain.finish()
    return result


class Summing:
    def __init__(self, send, me, size, whole=True):
        self.me, self.size = me, size
        self.next, self.moving = send, None
        rest = [1 << k for k in range(3, size.bit_length() - 1)]
        steps = [(k, flip(size, *bits)) for k, bits in enumerate(((1, 1), (2, 4), (4, 2)))]
        self.steps = steps + [("halve", bit) for bit in rest]
        if whole:
            self.steps += [("double", bit) for bit in rest[::-1]]
            self.steps += [("join", pairs) for _, pairs in steps[::-1]]

    @property
    def done(self):
        return not self.steps

    def start(self):
        kind, detail = self.steps[0]
        pairs = flip(self.size, detail, detail) if kind in ("halve", "double") else detail
        self.moving = lax.ppermute(self.next, AXIS, pairs)

    def finish(self):
        kind, detail = self.steps.pop(0)
        got = self.moving
        f32 = lambda t: t.astype(F32)
        if kind == 0:
            self.first = got
            self.next = (f32(self.keep[0:2]) + f32(got[0:2])).astype(BF16)
        elif kind == 1:
            self.second = got
            self.next = (f32(self.keep[2:3]) + f32(self.first[2:3]) + f32(got[0:1])).astype(BF16)
        elif kind == 2:
            own = f32(self.keep[3]) + f32(self.first[3]) + f32(self.second[1]) + f32(got[0])
            self.cut(own)
        elif kind == "halve":
            self.cut(self.own + f32(got))
        elif kind == "double":
            mine = bit_of(self.me, detail)
            self.next = jnp.where(
                mine == 0,
                jnp.concatenate([self.next, got], axis=0),
                jnp.concatenate([got, self.next], axis=0),
            )
            self.lift()
        elif len(self.steps):
            self.next = jnp.concatenate([got, self.next], axis=0)
        else:
            self.result = (got, self.next)

    def cut(self, own):
        kind, detail = self.steps[0] if self.steps else (None, None)
        if kind == "halve":
            mine = bit_of(self.me, detail)
            half = own.shape[0] // 2
            self.own = lax.dynamic_slice_in_dim(own, mine * half, half, 0)
            own = lax.dynamic_slice_in_dim(own, (1 - mine) * half, half, 0)
        self.next = own.astype(BF16)
        self.lift()

    def lift(self):
        if self.steps and self.steps[0][0] == "join":
            self.next = self.next[None]


def spread_kernel(ranges, places, *refs):
    outs = refs[2 * len(ranges) :]
    b = pl.program_id(0)
    half = pl.num_programs(0) // 2

    def store(out, value):
        value = value.astype(F32)
        height, width = out.shape
        if value.shape[1] == width:
            out[...] = value
        else:
            out[:, : width // 2] = value[:height]
            out[:, width // 2 :] = value[height:]

    for k, (low, high) in enumerate(ranges):
        here = (b >= low) & (b < high)

        @pl.when(here & (places[b] < half))
        def _():
            store(outs[k], refs[2 * k][0])

        @pl.when(here & (places[b] >= half))
        def _():
            store(outs[k], refs[2 * k + 1][0])


def spread_blocks(places, halves, parts):
    got, own = halves
    half, _, width = got.shape
    in_specs, out_specs, shapes = [], [], []

    def spec(shape, index):
        return pl.BlockSpec(shape, index)

    for shape, along, (low, high), height, skip in parts:
        at = lambda b, low=low, high=high: jnp.clip(b, low, high - 1)
        block = (1, height, width)
        in_specs.append(
            spec(block, lambda b, p, at=at, skip=skip: (jnp.minimum(p[at(b)], half - 1), skip, 0))
        )
        in_specs.append(
            spec(block, lambda b, p, at=at, skip=skip: (jnp.maximum(p[at(b)] - half, 0), skip, 0))
        )
        count = high - low
        if along == 0:
            out = (shape[0] // count, shape[1])
            out_specs.append(spec(out, lambda b, p, at=at, low=low: (at(b) - low, 0)))
        else:
            out = (shape[0], shape[1] // count)
            out_specs.append(spec(out, lambda b, p, at=at, low=low: (0, at(b) - low)))
        shapes.append(jax.ShapeDtypeStruct(shape, F32))
    return pl.pallas_call(
        functools.partial(spread_kernel, [part[2] for part in parts]),
        grid_spec=pltpu.PrefetchScalarGridSpec(
            num_scalar_prefetch=1, grid=(2 * half,), in_specs=in_specs, out_specs=tuple(out_specs)
        ),
        out_shape=tuple(shapes),
        compiler_params=pltpu.CompilerParams(vmem_limit_bytes=20 * MIB),
        cost_estimate=cost(5),
        name="spread_blocks",
    )(places, *(half for _ in parts for half in (got, own)))


def settle_kernel(first, order, half, *refs):
    triple, mixer, wide, sems = refs[-4:]
    width = wide.shape[2]
    split_at = triple.shape[1] // width
    copies = []
    for k in range(4):
        slot, label = k % 2, order[first + k]
        if k >= 2:
            copies[k - 2].wait()
        wide[slot] = half[k].astype(F32)

        @pl.when(label < split_at)
        def _():
            at = pl.multiple_of(label * width, 128)
            pltpu.make_async_copy(wide.at[slot], triple.at[:, pl.ds(at, width)], sems.at[slot]).start()

        @pl.when(label >= split_at)
        def _():
            at = pl.multiple_of((label - split_at) * width, 128)
            pltpu.make_async_copy(wide.at[slot], mixer.at[:, pl.ds(at, width)], sems.at[slot]).start()

        copies.append(pltpu.make_async_copy(wide.at[slot], mixer.at[:, pl.ds(0, width)], sems.at[slot]))
    copies[2].wait()
    copies[3].wait()


def settle(first, order, half, grads=None):
    _, height, width = half.shape
    shapes = (
        jax.ShapeDtypeStruct((height, 3 * height), F32),
        jax.ShapeDtypeStruct((height, height), F32),
    )
    given = [] if grads is None else list(grads)
    far = pl.BlockSpec(memory_space=pl.ANY)
    return pl.pallas_call(
        functools.partial(settle_kernel, first),
        grid_spec=pltpu.PrefetchScalarGridSpec(
            num_scalar_prefetch=1,
            grid=(1,),
            in_specs=[fixed(half.shape)] + [far] * len(given),
            out_specs=(far, far),
            scratch_shapes=[pltpu.VMEM((2, height, width), F32), pltpu.SemaphoreType.DMA((2,))],
        ),
        out_shape=shapes,
        input_output_aliases={2: 0, 3: 1} if given else {},
        compiler_params=pltpu.CompilerParams(vmem_limit_bytes=12 * MIB),
        cost_estimate=cost(3),
        name="settle",
    )(order, half, *given)


def on_device(
    tokens,
    segments,
    pairing,
    pair_weight,
    triple_weight,
    query_bias,
    value_bias,
    mixer_weight,
    mixer_bias,
    norm_gain,
    norm_shift,
    expand_weight,
    expand_bias,
    shrink_weight,
    shrink_bias,
    final_gain,
    final_shift,
):
    rows, length, width = tokens.shape
    fan = expand_weight.shape[1]
    size = lax.axis_size(AXIS)
    me = lax.axis_index(AXIS)
    order, places = block_order(me)
    (
        qkv,
        spread,
        stats,
        attended,
        scaled_a,
        first_low,
        active,
        slope,
        scaled_b,
        output,
        pooled,
    ) = layer(
        tokens,
        segments,
        triple_weight,
        query_bias,
        value_bias,
        mixer_weight,
        mixer_bias,
        norm_gain,
        norm_shift,
        expand_weight,
        expand_bias,
        shrink_weight,
        shrink_bias,
        final_gain,
        final_shift,
    )
    active, slope, expand_weight, shrink_weight, triple_weight = [
        pltpu.with_memory_space_constraint(array, pltpu.HBM)
        for array in (active, slope, expand_weight, shrink_weight, triple_weight)
    ]
    own = pooled.reshape(rows * SEG_ROW, width)
    gathered, (first_t, tokens_t) = gather_rows(own, size, [(turn, first_low), (turn, tokens)])
    loss, dpooled = contrast(gathered, own, pairing, pair_weight, me, size)

    dsecond, dshrunk, sums_b = second_grad(segments, dpooled, scaled_b, stats, final_gain)
    one = Summing(shrink_grad(0, order, dshrunk, active), me, size)
    beside(dshrunk, lambda t: shrink_grad(1, order, t, active), [one], [one], one)

    dexpanded, fan_sums = [], []

    def expand_parts(calls, starts, ends):
        found = beside(
            dshrunk,
            lambda t: [
                expand_grad(first, count, order, t, shrink_weight, slope, first_t, blocks)
                for first, count, blocks in calls
            ],
            starts,
            ends,
        )
        for (_, count, _), (_, part, sums) in zip(calls, found):
            dexpanded.append(part)
            fan_sums.append(sums[:count])
        return [blocks for blocks, _, _ in found]

    send, keep = expand_parts([(0, 2, None), (2, 1, None)], [one], [one])
    two = Summing(send, me, size)
    (two.keep,) = expand_parts([(3, 1, keep)], [one, two], [one])
    two.moving = lax.optimization_barrier((two.moving, fan_sums[-1]))[0]
    two.finish()
    dfirst = beside(
        dsecond, lambda t: first_grad(order, t, expand_weight, dexpanded), [two, one], [one]
    )
    dbranch, dbranch_low, dattended, dots, sums_a = beside(
        dfirst,
        lambda t: branch_grad(t, scaled_a, stats, norm_gain, mixer_weight, attended),
        [one],
        [one, two],
    )
    dmixed, sums_c = [], []
    for row in range(rows):
        part, sums = beside(
            dattended,
            lambda t: attention_grad(row, segments, qkv, t, spread, dots),
            [one, two] if row < 2 else [],
            [two, one] if row < 2 else [],
        )
        dmixed.append(part)
        sums_c.append(sums[0:2])
    send, keep = beside(
        tokens_t,
        lambda t: triple_grad(order, t, attended, dmixed, dbranch_low),
        [one, two],
        [one, two],
    )
    three = Summing(send, me, size)
    three.keep = keep
    fan_sums = jnp.concatenate(fan_sums, axis=0)
    pairs = order[0::2] // 2
    fan_sums = jnp.sum(
        jnp.where(pairs[None, :, None] == jnp.arange(4)[:, None, None], fan_sums[None], 0.0), axis=1
    )
    small = jnp.concatenate([sums_a[0:3], sums_b[0:3], sum(sums_c), fan_sums], axis=0)
    trades = [1 << k for k in range(size.bit_length() - 1)]

    def trade(*bits):
        def work(value):
            for bit in bits:
                if bit in trades:
                    trades.remove(bit)
                    value = value + lax.ppermute(value, AXIS, flip(size, bit, bit))
            return value

        return work

    def slot(starts, ends, work=lambda t: t):
        nonlocal small
        small = beside(small, work, starts, ends)

    def spread_beside(chain, parts, starts, ends):
        nonlocal small
        small, *grads = beside(
            small, lambda t: (t, *spread_blocks(places, chain.result, parts)), starts, ends
        )
        return grads

    slot([two, three], [three])
    tokens_out = beside(
        dbranch, lambda t: token_grad(t, dmixed, triple_weight), [three], [three, two]
    )
    slot([three, two], [three, two], trade(1, 4))
    slot([three, one], [three])
    slot([three, two], [three, one], trade(8))
    slot([three, one], [three, one, two], trade(2))
    while not one.done:
        slot([three, one], [three, one])
    (dshrink,) = spread_beside(
        one, [((fan, width), 0, (0, 8), fan // 8, 0)], [three, two], [three, two]
    )
    while not two.done:
        chains = [two] if len(three.steps) == 1 else [three, two]
        slot(chains, chains, trade(16))
    chains = [] if len(three.steps) == 1 else [three]
    (dexpand,) = spread_beside(two, [((width, fan), 1, (0, 8), width, 0)], chains, chains)
    while len(three.steps) > 1:
        slot([three], [three])
    small = trade(*trades[::-1])(small)
    small, dtriple, dmixer = beside(
        small, lambda t: (t, *settle(4, order, three.next)), [three], [three]
    )
    dtriple, dmixer = settle(0, order, three.result[0], (dtriple, dmixer))
    return (
        loss,
        output,
        tokens_out,
        dtriple,
        small[6],
        small[7],
        dmixer,
        small[2],
        small[0],
        small[1],
        dexpand,
        small[8:].reshape(-1),
        dshrink,
        small[5],
        small[3],
        small[4],
    )


def solution(mesh):
    wide = P(AXIS, None, None)
    return jax.shard_map(
        on_device,
        mesh=mesh,
        in_specs=(wide, P(AXIS, None)) + (P(),) * 15,
        out_specs=(P(), wide, wide) + (P(),) * 13,
        check_vma=False,
    )
```
